32 devices in a mesh: blk: 4 (over y, x), cells: 8 (over z, core).
Axes of the slice: x: 2, y: 2, z: 4, core: 2. Of those that a mesh axis runs over, the one named last changes fastest.
Arguments:
- tokens: bfloat16 [24, 1536, 512], P('cells', 'blk'), may hold values from -6 to 6
- known_flags: int32 [24, 1536], P('cells'), may hold values 0 or 1
- w_query: bfloat16 [512, 512], replicated, may hold values from -0.25 to 0.25
- b_query: bfloat16 [512], replicated, may hold values from -2 to 2
- w_key: bfloat16 [512, 512], replicated, may hold values from -0.25 to 0.25
- w_value: bfloat16 [512, 512], replicated, may hold values from -0.25 to 0.25
- b_value: bfloat16 [512], replicated, may hold values from -2 to 2
- w_out: bfloat16 [512, 512], replicated, may hold values from -6 to 6
- b_out: bfloat16 [512], replicated, may hold values from -2 to 2
- gain_one: bfloat16 [512], replicated, may hold values from 0.5 to 1.5
- shift_one: bfloat16 [512], replicated, may hold values from -2 to 2
- w_up: bfloat16 [512, 512], replicated, may hold values from -0.25 to 0.25
- b_up: bfloat16 [512], replicated, may hold values from -2 to 2
- w_down: bfloat16 [512, 512], replicated, may hold values from -0.25 to 0.25
- b_down: bfloat16 [512], replicated, may hold values from -2 to 2
- gain_two: bfloat16 [512], replicated, may hold values from 0.5 to 1.5
- shift_two: bfloat16 [512], replicated, may hold values from -2 to 2
- cotangent: bfloat16 [24, 1536, 512], P('cells', 'blk'), may hold values from -6 to 6
Outputs:
- layer_out: bfloat16 [24, 1536, 512], P('cells', 'blk')
- grad_tokens: float32 [24, 1536, 512], P('cells', 'blk')
- grad_w_query: float32 [512, 512], replicated
- grad_b_query: float32 [512], replicated
- grad_w_key: float32 [512, 512], replicated
- grad_w_value: float32 [512, 512], replicated
- grad_b_value: float32 [512], replicated
- grad_w_out: float32 [512, 512], replicated
- grad_b_out: float32 [512], replicated
- grad_gain_one: float32 [512], replicated
- grad_shift_one: float32 [512], replicated
- grad_w_up: float32 [512, 512], replicated
- grad_b_up: float32 [512], replicated
- grad_w_down: float32 [512, 512], replicated
- grad_b_down: float32 [512], replicated
- grad_gain_two: float32 [512], replicated
- grad_shift_two: float32 [512], replicated
The draws below stay inside these ranges and needn't reach their ends.
All inputs are finite; a program needn't handle non-finite values. No bound on the sum of `known_flags` on one device may be relied on, other than what follows from the above.
Results may differ from the reference program's by a relative error of at most 0.015.
Values may be sent and summed in bfloat16 or wider, within the bound.
No kernel may reach another device: no remote copies, remote signals or barrier semaphores. Data moves between devices by JAX's collectives and lax.ppermute only.
A program may use at most 256 MiB of HBM per device.

```python
import jax
import jax.numpy as jnp
from jax import lax

D = 512
HEADS = 8
HEAD = 64
FF = 512
LEN = 1536
CELLS = 24


def plant(drawn, rng, least, largest):
    longest = drawn.shape.index(max(drawn.shape))
    spots = []
    for shift in (0, 1):
        where = [jax.random.randint(jax.random.fold_in(rng, axis), (), 0, length) for axis, length in enumerate(drawn.shape)]
        where[longest] = (where[longest] + shift) % drawn.shape[longest]
        spots.append(tuple(where))
    return drawn.at[spots[0]].set(least).at[spots[1]].set(largest)


def shard_levels(own_key, dims, pieces, low, largest):
    def one(axis_at, parts):
        heights = jax.random.uniform(jax.random.fold_in(jax.random.fold_in(own_key, 6), axis_at), (parts,), jnp.float32, low / len(pieces), largest / len(pieces))
        return jnp.repeat(jnp.exp(heights), dims[axis_at] // parts).reshape((-1,) + (1,) * (len(dims) - axis_at - 1))

    loudness = one(*pieces[0])
    for cut in pieces[1:]:
        loudness = loudness * one(*cut)
    return loudness


def gaussian(key, shape, width, bound, pieces=(), held_as=jnp.bfloat16):
    array = width * jax.random.normal(key, shape, jnp.float32)
    if pieces:
        array = array * shard_levels(key, shape, pieces, -0.22, 0.18)
    return jnp.clip(array, -bound, bound).astype(held_as)


def setup_inputs(seed: int = 0) -> dict:
    seeds = jax.random.split(jax.random.key(seed), 19)
    return {
        "tokens": gaussian(seeds[0], (CELLS, LEN, D), 1.0, 6.0, ((0, 8), (1, 4))),
        "known_flags": plant((jax.random.randint(seeds[1], (CELLS, LEN), 0, 2) < 1).astype(jnp.int32), jax.random.fold_in(seeds[1], 1), 0, 1),
        "w_query": gaussian(seeds[2], (D, D), D ** -0.5, 0.25),
        "b_query": gaussian(seeds[3], (D,), 0.3, 2.0),
        "w_key": gaussian(seeds[4], (D, D), D ** -0.5, 0.25),
        "w_value": gaussian(seeds[5], (D, D), D ** -0.5, 0.25),
        "b_value": gaussian(seeds[6], (D,), 0.3, 2.0),
        "w_out": gaussian(seeds[7], (D, D), (max(1, 2 * D // LEN)) ** -0.5, 6.0),
        "b_out": gaussian(seeds[8], (D,), 0.3, 2.0),
        "gain_one": jnp.clip(1.0 + 0.1 * jax.random.normal(seeds[9], (D,), jnp.float32), 0.5, 1.5).astype(jnp.bfloat16),
        "shift_one": gaussian(seeds[10], (D,), 0.3, 2.0),
        "w_up": gaussian(seeds[11], (D, FF), D ** -0.5, 0.25),
        "b_up": gaussian(seeds[12], (FF,), 0.3, 2.0),
        "w_down": gaussian(seeds[13], (FF, D), FF ** -0.5, 0.25),
        "b_down": gaussian(seeds[14], (D,), 0.3, 2.0),
        "gain_two": jnp.clip(1.0 + 0.1 * jax.random.normal(seeds[15], (D,), jnp.float32), 0.5, 1.5).astype(jnp.bfloat16),
        "shift_two": gaussian(seeds[16], (D,), 0.3, 2.0),
        "cotangent": gaussian(seeds[17], (CELLS, LEN, D), 1.0, 6.0, ((0, 8), (1, 4))),
    }


@jax.custom_vjp
def low(v):
    return lax.optimization_barrier(v.astype(jnp.bfloat16)).astype(jnp.float32)

@jax.custom_vjp
def low_back(v):
    return v

def low_keep(v):
    return (low(v), None)

def low_pass(kept, grad):
    return (grad,)

def back_keep(v):
    return (v, None)

def back_low(kept, grad):
    return (low(grad),)
low.defvjp(low_keep, low_pass)
low_back.defvjp(back_keep, back_low)
epsilon = 1e-05
highest = lax.Precision.HIGHEST

def layer_norm(inputs, gain_vector, shift_vector):
    row_mean = lax.optimization_barrier(jnp.mean(inputs, axis=-1, keepdims=True))
    centered = inputs - row_mean
    spread = lax.optimization_barrier(jnp.mean(centered * centered, axis=-1, keepdims=True))
    return centered * lax.rsqrt(spread + epsilon) * gain_vector + shift_vector

def project(inputs, weight):
    return jnp.einsum('gtd,de->gte', inputs, weight, precision=highest)

def forward(tokens, known_flags, w_query, b_query, w_key, w_value, b_value, w_out, b_out, gain_one, shift_one, w_up, b_up, w_down, b_down, gain_two, shift_two):
    group_count = tokens.shape[0]
    queries = low_back(low(project(tokens, w_query) + b_query)).reshape(group_count, LEN, HEADS, HEAD)
    key_part = low_back(low(project(tokens, w_key))).reshape(group_count, LEN, HEADS, HEAD)
    values = low_back(low(project(tokens, w_value) + b_value)).reshape(group_count, LEN, HEADS, HEAD)
    places = jnp.arange(LEN, dtype=jnp.int32)
    allowed = (known_flags[:, None, None, :] > 0) | (places[:, None] == places[None, :])[None, None]
    raw_scores = low_back(jnp.einsum('gqhe,gkhe->ghqk', queries, key_part, precision=highest))
    scores = jnp.where(allowed, raw_scores * HEAD ** (-0.5), -1e+30)
    weights = jax.nn.softmax(scores, axis=-1)
    mixture = jnp.einsum('ghqk,gkhe->gqhe', weights, values, precision=highest).reshape(group_count, LEN, D)
    attn_in = low_back(low(mixture))
    attention = low_back(project(attn_in, w_out) + b_out)
    normed = layer_norm(tokens + attention, gain_one, shift_one)
    up_pre = low_back(project(low(normed), w_up) + b_up)
    activation = low(jax.nn.gelu(up_pre, approximate=False))
    down_part = low_back(project(activation, w_down) + b_down)
    return layer_norm(normed + down_part, gain_two, shift_two)

def reference(tokens, known_flags, w_query, b_query, w_key, w_value, b_value, w_out, b_out, gain_one, shift_one, w_up, b_up, w_down, b_down, gain_two, shift_two, cotangent):
    parameters = tuple((w.astype(jnp.float32) for w in (w_query, b_query, w_key, w_value, b_value, w_out, b_out, gain_one, shift_one, w_up, b_up, w_down, b_down, gain_two, shift_two)))
    group_size = 2 if CELLS % 2 == 0 else 1
    batches = CELLS // group_size
    token_groups = tokens.astype(jnp.float32).reshape(batches, group_size, LEN, D)
    flag_groups = known_flags.reshape(batches, group_size, LEN)
    cot_groups = cotangent.astype(jnp.float32).reshape(batches, group_size, LEN, D)

    def visit_group(running, member):
        token_block, flag_block, cot_block = member

        def apply_layer(inputs, *weights_in):
            return forward(inputs, flag_block, *weights_in)
        result, pullback = jax.vjp(apply_layer, token_block, *parameters)
        gradients = pullback(cot_block)
        updated = tuple((a + b for a, b in zip(running, gradients[1:])))
        return (updated, (result, gradients[0]))
    initial = tuple((jnp.zeros(p.shape, jnp.float32) for p in parameters))
    summed, (outputs, input_grads) = lax.scan(visit_group, initial, (token_groups, flag_groups, cot_groups))
    layer_out = outputs.reshape(CELLS, LEN, D).astype(jnp.bfloat16)
    grad_tokens = input_grads.reshape(CELLS, LEN, D)
    return (layer_out, grad_tokens, summed[0], summed[1], summed[2], summed[3], summed[4], summed[5], summed[6], summed[7], summed[8], summed[9], summed[10], summed[11], summed[12], summed[13], summed[14])
```

```python
import functools
import math

import jax
import jax.numpy as jnp
from jax import lax
from jax.experimental import pallas as pl
from jax.experimental.pallas import tpu as pltpu
from jax.sharding import PartitionSpec as P

HEADS = 8
EPSILON = 1e-05
LOG2E = math.log2(math.e)
NONE = -1e30
NN = (((1,), (0,)), ((), ()))
NT = (((1,), (1,)), ((), ()))
TN = (((0,), (0,)), ((), ()))
f32 = jnp.float32
bf16 = jnp.bfloat16
VMEM_BYTES = 60 * 1024 * 1024


def dot(a, b, dims=NN):
    return lax.dot_general(a, b, dims, preferred_element_type=f32)


def sizes_of(length):
    picked = [length * 13 // 24 // 64 * 64, length * 2 // 3 // 64 * 64]
    return [s for s in picked if s] + [length]


def by_size(count, sizes, run):
    low = 0
    for at, size in enumerate(sizes):
        fits = count <= size
        if at:
            fits = fits & (count > low)
        pl.when(fits)(functools.partial(run, size))
        low = size


def chunks_of(total, width):
    return [(at, min(width, total - at)) for at in range(0, total, width)]


def forward_kernel(
    sizes,
    count_ref,
    place_ref,
    hidden_ref,
    own_ref,
    other_ref,
    wqT_ref,
    wkT_ref,
    wk_ref,
    wvT_ref,
    bq_ref,
    bv_ref,
    mix_ref,
    lse_ref,
    self_ref,
    q_ref,
    ko_ref,
    vo_ref,
    packed_ref,
    keys_ref,
    k_s,
    v_s,
):
    heads, size, rows = q_ref.shape
    pairs = heads // 2
    model = heads * size
    scale = size ** (-0.5) * LOG2E
    count = count_ref[0]
    half = own_ref.shape[0]
    x_own = own_ref[0:rows, :]
    q = (dot(wqT_ref[...], x_own, NT) + bq_ref[...]).astype(bf16)
    ko = dot(wkT_ref[...], x_own, NT).astype(bf16)
    vo = (dot(wvT_ref[...], x_own, NT) + bv_ref[...]).astype(bf16)
    q_ref[...] = q.reshape(heads, size, rows)
    ko_ref[...] = ko.reshape(heads, size, rows)
    vo_ref[...] = vo.reshape(heads, size, rows)
    own_score = (q.astype(f32) * ko.astype(f32)).reshape(heads, size, rows).sum(1, keepdims=True)
    self_ref[...] = jnp.where(hidden_ref[...][None] > 0, own_score * scale, NONE)
    step = 256 if rows % 256 == 0 else 384 if rows % 384 == 0 else rows

    def run(n):
        spot = lax.broadcasted_iota(jnp.int32, (n, half), 0)
        pick_own = (spot == place_ref[:, 0:half]).astype(f32).astype(bf16)
        pick_other = (spot == place_ref[:, half:]).astype(f32).astype(bf16)
        packed = (dot(pick_own, own_ref[...]) + dot(pick_other, other_ref[...])).astype(bf16)
        packed_ref[0:n, :] = packed
        keys = dot(packed, wk_ref[...]).astype(bf16)
        keys_ref[0:n, :] = keys
        for p in range(pairs):
            k_s[p, 0:n, :] = keys[:, p * 2 * size : (p + 1) * 2 * size]
        v_s[:, :, 0:n] = (
            (dot(wvT_ref[...], packed, NT) + bv_ref[...]).astype(bf16).reshape(heads, size, n)
        )

        def pair(p, carry):
            k_pair = k_s[p, 0:n, :]
            for t in range(2):
                h = 2 * p + t
                for at, wide in chunks_of(rows, step):
                    q_head = q_ref[h, :, at : at + wide]
                    blank = jnp.zeros_like(q_head)
                    q_full = jnp.concatenate([q_head, blank] if t == 0 else [blank, q_head], 0)
                    raw = dot(k_pair, q_full)
                    seen = lax.broadcasted_iota(jnp.int32, raw.shape, 0) < count
                    scores = jnp.where(seen, raw * scale, NONE)
                    own = self_ref[h, :, at : at + wide]
                    top = jnp.maximum(jnp.max(scores, axis=0, keepdims=True), own)
                    weights = jnp.exp2(scores - top)
                    own_weight = jnp.exp2(own - top)
                    total = jnp.sum(weights, axis=0, keepdims=True) + own_weight
                    mixed = dot(v_s[h, :, 0:n], weights.astype(bf16))
                    mixed = mixed + own_weight * vo_ref[h, :, at : at + wide].astype(f32)
                    mix_ref[h, :, at : at + wide] = (mixed / total).astype(bf16)
                    lse_ref[h, :, at : at + wide] = top + jnp.log(total) * LOG2E
            return carry

        lax.fori_loop(0, pairs, pair, 0)

    by_size(count, sizes, run)


def attention_forward(count, place, hidden, own, other, weights, rows):
    wqT, wkT, wk, wvT, bq, bv = weights
    half, model = own.shape
    length = 2 * half
    size = model // HEADS
    vmem = pl.BlockSpec(memory_space=pltpu.VMEM)
    head_rows = jax.ShapeDtypeStruct((HEADS, size, rows), bf16)
    row_stat = jax.ShapeDtypeStruct((HEADS, 1, rows), f32)
    return pl.pallas_call(
        functools.partial(forward_kernel, sizes_of(length)),
        out_shape=(
            head_rows,
            row_stat,
            row_stat,
            head_rows,
            head_rows,
            head_rows,
            jax.ShapeDtypeStruct((length, model), bf16),
            jax.ShapeDtypeStruct((length, model), bf16),
        ),
        in_specs=[pl.BlockSpec(memory_space=pltpu.SMEM)] + [vmem] * 10,
        out_specs=(vmem,) * 8,
        scratch_shapes=[
            pltpu.VMEM((HEADS // 2, length, 2 * size), bf16),
            pltpu.VMEM((HEADS, size, length), bf16),
        ],
        compiler_params=pltpu.CompilerParams(vmem_limit_bytes=VMEM_BYTES),
        cost_estimate=pl.CostEstimate(
            flops=16 * rows * length * model, bytes_accessed=8 << 20, transcendentals=0
        ),
        name="attention_forward",
    )(count, place, hidden, own, other, wqT, wkT, wk, wvT, bq, bv)


def middle_kernel(
    has_before,
    mix_ref,
    x_ref,
    cot_ref,
    w_out_ref,
    w_up_ref,
    w_down_ref,
    vec_ref,
    *rest,
):
    if has_before:
        before_w_ref, before_v_ref, *rest = rest
    out_ref, gh1_ref, gmix_ref, delta_ref, dw_ref, dv_ref, w_acc, v_acc = rest
    step = pl.program_id(0)
    model = x_ref.shape[1]

    @pl.when(step == 0)
    def _():
        if has_before:
            w_acc[...] = before_w_ref[...]
            v_acc[...] = before_v_ref[...]
        else:
            w_acc[...] = jnp.zeros_like(w_acc)
            v_acc[...] = jnp.zeros_like(v_acc)

    b_out, gain_one, shift_one, b_up, b_down, gain_two, shift_two = (
        vec_ref[i : i + 1, :] for i in range(7)
    )

    def mean(v):
        return jnp.mean(v, axis=-1, keepdims=True)

    def rows(v):
        return jnp.sum(v, axis=0, keepdims=True)

    attn_in = mix_ref[...]
    h1 = x_ref[...].astype(f32) + dot(attn_in, w_out_ref[...], TN) + b_out
    c1 = h1 - mean(h1)
    inv1 = lax.rsqrt(mean(c1 * c1) + EPSILON)
    n1 = c1 * inv1
    x1 = n1 * gain_one + shift_one
    x1_low = x1.astype(bf16)
    up = dot(x1_low, w_up_ref[...]) + b_up
    cdf = 0.5 + 0.5 * lax.erf(up * (0.5**0.5))
    slope = cdf + up * (jnp.exp(-0.5 * up * up) * (1.0 / math.sqrt(2.0 * math.pi)))
    act = (up * cdf).astype(bf16)
    h2 = x1 + dot(act, w_down_ref[...]) + b_down
    c2 = h2 - mean(h2)
    inv2 = lax.rsqrt(mean(c2 * c2) + EPSILON)
    n2 = c2 * inv2
    out_ref[...] = (n2 * gain_two + shift_two).astype(bf16)
    cot = cot_ref[...].astype(f32)
    g_gain_two = rows(cot * n2)
    g_shift_two = rows(cot)
    gn2 = cot * gain_two
    gh2 = inv2 * (gn2 - mean(gn2) - n2 * mean(gn2 * n2))
    g_down = gh2.astype(bf16)
    w_acc[2 * model :, :] += dot(act, g_down, TN)
    g_b_down = rows(g_down.astype(f32))
    g_up = (slope * dot(g_down, w_down_ref[...], NT)).astype(bf16)
    w_acc[model : 2 * model, :] += dot(x1_low, g_up, TN)
    g_b_up = rows(g_up.astype(f32))
    gx1 = gh2 + dot(g_up, w_up_ref[...], NT)
    g_gain_one = rows(gx1 * n1)
    g_shift_one = rows(gx1)
    gn1 = gx1 * gain_one
    gh1 = inv1 * (gn1 - mean(gn1) - n1 * mean(gn1 * n1))
    gh1_ref[...] = gh1
    g_attn = gh1.astype(bf16)
    w_acc[0:model, :] += dot(attn_in, g_attn)
    g_b_out = rows(g_attn.astype(f32))
    g_mix = dot(w_out_ref[...], g_attn, NT).astype(bf16)
    gmix_ref[...] = g_mix
    delta_ref[...] = (
        (g_mix.astype(f32) * attn_in.astype(f32)).reshape(HEADS, model // HEADS, -1).sum(1)
    )
    sums = (g_b_out, g_gain_one, g_shift_one, g_b_up, g_b_down, g_gain_two, g_shift_two)
    for at, term in enumerate(sums):
        v_acc[at : at + 1, :] += term

    @pl.when(step == pl.num_programs(0) - 1)
    def _():
        dw_ref[...] = w_acc[...].astype(dw_ref.dtype)
        dv_ref[...] = v_acc[...].astype(dv_ref.dtype)


def middle(mix, x, cot, weights, vectors, before, block):
    rows, model = cot.shape
    whole = lambda shape: pl.BlockSpec(shape, lambda i: (0,) * len(shape))
    by_row = pl.BlockSpec((block, model), lambda i: (i, 0))
    by_column = pl.BlockSpec((model, block), lambda i: (0, i))
    square = whole((model, model))
    sums = [whole((3 * model, model)), whole((16, model))]
    kept = f32 if before is None else bf16
    return pl.pallas_call(
        functools.partial(middle_kernel, before is not None),
        grid=(rows // block,),
        out_shape=(
            jax.ShapeDtypeStruct((rows, model), bf16),
            jax.ShapeDtypeStruct((rows, model), f32),
            jax.ShapeDtypeStruct((model, rows), bf16),
            jax.ShapeDtypeStruct((HEADS, rows), f32),
            jax.ShapeDtypeStruct((3 * model, model), kept),
            jax.ShapeDtypeStruct((16, model), kept),
        ),
        in_specs=[by_column, by_row, by_row, square, square, square, whole(vectors.shape)]
        + (sums if before is not None else []),
        out_specs=(
            by_row,
            by_row,
            by_column,
            pl.BlockSpec((HEADS, block), lambda i: (0, i)),
            *sums,
        ),
        scratch_shapes=[pltpu.VMEM((3 * model, model), f32), pltpu.VMEM((16, model), f32)],
        compiler_params=pltpu.CompilerParams(
            vmem_limit_bytes=VMEM_BYTES, dimension_semantics=("arbitrary",)
        ),
        cost_estimate=pl.CostEstimate(
            flops=36 * rows * model * model, bytes_accessed=8 << 20, transcendentals=0
        ),
        name="middle",
    )(mix, x, cot, *weights, vectors, *(before or ()))


def backward_kernel(
    sizes,
    has_before,
    count_ref,
    column_ref,
    own_ref,
    wqT_ref,
    wkT_ref,
    wv_ref,
    wvT_ref,
    bv_ref,
    q_ref,
    ko_ref,
    vo_ref,
    packed_ref,
    keys_ref,
    lse_ref,
    self_ref,
    gmix_ref,
    delta_ref,
    gh1_ref,
    *rest,
):
    if has_before:
        before_w_ref, before_v_ref, *rest = rest
    kept_ref, sent_ref, dw_ref, dv_ref, k_s, kT_s, v_s, gk_s, gv_s, gq_s, gko_s, gvo_s, w_acc, v_acc, full_s = rest
    heads, size, rows = q_ref.shape
    pairs = heads // 2
    model = heads * size
    length = packed_ref.shape[0]
    half = length // 2
    plain = size ** (-0.5)
    scale = plain * LOG2E
    count = count_ref[0]
    step = 256 if rows % 256 == 0 else 384 if rows % 384 == 0 else rows

    def run(n):
        packed = packed_ref[0:n, :]
        kT_s[:, :, 0:n] = dot(wkT_ref[...], packed, NT).astype(bf16).reshape(heads, size, n)
        values = (dot(packed, wv_ref[...]) + bv_ref[...]).astype(bf16)
        for p in range(pairs):
            k_s[p, 0:n, :] = keys_ref[0:n, p * 2 * size : (p + 1) * 2 * size]
            v_s[p, 0:n, :] = values[:, p * 2 * size : (p + 1) * 2 * size]

        def pair(p, carry):
            k_pair = k_s[p, 0:n, :]
            v_pair = v_s[p, 0:n, :]
            gk = jnp.zeros((n, 2 * size), f32)
            gv = jnp.zeros((n, 2 * size), f32)
            for t in range(2):
                h = 2 * p + t
                for at, wide in chunks_of(rows, step):
                    q_head = q_ref[h, :, at : at + wide]
                    gm_head = gmix_ref[h, :, at : at + wide]
                    blank = jnp.zeros_like(q_head)
                    fill = lambda v: jnp.concatenate([v, blank] if t == 0 else [blank, v], 0)
                    q_full = fill(q_head)
                    gm_full = fill(gm_head)
                    lse = lse_ref[h, :, at : at + wide]
                    delta = delta_ref[h, :, at : at + wide]
                    raw = dot(k_pair, q_full)
                    seen = lax.broadcasted_iota(jnp.int32, raw.shape, 0) < count
                    weights = jnp.where(seen, jnp.exp2(raw * scale - lse), 0.0)
                    g_weights = dot(v_pair, gm_full)
                    g_raw = ((plain * weights) * (g_weights - delta)).astype(bf16)
                    gv = gv + dot(weights.astype(bf16), gm_full, NT)
                    gk = gk + dot(g_raw, q_full, NT)
                    gq = dot(kT_s[h, :, 0:n], g_raw)
                    own_weight = jnp.exp2(self_ref[h, :, at : at + wide] - lse)
                    ko = ko_ref[h, :, at : at + wide].astype(f32)
                    vo = vo_ref[h, :, at : at + wide].astype(f32)
                    gm = gm_head.astype(f32)
                    g_own = jnp.sum(gm * vo, axis=0, keepdims=True)
                    g_own_raw = (plain * own_weight * (g_own - delta)).astype(bf16).astype(f32)
                    gq_s[h, :, at : at + wide] = (gq + g_own_raw * ko).astype(bf16)
                    gko_s[h, :, at : at + wide] = (g_own_raw * q_head.astype(f32)).astype(bf16)
                    gvo_s[h, :, at : at + wide] = (own_weight * gm).astype(bf16)
            gk_s[p, 0:n, :] = gk.astype(bf16)
            gv_s[p, 0:n, :] = gv.astype(bf16)
            return carry

        lax.fori_loop(0, pairs, pair, 0)
        gk = jnp.concatenate([gk_s[p, 0:n, :] for p in range(pairs)], 1)
        gv = jnp.concatenate([gv_s[p, 0:n, :] for p in range(pairs)], 1)
        w_acc[model : 2 * model, :] = dot(gk, packed, TN)
        w_acc[2 * model :, :] = dot(gv, packed, TN)
        v_acc[1:2, :] = jnp.sum(gv.astype(f32), axis=0, keepdims=True)
        g_packed = (dot(gk, wkT_ref[...]) + dot(gv, wvT_ref[...])).astype(bf16)
        spot = lax.broadcasted_iota(jnp.int32, (length, n), 1)
        place = (spot == column_ref[...]).astype(f32).astype(bf16)
        full_s[...] = dot(place, g_packed)

    by_size(count, sizes, run)
    gq = gq_s[...].reshape(model, rows)
    gko = gko_s[...].reshape(model, rows)
    gvo = gvo_s[...].reshape(model, rows)
    x_own = own_ref[0:rows, :]
    ones = jnp.ones((8, rows), bf16)
    w_q = dot(gq, x_own)
    w_k = w_acc[model : 2 * model, :] + dot(gko, x_own)
    w_v = w_acc[2 * model :, :] + dot(gvo, x_own)
    v_q = dot(ones, gq, NT)[0:1, :]
    v_v = v_acc[1:2, :] + dot(ones, gvo, NT)[0:1, :]
    if has_before:
        w_q = w_q + before_w_ref[0:model, :]
        w_k = w_k + before_w_ref[model : 2 * model, :]
        w_v = w_v + before_w_ref[2 * model :, :]
        v_q = v_q + before_v_ref[0:1, :]
        v_v = v_v + before_v_ref[1:2, :]
    dw_ref[0:model, :] = w_q.astype(dw_ref.dtype)
    dw_ref[model : 2 * model, :] = w_k.astype(dw_ref.dtype)
    dw_ref[2 * model :, :] = w_v.astype(dw_ref.dtype)
    dv_ref[...] = jnp.concatenate([v_q, v_v, jnp.zeros((14, model), f32)], 0).astype(dv_ref.dtype)
    mine = dot(gq, wqT_ref[...], TN) + dot(gko, wkT_ref[...], TN) + dot(gvo, wvT_ref[...], TN)
    kept_ref[0:rows, :] = full_s[0:rows, :] + mine + gh1_ref[...]
    if rows < half:
        kept_ref[rows:, :] = full_s[rows:half, :]
    sent_ref[...] = full_s[half:, :].astype(bf16)


def attention_backward(count, column, own, weights, saved, grads, before, rows):
    wqT, wkT, wv, wvT, bv = weights
    half, model = own.shape
    length = 2 * half
    size = model // HEADS
    vmem = pl.BlockSpec(memory_space=pltpu.VMEM)
    kept = f32 if before is None else bf16
    inputs = (count, column, own, wqT, wkT, wv, wvT, bv, *saved, *grads, *(before or ()))
    by_pair = pltpu.VMEM((HEADS // 2, length, 2 * size), bf16)
    by_head = pltpu.VMEM((HEADS, size, rows), bf16)
    return pl.pallas_call(
        functools.partial(backward_kernel, sizes_of(length), before is not None),
        out_shape=(
            jax.ShapeDtypeStruct((half, model), f32),
            jax.ShapeDtypeStruct((half, model), bf16),
            jax.ShapeDtypeStruct((3 * model, model), kept),
            jax.ShapeDtypeStruct((16, model), kept),
        ),
        in_specs=[pl.BlockSpec(memory_space=pltpu.SMEM)] + [vmem] * (len(inputs) - 1),
        out_specs=(vmem,) * 4,
        scratch_shapes=[
            by_pair,
            pltpu.VMEM((HEADS, size, length), bf16),
            by_pair,
            by_pair,
            by_pair,
            by_head,
            by_head,
            by_head,
            pltpu.VMEM((3 * model, model), f32),
            pltpu.VMEM((8, model), f32),
            pltpu.VMEM((length, model), f32),
        ],
        compiler_params=pltpu.CompilerParams(vmem_limit_bytes=VMEM_BYTES),
        cost_estimate=pl.CostEstimate(
            flops=36 * rows * length * model, bytes_accessed=16 << 20, transcendentals=0
        ),
        name="attention_backward",
    )(*inputs)


def exchange(piece, axis, partner):
    count = lax.axis_size(axis)
    return lax.ppermute(piece, axis, [(i, i ^ partner) for i in range(count)])


def radices_of(count):
    radices = []
    while count > 1:
        radix = 4 if count % 4 == 0 else 2
        radices.append(radix)
        count //= radix
    return radices


def reduce_plan():
    plan = [("cells", 2, 1)]
    for axis, stride in (("blk", 1), ("cells", 2)):
        for radix in radices_of(lax.axis_size(axis) // stride):
            plan.append((axis, radix, stride))
            stride *= radix
    return plan


def sum_everywhere(big, small):
    plan = reduce_plan()
    tail = small.shape[0]
    for axis, radix, stride in plan:
        digit = (lax.axis_index(axis) // stride) % radix
        count = big.shape[0] // radix
        arrived = []
        for other in range(1, radix):
            piece = lax.dynamic_slice_in_dim(big, (digit ^ other) * count, count, 0)
            arrived.append(exchange(jnp.concatenate([piece, small], 0), axis, other * stride))
        big = lax.dynamic_slice_in_dim(big, digit * count, count, 0).astype(f32)
        small = small.astype(f32)
        for got in arrived:
            big = big + got[:count].astype(f32)
            small = small + got[count:].astype(f32)
        big, small = big.astype(bf16), small.astype(bf16)
    for axis, radix, stride in reversed(plan):
        digit = (lax.axis_index(axis) // stride) % radix
        parts = [big] + [exchange(big, axis, other * stride) for other in range(1, radix)]
        ordered = []
        for place in range(radix):
            chosen = parts[place]
            for d in range(1, radix):
                chosen = jnp.where(digit == d, parts[place ^ d], chosen)
            ordered.append(chosen)
        big = jnp.concatenate(ordered, 0)
    return big, small


def swap(parts, flag):
    first, second = parts
    return jnp.where(flag == 1, second, first), jnp.where(flag == 1, first, second)


def body(
    tokens,
    known_flags,
    w_query,
    b_query,
    w_key,
    w_value,
    b_value,
    w_out,
    b_out,
    gain_one,
    shift_one,
    w_up,
    b_up,
    w_down,
    b_down,
    gain_two,
    shift_two,
    cotangent,
):
    cells, rows, model = tokens.shape
    blocks = lax.axis_size("blk")
    places = lax.axis_size("cells")
    part = rows // 2
    half = 2 * rows
    length = 2 * half
    block = lax.axis_index("blk")
    core = lax.axis_index("cells") % 2
    x, y = block % 2, block // 2
    axes = ("blk", "cells")

    def route(i, j):
        pairs = []
        for b in range(blocks):
            for c in range(places):
                there = 2 * (c % 2) + ((b % 2) ^ i)
                pairs.append((b * places + c, there * places + c - c % 2 + ((b // 2) ^ j)))
        return pairs

    def route_back(i, j):
        return [(there, here) for here, there in route(i, j)]

    both = ((0, 0), (0, 1), (1, 0), (1, 1))

    def payload(source, i, j, cells_sent):
        rows_sent = lax.dynamic_slice_in_dim(source, (y ^ j) * part, part, 1)
        picked = []
        if 0 in cells_sent:
            picked.append(lax.dynamic_slice_in_dim(rows_sent, x ^ i, 1, 0))
        if 1 in cells_sent:
            picked.append(rows_sent[2:3])
        return jnp.concatenate(picked, 0)

    def send(source, i, j, cells_sent):
        return lax.ppermute(payload(source, i, j, cells_sent), axes, route(i, j))

    got = {ij: send(tokens, *ij, (0, 1)) for ij in both}
    own = [jnp.concatenate([got[ij][k] for ij in both], 0) for k in range(2)]
    other = [exchange(own[k], "cells", 1) for k in range(2)]

    flags = exchange(known_flags, "cells", 1)
    flags = jnp.where(core == y, known_flags, flags)
    flags = jnp.stack([jnp.where(x == 1, flags[1], flags[0]), flags[2]])
    grid = flags.reshape(2, 2, 2, 2, part)
    grid = jnp.where(x == 1, grid[:, :, ::-1], grid)
    turned = grid[:, ::-1]
    straight = (core == 0)
    first = jnp.where(straight, grid[:, :, :, 0], turned[:, :, :, 1])
    second = jnp.where(straight, turned[:, :, :, 1], grid[:, :, :, 0])
    order = lambda g: g.transpose(0, 2, 1, 3).reshape(2, half)
    flags = (jnp.concatenate([order(first), order(second)], 1) > 0).astype(f32)
    width = 128
    tiles = flags.reshape(2, length // width, width)
    lower = jnp.tril(jnp.ones((width, width), f32)).T
    inside = jnp.einsum("ctk,kl->ctl", tiles, lower, precision=lax.Precision.HIGHEST)
    totals = inside[:, :, -1]
    steps = jnp.triu(jnp.ones((length // width,) * 2, f32), 1)
    ahead = jnp.einsum("ct,ts->cs", totals, steps, precision=lax.Precision.HIGHEST)
    place = (inside + ahead[:, :, None]).reshape(2, length) - 1.0
    place = jnp.where(flags > 0, place, -1.0).astype(jnp.int32)
    counts = jnp.sum(flags, 1).astype(jnp.int32)
    hidden = 1.0 - flags

    wqT, wkT, wvT = w_query.T, w_key.T, w_value.T
    bq = b_query.astype(f32).reshape(model, 1)
    bv = b_value.astype(f32).reshape(model, 1)
    vectors = jnp.stack([b_out, gain_one, shift_one, b_up, b_down, gain_two, shift_two, b_value])
    vectors = vectors.astype(f32)

    cot_got = {ij: send(cotangent, *ij, (0, 1) if ij[0] == 0 else (0,)) for ij in both}
    cot = [
        jnp.concatenate([cot_got[ij][0] for ij in both], 0),
        jnp.concatenate([cot_got[0, j][1] for j in range(2)], 0),
    ]

    work = (half, rows)
    forward = [
        attention_forward(
            counts[k : k + 1],
            place[k : k + 1],
            hidden[k : k + 1, : work[k]],
            own[k],
            other[k],
            (wqT, wkT, w_key, wvT, bq, bv),
            work[k],
        )
        for k in range(2)
    ]
    sums = None
    mids = []
    for k in range(2):
        mix = forward[k][0].reshape(model, work[k])
        out, gh1, gmix, delta, *sums = middle(
            mix, own[k], cot[k], (w_out, w_up, w_down), vectors, sums, rows
        )
        size = model // HEADS
        mids.append((out, gmix.reshape(HEADS, size, work[k]), delta.reshape(HEADS, 1, work[k]), gh1))
    early, early_small = sum_everywhere(*sums)

    out_back = {}
    for i, j in both:
        pieces = [mids[0][0][(2 * i + j) * part : (2 * i + j + 1) * part]]
        if i == 0:
            pieces.append(mids[1][0][j * part : (j + 1) * part])
        out_back[i, j] = lax.ppermute(jnp.stack(pieces), axes, route_back(i, j))
    sums = None
    kept = []
    for k in range(2):
        mix, lse, own_score, q, ko, vo, packed, keys = forward[k]
        out, gmix, delta, gh1 = mids[k]
        mine, sent, *sums = attention_backward(
            counts[k : k + 1],
            place[k].reshape(length, 1),
            own[k],
            (wqT, wkT, w_value, wvT, vectors[7:8]),
            (q, ko, vo, packed, keys, lse, own_score),
            (gmix, delta, gh1),
            sums,
            work[k],
        )
        arrived = exchange(sent, "cells", 1)
        kept.append((mine + arrived.astype(f32)).astype(bf16))
    back = {}
    for i, j in both:
        at = (2 * i + j) * part
        back[i, j] = lax.ppermute(
            jnp.stack([kept[0][at : at + part], kept[1][at : at + part]]), axes, route_back(i, j)
        )
    late, late_small = sum_everywhere(*sums)

    def rejoin(from_i):
        return jnp.concatenate(swap(from_i, y), 1)

    def cells_of(near, far, last):
        return jnp.stack([*swap((near, far), x), last])

    near, far = (rejoin((back[i, 0].astype(f32), back[i, 1].astype(f32))) for i in range(2))
    grad_tokens = cells_of(near[0], far[0], near[1] + far[1])
    near, far = (rejoin((out_back[i, 0], out_back[i, 1])) for i in range(2))
    layer_out = cells_of(near[0], far[0], near[1])

    early, late = early.astype(f32), late.astype(f32)
    early_small, late_small = early_small.astype(f32), late_small.astype(f32)
    g_out, g_up, g_down = (early[n * model : (n + 1) * model] for n in range(3))
    g_query, g_key, g_value = (late[n * model : (n + 1) * model].T for n in range(3))
    g_b_out, g_gain_one, g_shift_one, g_b_up, g_b_down, g_gain_two, g_shift_two = (
        early_small[n] for n in range(7)
    )
    return (
        layer_out,
        grad_tokens,
        g_query,
        late_small[0],
        g_key,
        g_value,
        late_small[1],
        g_out,
        g_b_out,
        g_gain_one,
        g_shift_one,
        g_up,
        g_b_up,
        g_down,
        g_b_down,
        g_gain_two,
        g_shift_two,
    )


def solution(mesh):
    rows = P("cells", "blk", None)
    return jax.shard_map(
        body,
        mesh=mesh,
        in_specs=(rows, P("cells", None)) + (P(),) * 15 + (rows,),
        out_specs=(rows, rows) + (P(),) * 15,
        check_vma=False,
    )
```

```python
import functools
import math

import jax
import jax.numpy as jnp
from jax import lax
from jax.experimental import pallas as pl
from jax.experimental.pallas import tpu as pltpu
from jax.sharding import PartitionSpec as P

HEADS = 8
EPSILON = 1e-05
LOG2E = math.log2(math.e)
NONE = -1e30
NN = (((1,), (0,)), ((), ()))
NT = (((1,), (1,)), ((), ()))
TN = (((0,), (0,)), ((), ()))
f32 = jnp.float32
bf16 = jnp.bfloat16
VMEM_BYTES = 60 * 1024 * 1024
UNROLL = 2


def dot(a, b, dims=NN):
    return lax.dot_general(a, b, dims, preferred_element_type=f32)


def sizes_of(length):
    return [length * 13 // 24 // 64 * 64, length]


def by_size(count, sizes, run):
    low = 0
    for at, size in enumerate(sizes):
        fits = count <= size
        if at:
            fits = fits & (count > low)
        pl.when(fits)(functools.partial(run, size))
        low = size


def pad_heads(padded, whole):
    heads, double, _ = padded.shape
    size = double // 2
    blank = jnp.zeros((size, whole.shape[1]), whole.dtype)
    for h in range(heads):
        part = whole[h * size : (h + 1) * size, :]
        padded[h] = jnp.concatenate([part, blank] if h % 2 == 0 else [blank, part], 0)


def over_heads(run, heads, rows, common):
    if common:

        def step(i, carry):
            for t in range(UNROLL):
                run(UNROLL * i + t, 0, rows)
            return carry

        lax.fori_loop(0, heads // UNROLL, step, 0)
    else:
        wide = 128
        chunks = rows // wide

        def step(i, carry):
            run(i // chunks, pl.multiple_of(i % chunks * wide, wide), wide)
            return carry

        lax.fori_loop(0, heads * chunks, step, 0)


def places_kernel(here_ref, near_ref, far_ref, place_ref):
    x, y, core = here_ref[0], here_ref[1], here_ref[2]
    length = near_ref.shape[1]
    part = length // 8
    flags = jnp.where(core == y, near_ref[...], far_ref[...]).astype(f32)
    flags = jnp.concatenate([jnp.where(x == 1, flags[1:2], flags[0:1]), flags[2:3]], 0)
    pieces = {}
    for at in range(8):
        pieces[at // 4, at // 2 % 2, at % 2] = flags[:, at * part : (at + 1) * part]
    for bit, axis in ((core, 2), (x, 1)):
        turn = lambda k, axis=axis: tuple(1 - v if n == axis else v for n, v in enumerate(k))
        pieces = {k: jnp.where(bit == 1, pieces[turn(k)], v) for k, v in pieces.items()}
    ordered = []
    for side in range(2):
        for i in range(2):
            for j in range(2):
                swapped = core != side
                ordered.append(jnp.where(swapped, pieces[1 - j, i, side], pieces[j, i, side]))
    flags = jnp.concatenate(ordered, 1)
    width = 128
    rows = lax.broadcasted_iota(jnp.int32, (width, width), 0)
    lower = (rows <= lax.broadcasted_iota(jnp.int32, (width, width), 1)).astype(f32).astype(bf16)
    tiles = jnp.concatenate([flags[:, at : at + width] for at in range(0, length, width)], 0)
    inside = dot(tiles.astype(bf16), lower)
    ahead = jnp.full((2, 1), -1.0, f32)
    placed = []
    for at in range(length // width):
        tile = inside[2 * at : 2 * at + 2, :]
        placed.append(tile + ahead)
        ahead = ahead + tile[:, width - 1 :]
    place_ref[...] = jnp.where(flags > 0, jnp.concatenate(placed, 1), -1.0)


def places(here, near, far):
    vmem = pl.BlockSpec(memory_space=pltpu.VMEM)
    return pl.pallas_call(
        places_kernel,
        out_shape=jax.ShapeDtypeStruct((2, near.shape[1]), f32),
        in_specs=[pl.BlockSpec(memory_space=pltpu.SMEM), vmem, vmem],
        out_specs=vmem,
        name="places",
    )(here, near, far)


def count_of(place):
    return (jnp.max(place) + 1.0).astype(jnp.int32)


def column(row, lanes):
    return jnp.broadcast_to(row, (lanes, row.shape[1])).T[:, 0:1]


def forward_kernel(
    sizes,
    cell,
    place_ref,
    own_ref,
    other_ref,
    wqT_ref,
    wkT_ref,
    wk_ref,
    wvT_ref,
    vec_ref,
    mix_ref,
    lse_ref,
    self_ref,
    q_ref,
    ko_ref,
    vo_ref,
    packed_ref,
    keys_ref,
    k_s,
    v_s,
    q_s,
):
    heads, size, rows = q_ref.shape
    pairs = heads // 2
    model = heads * size
    scale = size ** (-0.5) * LOG2E
    place = place_ref[cell : cell + 1, :]
    count = count_of(place)
    half = own_ref.shape[0]
    length = 2 * half
    b_value = column(vec_ref[7:8, :], 8)
    x_own = own_ref[0:rows, :]
    q = (dot(wqT_ref[...], x_own, NT) + column(vec_ref[8:9, :], 8)).astype(bf16)
    ko = dot(wkT_ref[...], x_own, NT).astype(bf16)
    vo = (dot(wvT_ref[...], x_own, NT) + b_value).astype(bf16)
    q_ref[...] = q.reshape(heads, size, rows)
    ko_ref[...] = ko.reshape(heads, size, rows)
    vo_ref[...] = vo.reshape(heads, size, rows)
    own_score = (q.astype(f32) * ko.astype(f32)).reshape(heads, size, rows).sum(1, keepdims=True)
    self_ref[...] = jnp.where(place[None, :, 0:rows] < 0, own_score * scale, NONE)
    pad_heads(q_s, q)

    def run(n):
        spot = lax.broadcasted_iota(jnp.int32, (n, half), 0).astype(f32)
        pick_own = (spot == place[:, 0:half]).astype(f32).astype(bf16)
        pick_other = (spot == place[:, half:]).astype(f32).astype(bf16)
        packed = (dot(pick_own, own_ref[...]) + dot(pick_other, other_ref[...])).astype(bf16)
        packed_ref[0:n, :] = packed
        keys = dot(packed, wk_ref[...]).astype(bf16)
        keys_ref[0:n, :] = keys
        for p in range(pairs):
            k_s[p, 0:n, :] = keys[:, p * 2 * size : (p + 1) * 2 * size]
        v_s[:, :, 0:n] = (
            (dot(wvT_ref[...], packed, NT) + b_value).astype(bf16).reshape(heads, size, n)
        )

        def head(h, at, wide):
            raw = dot(k_s[h // 2, 0:n, :], q_s[h, :, pl.ds(at, wide)])
            seen = lax.broadcasted_iota(jnp.int32, raw.shape, 0) < count
            scores = jnp.where(seen, raw * scale, NONE)
            own = self_ref[h, :, pl.ds(at, wide)]
            top = jnp.maximum(jnp.max(scores, axis=0, keepdims=True), own)
            weights = jnp.exp2(scores - top)
            own_weight = jnp.exp2(own - top)
            total = jnp.sum(weights, axis=0, keepdims=True) + own_weight
            mixed = dot(v_s[h, :, 0:n], weights.astype(bf16))
            mixed = mixed + own_weight * vo_ref[h, :, pl.ds(at, wide)].astype(f32)
            mix_ref[h, :, pl.ds(at, wide)] = (mixed / total).astype(bf16)
            lse_ref[h, :, pl.ds(at, wide)] = top + jnp.log(total) * LOG2E

        over_heads(head, heads, rows, n < length)

    by_size(count, sizes, run)


def attention_forward(cell, place, own, other, weights, rows):
    half, model = own.shape
    length = 2 * half
    size = model // HEADS
    vmem = pl.BlockSpec(memory_space=pltpu.VMEM)
    head_rows = jax.ShapeDtypeStruct((HEADS, size, rows), bf16)
    row_stat = jax.ShapeDtypeStruct((HEADS, 1, rows), f32)
    return pl.pallas_call(
        functools.partial(forward_kernel, sizes_of(length), cell),
        out_shape=(
            head_rows,
            row_stat,
            row_stat,
            head_rows,
            head_rows,
            head_rows,
            jax.ShapeDtypeStruct((length, model), bf16),
            jax.ShapeDtypeStruct((length, model), bf16),
        ),
        in_specs=[vmem] * (3 + len(weights)),
        out_specs=(vmem,) * 8,
        scratch_shapes=[
            pltpu.VMEM((HEADS // 2, length, 2 * size), bf16),
            pltpu.VMEM((HEADS, size, length), bf16),
            pltpu.VMEM((HEADS, 2 * size, rows), bf16),
        ],
        compiler_params=pltpu.CompilerParams(vmem_limit_bytes=VMEM_BYTES),
        cost_estimate=pl.CostEstimate(
            flops=16 * rows * length * model, bytes_accessed=8 << 20, transcendentals=0
        ),
        name="attention_forward",
    )(place, own, other, *weights)


def middle_kernel(
    mix_a_ref,
    x_a_ref,
    cot_a_ref,
    mix_b_ref,
    x_b_ref,
    cot_b_ref,
    w_out_ref,
    w_up_ref,
    w_down_ref,
    vec_ref,
    *rest,
):
    outs_a, outs_b, (dw_ref, dv_ref, mix_ref, x_ref, cot_ref, w_acc, v_acc) = rest[:4], rest[4:8], rest[8:]
    step = pl.program_id(0)
    last = pl.num_programs(0) - 1
    model = x_ref.shape[1]

    @pl.when(step == 0)
    def _():
        w_acc[...] = jnp.zeros_like(w_acc)
        v_acc[...] = jnp.zeros_like(v_acc)

    @pl.when(step < last)
    def _():
        mix_ref[...] = mix_a_ref[...]
        x_ref[...] = x_a_ref[...]
        cot_ref[...] = cot_a_ref[...]

    @pl.when(step == last)
    def _():
        mix_ref[...] = mix_b_ref[...]
        x_ref[...] = x_b_ref[...]
        cot_ref[...] = cot_b_ref[...]

    b_out, gain_one, shift_one, b_up, b_down, gain_two, shift_two = (
        vec_ref[i : i + 1, :] for i in range(7)
    )

    def mean(v):
        return jnp.mean(v, axis=-1, keepdims=True)

    def rows(v):
        return jnp.sum(v, axis=0, keepdims=True)

    attn_in = mix_ref[...]
    h1 = x_ref[...].astype(f32) + dot(attn_in, w_out_ref[...], TN) + b_out
    c1 = h1 - mean(h1)
    inv1 = lax.rsqrt(mean(c1 * c1) + EPSILON)
    n1 = c1 * inv1
    x1 = n1 * gain_one + shift_one
    x1_low = x1.astype(bf16)
    up = dot(x1_low, w_up_ref[...]) + b_up
    cdf = 0.5 + 0.5 * lax.erf(up * (0.5**0.5))
    slope = cdf + up * (jnp.exp(-0.5 * up * up) * (1.0 / math.sqrt(2.0 * math.pi)))
    act = (up * cdf).astype(bf16)
    h2 = x1 + dot(act, w_down_ref[...]) + b_down
    c2 = h2 - mean(h2)
    inv2 = lax.rsqrt(mean(c2 * c2) + EPSILON)
    n2 = c2 * inv2
    out = (n2 * gain_two + shift_two).astype(bf16)
    cot = cot_ref[...].astype(f32)
    g_gain_two = rows(cot * n2)
    g_shift_two = rows(cot)
    gn2 = cot * gain_two
    gh2 = inv2 * (gn2 - mean(gn2) - n2 * mean(gn2 * n2))
    g_down = gh2.astype(bf16)
    w_acc[2 * model :, :] += dot(act, g_down, TN)
    g_b_down = rows(g_down.astype(f32))
    g_up = (slope * dot(g_down, w_down_ref[...], NT)).astype(bf16)
    w_acc[model : 2 * model, :] += dot(x1_low, g_up, TN)
    g_b_up = rows(g_up.astype(f32))
    gx1 = gh2 + dot(g_up, w_up_ref[...], NT)
    g_gain_one = rows(gx1 * n1)
    g_shift_one = rows(gx1)
    gn1 = gx1 * gain_one
    gh1 = inv1 * (gn1 - mean(gn1) - n1 * mean(gn1 * n1))
    g_attn = gh1.astype(bf16)
    w_acc[0:model, :] += dot(attn_in, g_attn)
    g_b_out = rows(g_attn.astype(f32))
    g_mix = dot(w_out_ref[...], g_attn, NT).astype(bf16)
    size = model // HEADS
    delta = (g_mix.astype(f32) * attn_in.astype(f32)).reshape(HEADS, size, -1).sum(1, keepdims=True)
    results = (out, gh1, g_mix.reshape(HEADS, size, -1), delta)
    sums = (g_b_out, g_gain_one, g_shift_one, g_b_up, g_b_down, g_gain_two, g_shift_two)
    for at, term in enumerate(sums):
        v_acc[at : at + 1, :] += term

    @pl.when(step < last)
    def _():
        for ref, value in zip(outs_a, results):
            ref[...] = value

    @pl.when(step == last)
    def _():
        for ref, value in zip(outs_b, results):
            ref[...] = value
        dw_ref[...] = w_acc[...].astype(bf16)
        dv_ref[...] = v_acc[...].astype(bf16)


def middle(mix, x, cot, weights, vectors):
    block, model = cot[1].shape
    size = model // HEADS
    steps = cot[0].shape[0] // block
    whole = lambda shape: pl.BlockSpec(shape, lambda i: (0,) * len(shape))
    places = (lambda i: jnp.minimum(i, steps - 1), lambda i: 0)
    by_row = [pl.BlockSpec((block, model), lambda i, at=at: (at(i), 0)) for at in places]
    by_column = [pl.BlockSpec((model, block), lambda i, at=at: (0, at(i))) for at in places]
    by_head = [pl.BlockSpec((HEADS, size, block), lambda i, at=at: (0, 0, at(i))) for at in places]
    stats = [pl.BlockSpec((HEADS, 1, block), lambda i, at=at: (0, 0, at(i))) for at in places]
    square = whole((model, model))
    inputs, in_specs, out_shape, out_specs = [], [], [], []
    for k in range(2):
        rows = cot[k].shape[0]
        inputs += [mix[k], x[k], cot[k]]
        in_specs += [by_column[k], by_row[k], by_row[k]]
        out_shape += [
            jax.ShapeDtypeStruct((rows, model), bf16),
            jax.ShapeDtypeStruct((rows, model), f32),
            jax.ShapeDtypeStruct((HEADS, size, rows), bf16),
            jax.ShapeDtypeStruct((HEADS, 1, rows), f32),
        ]
        out_specs += [by_row[k], by_row[k], by_head[k], stats[k]]
    return pl.pallas_call(
        middle_kernel,
        grid=(steps + 1,),
        out_shape=(
            *out_shape,
            jax.ShapeDtypeStruct((3 * model, model), bf16),
            jax.ShapeDtypeStruct((16, model), bf16),
        ),
        in_specs=[*in_specs, square, square, square, whole(vectors.shape)],
        out_specs=(*out_specs, whole((3 * model, model)), whole((16, model))),
        scratch_shapes=[
            pltpu.VMEM((model, block), bf16),
            pltpu.VMEM((block, model), bf16),
            pltpu.VMEM((block, model), bf16),
            pltpu.VMEM((3 * model, model), f32),
            pltpu.VMEM((16, model), f32),
        ],
        compiler_params=pltpu.CompilerParams(
            vmem_limit_bytes=VMEM_BYTES, dimension_semantics=("arbitrary",)
        ),
        cost_estimate=pl.CostEstimate(
            flops=36 * (steps + 1) * block * model * model,
            bytes_accessed=8 << 20,
            transcendentals=0,
        ),
        name="middle",
    )(*inputs, *weights, vectors)


def backward_kernel(
    sizes,
    has_before,
    cell,
    place_ref,
    own_ref,
    wqT_ref,
    wkT_ref,
    wv_ref,
    wvT_ref,
    vec_ref,
    q_ref,
    ko_ref,
    vo_ref,
    packed_ref,
    keys_ref,
    lse_ref,
    self_ref,
    gmix_ref,
    delta_ref,
    gh1_ref,
    *rest,
):
    if has_before:
        before_w_ref, before_v_ref, *rest = rest
    kept_ref, sent_ref, dw_ref, dv_ref, k_s, kT_s, v_s, gk_s, gv_s, gq_s, gko_s, gvo_s, w_acc, v_acc, full_s, q_s, gm_s = rest
    heads, size, rows = q_ref.shape
    pairs = heads // 2
    model = heads * size
    length = packed_ref.shape[0]
    half = length // 2
    plain = size ** (-0.5)
    scale = plain * LOG2E
    place = place_ref[cell : cell + 1, :]
    count = count_of(place)
    pad_heads(q_s, q_ref[...].reshape(model, rows))
    pad_heads(gm_s, gmix_ref[...].reshape(model, rows))

    def run(n):
        packed = packed_ref[0:n, :]
        kT_s[:, :, 0:n] = dot(wkT_ref[...], packed, NT).astype(bf16).reshape(heads, size, n)
        values = (dot(packed, wv_ref[...]) + vec_ref[7:8, :]).astype(bf16)
        for p in range(pairs):
            k_s[p, 0:n, :] = keys_ref[0:n, p * 2 * size : (p + 1) * 2 * size]
            v_s[p, 0:n, :] = values[:, p * 2 * size : (p + 1) * 2 * size]

        def head(h, at, wide):
            here = pl.ds(at, wide)
            k_pair = k_s[h // 2, 0:n, :]
            v_pair = v_s[h // 2, 0:n, :]
            q_full = q_s[h, :, here]
            gm_full = gm_s[h, :, here]
            lse = lse_ref[h, :, here]
            delta = delta_ref[h, :, here]
            raw = dot(k_pair, q_full)
            seen = lax.broadcasted_iota(jnp.int32, raw.shape, 0) < count
            weights = jnp.where(seen, jnp.exp2(raw * scale - lse), 0.0)
            g_weights = dot(v_pair, gm_full)
            g_raw = ((plain * weights) * (g_weights - delta)).astype(bf16)
            gv_s[h // 2, 0:n, :] += dot(weights.astype(bf16), gm_full, NT)
            gk_s[h // 2, 0:n, :] += dot(g_raw, q_full, NT)
            gq = dot(kT_s[h, :, 0:n], g_raw)
            own_weight = jnp.exp2(self_ref[h, :, here] - lse)
            ko = ko_ref[h, :, here].astype(f32)
            vo = vo_ref[h, :, here].astype(f32)
            gm = gmix_ref[h, :, here].astype(f32)
            g_own = jnp.sum(gm * vo, axis=0, keepdims=True)
            g_own_raw = (plain * own_weight * (g_own - delta)).astype(bf16).astype(f32)
            gq_s[h, :, here] = (gq + g_own_raw * ko).astype(bf16)
            gko_s[h, :, here] = (g_own_raw * q_ref[h, :, here].astype(f32)).astype(bf16)
            gvo_s[h, :, here] = (own_weight * gm).astype(bf16)

        gk_s[:, 0:n, :] = jnp.zeros((pairs, n, 2 * size), f32)
        gv_s[:, 0:n, :] = jnp.zeros((pairs, n, 2 * size), f32)
        over_heads(head, heads, rows, n < length)
        gk = jnp.concatenate([gk_s[p, 0:n, :] for p in range(pairs)], 1).astype(bf16)
        gv = jnp.concatenate([gv_s[p, 0:n, :] for p in range(pairs)], 1).astype(bf16)
        w_acc[model : 2 * model, :] = dot(gk, packed, TN)
        w_acc[2 * model :, :] = dot(gv, packed, TN)
        v_acc[1:2, :] = jnp.sum(gv.astype(f32), axis=0, keepdims=True)
        g_packed = (dot(gk, wkT_ref[...]) + dot(gv, wvT_ref[...])).astype(bf16)
        spot = lax.broadcasted_iota(jnp.int32, (length, n), 1).astype(f32)
        spread = (spot == column(place, 8)).astype(f32).astype(bf16)
        full_s[...] = dot(spread, g_packed)

    by_size(count, sizes, run)
    gq = gq_s[...].reshape(model, rows)
    gko = gko_s[...].reshape(model, rows)
    gvo = gvo_s[...].reshape(model, rows)
    x_own = own_ref[0:rows, :]
    ones = jnp.ones((8, rows), bf16)
    w_q = dot(gq, x_own)
    w_k = w_acc[model : 2 * model, :] + dot(gko, x_own)
    w_v = w_acc[2 * model :, :] + dot(gvo, x_own)
    v_q = dot(ones, gq, NT)[0:1, :]
    v_v = v_acc[1:2, :] + dot(ones, gvo, NT)[0:1, :]
    if has_before:
        w_q = w_q + before_w_ref[0:model, :]
        w_k = w_k + before_w_ref[model : 2 * model, :]
        w_v = w_v + before_w_ref[2 * model :, :]
        v_q = v_q + before_v_ref[8:9, :]
        v_v = v_v + before_v_ref[9:10, :]
    for at, total in enumerate((w_q, w_k, w_v)):
        total = total.T if has_before else total
        dw_ref[at * model : (at + 1) * model, :] = total.astype(dw_ref.dtype)
    blank = jnp.zeros((8, model), f32)
    dv_ref[...] = jnp.concatenate([blank, v_q, v_v, blank[2:]], 0).astype(dv_ref.dtype)
    mine = dot(gq, wqT_ref[...], TN) + dot(gko, wkT_ref[...], TN) + dot(gvo, wvT_ref[...], TN)
    kept_ref[0:rows, :] = full_s[0:rows, :] + mine + gh1_ref[...]
    if rows < half:
        kept_ref[rows:, :] = full_s[rows:half, :]
    sent_ref[...] = full_s[half:, :].astype(bf16)


def attention_backward(cell, place, own, weights, saved, grads, before, rows):
    half, model = own.shape
    length = 2 * half
    size = model // HEADS
    vmem = pl.BlockSpec(memory_space=pltpu.VMEM)
    kept = f32 if before is None else bf16
    inputs = (place, own, *weights, *saved, *grads, *(before or ()))
    by_pair = pltpu.VMEM((HEADS // 2, length, 2 * size), bf16)
    by_head = pltpu.VMEM((HEADS, size, rows), bf16)
    pair_sum = pltpu.VMEM((HEADS // 2, length, 2 * size), f32)
    padded = pltpu.VMEM((HEADS, 2 * size, rows), bf16)
    return pl.pallas_call(
        functools.partial(backward_kernel, sizes_of(length), before is not None, cell),
        out_shape=(
            jax.ShapeDtypeStruct((half, model), f32),
            jax.ShapeDtypeStruct((half, model), bf16),
            jax.ShapeDtypeStruct((3 * model, model), kept),
            jax.ShapeDtypeStruct((16, model), kept),
        ),
        in_specs=[vmem] * len(inputs),
        out_specs=(vmem,) * 4,
        scratch_shapes=[
            by_pair,
            pltpu.VMEM((HEADS, size, length), bf16),
            by_pair,
            pair_sum,
            pair_sum,
            by_head,
            by_head,
            by_head,
            pltpu.VMEM((3 * model, model), f32),
            pltpu.VMEM((8, model), f32),
            pltpu.VMEM((length, model), f32),
            padded,
            padded,
        ],
        compiler_params=pltpu.CompilerParams(vmem_limit_bytes=VMEM_BYTES),
        cost_estimate=pl.CostEstimate(
            flops=36 * rows * length * model, bytes_accessed=16 << 20, transcendentals=0
        ),
        name="attention_backward",
    )(*inputs)


def exchange(piece, axis, partner):
    count = lax.axis_size(axis)
    return lax.ppermute(piece, axis, [(i, i ^ partner) for i in range(count)])


def radices_of(count):
    radices = []
    while count > 1:
        radix = 4 if count % 4 == 0 else 2
        radices.append(radix)
        count //= radix
    return radices


def reduce_plan():
    plan = [("cells", 2, 1)]
    for axis, stride in (("blk", 1), ("cells", 2)):
        for radix in radices_of(lax.axis_size(axis) // stride):
            plan.append((axis, radix, stride))
            stride *= radix
    return plan


def reduce_step(step, big, small):
    axis, radix, stride = step
    digit = (lax.axis_index(axis) // stride) % radix
    parts, rows, model = big.shape
    count = rows // radix
    arrived = []
    for other in range(1, radix):
        piece = lax.dynamic_slice_in_dim(big, (digit ^ other) * count, count, 1)
        sent = jnp.concatenate([piece.reshape(parts * count, model), small], 0)
        arrived.append(exchange(sent, axis, other * stride))
    big = lax.dynamic_slice_in_dim(big, digit * count, count, 1).astype(f32)
    small = small.astype(f32)
    for got in arrived:
        big = big + got[: parts * count].reshape(parts, count, model).astype(f32)
        small = small + got[parts * count :].astype(f32)
    return big.astype(bf16), small.astype(bf16)


def gather_step(step, big):
    axis, radix, stride = step
    digit = (lax.axis_index(axis) // stride) % radix
    parts = [big] + [exchange(big, axis, other * stride) for other in range(1, radix)]
    ordered = []
    for place in range(radix):
        chosen = parts[place]
        for d in range(1, radix):
            chosen = jnp.where(digit == d, parts[place ^ d], chosen)
        ordered.append(chosen)
    return jnp.concatenate(ordered, 1)


def swap(parts, flag):
    first, second = parts
    return jnp.where(flag == 1, second, first), jnp.where(flag == 1, first, second)


def body(
    tokens,
    known_flags,
    w_query,
    b_query,
    w_key,
    w_value,
    b_value,
    w_out,
    b_out,
    gain_one,
    shift_one,
    w_up,
    b_up,
    w_down,
    b_down,
    gain_two,
    shift_two,
    cotangent,
):
    cells, rows, model = tokens.shape
    blocks = lax.axis_size("blk")
    others = lax.axis_size("cells")
    part = rows // 2
    half = 2 * rows
    length = 2 * half
    block = lax.axis_index("blk")
    core = lax.axis_index("cells") % 2
    x, y = block % 2, block // 2
    axes = ("blk", "cells")

    def route(i, j):
        pairs = []
        for b in range(blocks):
            for c in range(others):
                there = 2 * (c % 2) + ((b % 2) ^ i)
                pairs.append((b * others + c, there * others + c - c % 2 + ((b // 2) ^ j)))
        return pairs

    def route_back(i, j):
        return [(there, here) for here, there in route(i, j)]

    both = ((0, 0), (0, 1), (1, 0), (1, 1))

    def near_rows(source, j):
        return lax.dynamic_slice_in_dim(source, (y ^ j) * part, part, 1)

    def cell_of(rows_sent, i):
        return lax.dynamic_slice_in_dim(rows_sent, x ^ i, 1, 0)

    turned = (w_query.T, w_key.T, w_value.T)
    vectors = [b_out, gain_one, shift_one, b_up, b_down, gain_two, shift_two, b_value, b_query]
    vectors = jnp.concatenate([jnp.stack(vectors).astype(f32), jnp.zeros((7, model), f32)], 0)
    first = {}
    for i, j in both:
        first[i, j] = lax.ppermute(cell_of(near_rows(tokens, j), i)[0], axes, route(i, j))
    here = jnp.stack([x, y, core]).astype(jnp.int32)
    place = places(here, known_flags, exchange(known_flags, "cells", 1))
    later_tokens, cotangent, first[0, 0] = lax.optimization_barrier(
        (tokens, cotangent, first[0, 0])
    )
    rest = {}
    for i, j in both:
        cot_rows = near_rows(cotangent, j)
        picked = [near_rows(later_tokens, j)[2:3], cell_of(cot_rows, i)]
        if i == 0:
            picked.append(cot_rows[2:3])
        rest[i, j] = lax.ppermute(jnp.concatenate(picked, 0), axes, route(i, j))
    first, place, turned, vectors = lax.optimization_barrier((first, place, turned, vectors))
    wqT, wkT, wvT = turned
    own = [jnp.concatenate([first[ij] for ij in both], 0)]
    other = [exchange(own[0], "cells", 1)]
    work = (half, rows)

    def attend(k):
        return attention_forward(
            k, place, own[k], other[k], (wqT, wkT, w_key, wvT, vectors), work[k]
        )

    forward = [attend(0)]
    rest, mix = lax.optimization_barrier((rest, forward[0][0]))
    own.append(jnp.concatenate([rest[ij][0] for ij in both], 0))
    other.append(exchange(own[1], "cells", 1))
    cot = [
        jnp.concatenate([rest[ij][1] for ij in both], 0),
        jnp.concatenate([rest[0, j][2] for j in range(2)], 0),
    ]
    forward.append(attend(1))
    mids = middle(
        [mix.reshape(model, half), forward[1][0].reshape(model, rows)],
        own,
        cot,
        (w_out, w_up, w_down),
        vectors,
    )
    mids, early, early_small = (mids[:4], mids[4:8]), mids[8][None], mids[9]
    plan = reduce_plan()
    early, early_small = reduce_step(plan[0], early, early_small)

    out_back = {}
    for i, j in both:
        pieces = [mids[0][0][(2 * i + j) * part : (2 * i + j + 1) * part]]
        if i == 0:
            pieces.append(mids[1][0][j * part : (j + 1) * part])
        out_back[i, j] = lax.ppermute(jnp.stack(pieces), axes, route_back(i, j))

    def rejoin(from_i):
        return jnp.concatenate(swap(from_i, y), 0)

    near, far = (rejoin((out_back[i, 0][0], out_back[i, 1][0])) for i in range(2))
    layer_out = jnp.stack([*swap((near, far), x), rejoin((out_back[0, 0][1], out_back[0, 1][1]))])

    def attend_back(k, grads, before):
        mix, lse, own_score, q, ko, vo, packed, keys = forward[k]
        return attention_backward(
            k,
            place,
            own[k],
            (wqT, wkT, w_value, wvT, vectors),
            (q, ko, vo, packed, keys, lse, own_score),
            grads,
            before,
            work[k],
        )

    def give_back(mine, sent):
        arrived = exchange(sent, "cells", 1)
        kept = (mine + arrived.astype(f32)).astype(bf16)
        return {
            (i, j): lax.ppermute(
                kept[(2 * i + j) * part : (2 * i + j + 1) * part], axes, route_back(i, j)
            )
            for i, j in both
        }

    mine, sent, *sums = attend_back(0, (mids[0][2], mids[0][3], mids[0][1]), None)
    back = [give_back(mine, sent)]
    early, early_small, g_mix, layer_out = lax.optimization_barrier(
        (early, early_small, mids[1][2], layer_out)
    )
    early, early_small = reduce_step(plan[1], early, early_small)
    mine, sent, *late = attend_back(1, (g_mix, mids[1][3], mids[1][1]), sums)
    back.append(give_back(mine, sent))
    late, late_small, early, early_small = lax.optimization_barrier((*late, early, early_small))
    late, late_small = late[None], late_small
    for step in plan[:2]:
        late, late_small = reduce_step(step, late, late_small)
    big = jnp.concatenate([early, late], 0)
    small = (early_small.astype(f32) + late_small.astype(f32)).astype(bf16)
    for step in plan[2:]:
        big, small = reduce_step(step, big, small)
    for step in reversed(plan):
        big = gather_step(step, big)

    near, far, near_last, far_last = (
        rejoin((back[k][i, 0], back[k][i, 1])).astype(f32) for k in range(2) for i in range(2)
    )
    grad_tokens = jnp.stack([*swap((near, far), x), near_last + far_last])
    early, late = big[0].astype(f32), big[1].astype(f32)
    small = small.astype(f32)
    g_out, g_up, g_down = (early[n * model : (n + 1) * model] for n in range(3))
    g_query, g_key, g_value = (late[n * model : (n + 1) * model] for n in range(3))
    g_b_out, g_gain_one, g_shift_one, g_b_up, g_b_down, g_gain_two, g_shift_two = (
        small[n] for n in range(7)
    )
    return (
        layer_out,
        grad_tokens,
        g_query,
        small[8],
        g_key,
        g_value,
        small[9],
        g_out,
        g_b_out,
        g_gain_one,
        g_shift_one,
        g_up,
        g_b_up,
        g_down,
        g_b_down,
        g_gain_two,
        g_shift_two,
    )


def solution(mesh):
    rows = P("cells", "blk", None)
    return jax.shard_map(
        body,
        mesh=mesh,
        in_specs=(rows, P("cells", None)) + (P(),) * 15 + (rows,),
        out_specs=(rows, rows) + (P(),) * 15,
        check_vma=False,
    )
```

```python
import functools
import math

import jax
import jax.numpy as jnp
from jax import lax
from jax.experimental import pallas as pl
from jax.experimental.pallas import tpu as pltpu
from jax.sharding import PartitionSpec as P

HEADS = 8
EPSILON = 1e-05
LOG2E = math.log2(math.e)
NONE = -1e30
NN = (((1,), (0,)), ((), ()))
NT = (((1,), (1,)), ((), ()))
TN = (((0,), (0,)), ((), ()))
f32 = jnp.float32
bf16 = jnp.bfloat16
SMALL_BYTES = 6 * 1024 * 1024
INPUTS_BYTES = 20 * 1024 * 1024
FORWARD_BYTES = 20 * 1024 * 1024
MIDDLE_BYTES = 20 * 1024 * 1024
BACKWARD_BYTES = 40 * 1024 * 1024
UNROLL = 2


def dot(a, b, dims=NN):
    return lax.dot_general(a, b, dims, preferred_element_type=f32)


def sizes_of(length):
    return [length * 13 // 24 // 64 * 64, length]


def by_size(count, sizes, run):
    low = 0
    for at, size in enumerate(sizes):
        fits = count <= size
        if at:
            fits = fits & (count > low)
        pl.when(fits)(functools.partial(run, size))
        low = size


def pad_heads(padded, whole):
    heads, double, _ = padded.shape
    size = double // 2
    blank = jnp.zeros((size, whole.shape[1]), whole.dtype)
    for h in range(heads):
        part = whole[h * size : (h + 1) * size, :]
        padded[h] = jnp.concatenate([part, blank] if h % 2 == 0 else [blank, part], 0)


def over_heads(run, heads, rows, common):
    if common:

        def step(i, carry):
            for t in range(UNROLL):
                run(UNROLL * i + t, 0, rows)
            return carry

        lax.fori_loop(0, heads // UNROLL, step, 0)
    else:
        wide = 128
        chunks = rows // wide

        def step(i, carry):
            run(i // chunks, pl.multiple_of(i % chunks * wide, wide), wide)
            return carry

        lax.fori_loop(0, heads * chunks, step, 0)


def prepare_kernel(here_ref, near_ref, far_ref, tokens_ref, cot_ref, place_ref, *sent):
    x, y, core = here_ref[0], here_ref[1], here_ref[2]
    count = tokens_ref.shape[1] // 2
    sent, cots = sent[:4], sent[4:]
    for at, ref in enumerate(sent):
        rows = pl.ds(pl.multiple_of((y ^ (at % 2)) * count, count), count)
        ref[...] = tokens_ref[2, rows, :]
        cots[at][0] = cot_ref[x ^ (at // 2), rows, :]
        if at < 2:
            cots[at][1] = cot_ref[2, rows, :]
    length = near_ref.shape[1]
    part = length // 8
    flags = jnp.where(core == y, near_ref[...], far_ref[...]).astype(f32)
    flags = jnp.concatenate([jnp.where(x == 1, flags[1:2], flags[0:1]), flags[2:3]], 0)
    pieces = {}
    for at in range(8):
        pieces[at // 4, at // 2 % 2, at % 2] = flags[:, at * part : (at + 1) * part]
    for bit, axis in ((core, 2), (x, 1)):
        turn = lambda k, axis=axis: tuple(1 - v if n == axis else v for n, v in enumerate(k))
        pieces = {k: jnp.where(bit == 1, pieces[turn(k)], v) for k, v in pieces.items()}
    ordered = []
    for side in range(2):
        for i in range(2):
            for j in range(2):
                swapped = core != side
                ordered.append(jnp.where(swapped, pieces[1 - j, i, side], pieces[j, i, side]))
    flags = jnp.concatenate(ordered, 1)
    width = 128
    rows = lax.broadcasted_iota(jnp.int32, (width, width), 0)
    lower = (rows <= lax.broadcasted_iota(jnp.int32, (width, width), 1)).astype(f32).astype(bf16)
    tiles = jnp.concatenate([flags[:, at : at + width] for at in range(0, length, width)], 0)
    inside = dot(tiles.astype(bf16), lower)
    ahead = jnp.full((2, 1), -1.0, f32)
    placed = []
    for at in range(length // width):
        tile = inside[2 * at : 2 * at + 2, :]
        placed.append(tile + ahead)
        ahead = ahead + tile[:, width - 1 :]
    place_ref[...] = jnp.where(flags > 0, jnp.concatenate(placed, 1), -1.0)


def prepare(here, near, far, tokens, cotangent):
    _, rows, model = tokens.shape
    vmem = pl.BlockSpec(memory_space=pltpu.VMEM)
    sent = [jax.ShapeDtypeStruct((rows // 2, model), bf16)] * 4
    sent += [jax.ShapeDtypeStruct((n, rows // 2, model), bf16) for n in (2, 2, 1, 1)]
    return pl.pallas_call(
        prepare_kernel,
        out_shape=[jax.ShapeDtypeStruct((2, near.shape[1]), f32), *sent],
        in_specs=[pl.BlockSpec(memory_space=pltpu.SMEM)] + [vmem] * 4,
        out_specs=[vmem] * 9,
        compiler_params=pltpu.CompilerParams(vmem_limit_bytes=SMALL_BYTES),
        name="prepare",
    )(here, near, far, tokens, cotangent)


def count_of(place):
    return (jnp.max(place) + 1.0).astype(jnp.int32)


def column(row, lanes):
    return jnp.broadcast_to(row, (lanes, row.shape[1])).T[:, 0:1]


def join_kernel(layout, after, *refs):
    outs = refs[len(refs) - len(layout) :]
    for out_ref, pieces in zip(outs, layout):
        count = out_ref.shape[0] // len(pieces)
        for at, (source, place) in enumerate(pieces):
            piece = refs[source][...] if place is None else refs[source][place]
            out_ref[at * count : (at + 1) * count, :] = piece


def join(pieces, layout, after=()):
    count, model = pieces[0].shape[-2:]
    vmem = pl.BlockSpec(memory_space=pltpu.VMEM)
    anywhere = pl.BlockSpec(memory_space=pl.ANY)
    return pl.pallas_call(
        functools.partial(join_kernel, layout, len(after)),
        out_shape=[jax.ShapeDtypeStruct((count * len(p), model), bf16) for p in layout],
        in_specs=[vmem] * len(pieces) + [anywhere] * len(after),
        out_specs=[vmem] * len(layout),
        compiler_params=pltpu.CompilerParams(vmem_limit_bytes=SMALL_BYTES),
        name="join",
    )(*pieces, *after)


def forward_kernel(
    sizes,
    cell,
    place_ref,
    own_ref,
    other_ref,
    wqT_ref,
    wkT_ref,
    wk_ref,
    wvT_ref,
    vec_ref,
    mix_ref,
    lse_ref,
    self_ref,
    q_hbm,
    ko_hbm,
    vo_hbm,
    packed_hbm,
    keys_hbm,
    q_ref,
    ko_ref,
    vo_ref,
    packed_ref,
    keys_ref,
    v_s,
    q_s,
    sems,
):
    heads, size, rows = q_ref.shape
    scale = size ** (-0.5) * LOG2E
    place = place_ref[cell : cell + 1, :]
    count = count_of(place)
    half = own_ref.shape[0]
    length = 2 * half
    b_value = column(vec_ref[7:8, :], 8)
    x_own = own_ref[0:rows, :]
    q = (dot(wqT_ref[...], x_own, NT) + column(vec_ref[8:9, :], 8)).astype(bf16)
    ko = dot(wkT_ref[...], x_own, NT).astype(bf16)
    vo = (dot(wvT_ref[...], x_own, NT) + b_value).astype(bf16)
    q_ref[...] = q.reshape(heads, size, rows)
    ko_ref[...] = ko.reshape(heads, size, rows)
    vo_ref[...] = vo.reshape(heads, size, rows)
    held = ((q_ref, q_hbm), (ko_ref, ko_hbm), (vo_ref, vo_hbm))
    saves = [pltpu.make_async_copy(*pair, sems.at[n]) for n, pair in enumerate(held)]
    for save in saves:
        save.start()
    own_score = (q.astype(f32) * ko.astype(f32)).reshape(heads, size, rows).sum(1, keepdims=True)
    self_ref[...] = jnp.where(place[None, :, 0:rows] < 0, own_score * scale, NONE)
    pad_heads(q_s, q)

    def run(n):
        spot = lax.broadcasted_iota(jnp.int32, (n, half), 0).astype(f32)
        pick_own = (spot == place[:, 0:half]).astype(f32).astype(bf16)
        pick_other = (spot == place[:, half:]).astype(f32).astype(bf16)
        packed = (dot(pick_own, own_ref[...]) + dot(pick_other, other_ref[...])).astype(bf16)
        packed_ref[0:n, :] = packed
        keys = dot(packed, wk_ref[...]).astype(bf16)
        keys_ref[0:n, :] = keys
        first = pl.ds(0, n)
        held = ((packed_ref, packed_hbm), (keys_ref, keys_hbm))
        late = [
            pltpu.make_async_copy(near.at[first], far.at[first], sems.at[3 + at])
            for at, (near, far) in enumerate(held)
        ]
        for save in late:
            save.start()
        v_s[:, :, 0:n] = (
            (dot(wvT_ref[...], packed, NT) + b_value).astype(bf16).reshape(heads, size, n)
        )

        def head(h, at, wide):
            pair = pl.ds(pl.multiple_of(h // 2 * 2 * size, 2 * size), 2 * size)
            raw = dot(keys_ref[0:n, pair], q_s[h, :, pl.ds(at, wide)])
            seen = lax.broadcasted_iota(jnp.int32, raw.shape, 0) < count
            scores = jnp.where(seen, raw * scale, NONE)
            own = self_ref[h, :, pl.ds(at, wide)]
            top = jnp.maximum(jnp.max(scores, axis=0, keepdims=True), own)
            weights = jnp.exp2(scores - top)
            own_weight = jnp.exp2(own - top)
            total = jnp.sum(weights, axis=0, keepdims=True) + own_weight
            mixed = dot(v_s[h, :, 0:n], weights.astype(bf16))
            mixed = mixed + own_weight * vo_ref[h, :, pl.ds(at, wide)].astype(f32)
            mix_ref[h, :, pl.ds(at, wide)] = (mixed / total).astype(bf16)
            lse_ref[h, :, pl.ds(at, wide)] = top + jnp.log(total) * LOG2E

        over_heads(head, heads, rows, n < length)
        for save in late:
            save.wait()

    by_size(count, sizes, run)
    for save in saves:
        save.wait()


def attention_forward(cell, place, own, other, weights, rows):
    half, model = own.shape
    length = 2 * half
    size = model // HEADS
    vmem = pl.BlockSpec(memory_space=pltpu.VMEM)
    by_head = pltpu.VMEM((HEADS, size, rows), bf16)
    by_key = pltpu.VMEM((length, model), bf16)
    head_rows = jax.ShapeDtypeStruct((HEADS, size, rows), bf16)
    row_stat = jax.ShapeDtypeStruct((HEADS, 1, rows), f32)
    return pl.pallas_call(
        functools.partial(forward_kernel, sizes_of(length), cell),
        out_shape=(
            head_rows,
            row_stat,
            row_stat,
            *[pltpu.HBM(head_rows.shape, bf16)] * 3,
            *[pltpu.HBM((length, model), bf16)] * 2,
        ),
        in_specs=[vmem] * (3 + len(weights)),
        out_specs=(vmem,) * 3 + (pl.BlockSpec(memory_space=pltpu.HBM),) * 5,
        scratch_shapes=[
            by_head,
            by_head,
            by_head,
            by_key,
            by_key,
            pltpu.VMEM((HEADS, size, length), bf16),
            pltpu.VMEM((HEADS, 2 * size, rows), bf16),
            pltpu.SemaphoreType.DMA((5,)),
        ],
        compiler_params=pltpu.CompilerParams(vmem_limit_bytes=FORWARD_BYTES),
        cost_estimate=pl.CostEstimate(
            flops=16 * rows * length * model, bytes_accessed=8 << 20, transcendentals=0
        ),
        name="attention_forward",
    )(place, own, other, *[pltpu.with_memory_space_constraint(w, pltpu.HBM) for w in weights])


def split_halves(here_ref, mine_ref, other_ref, whole_ref, small):
    count = whole_ref.shape[0] // 2
    core = here_ref[2]
    for ref, side in ((mine_ref, core), (other_ref, 1 - core)):
        ref[0:count, :] = whole_ref[pl.ds(pl.multiple_of(side * count, count), count), :]
        ref[count:, :] = small.astype(bf16)


def middle_kernel(
    here_ref,
    mix_a_ref,
    x_a_ref,
    mix_b_ref,
    x_b_ref,
    cot_0_ref,
    cot_1_ref,
    cot_2_ref,
    cot_3_ref,
    w_out_ref,
    w_up_ref,
    w_down_ref,
    vec_ref,
    *rest,
):
    outs_a, outs_b, (mine_ref, other_ref, mix_ref, x_ref, cot_ref, w_acc, v_acc, w_low) = (
        rest[:4],
        rest[4:8],
        rest[8:],
    )
    step = pl.program_id(0)
    last = pl.num_programs(0) - 1
    model = x_ref.shape[1]

    @pl.when(step == 0)
    def _():
        w_acc[...] = jnp.zeros_like(w_acc)
        v_acc[...] = jnp.zeros_like(v_acc)

    part = cot_ref.shape[0] // 2
    for at, pair in enumerate(((cot_0_ref, cot_1_ref), (cot_2_ref, cot_3_ref))):

        @pl.when(step == at)
        def _():
            mix_ref[...] = mix_a_ref[...]
            x_ref[...] = x_a_ref[...]
            cot_ref[0:part, :] = pair[0][0]
            cot_ref[part:, :] = pair[1][0]

    @pl.when(step == last)
    def _():
        mix_ref[...] = mix_b_ref[...]
        x_ref[...] = x_b_ref[...]
        cot_ref[0:part, :] = cot_0_ref[1]
        cot_ref[part:, :] = cot_1_ref[1]

    b_out, gain_one, shift_one, b_up, b_down, gain_two, shift_two = (
        vec_ref[i : i + 1, :] for i in range(7)
    )

    def mean(v):
        return jnp.mean(v, axis=-1, keepdims=True)

    def rows(v):
        return jnp.sum(v, axis=0, keepdims=True)

    attn_in = mix_ref[...]
    h1 = x_ref[...].astype(f32) + dot(attn_in, w_out_ref[...], TN) + b_out
    c1 = h1 - mean(h1)
    inv1 = lax.rsqrt(mean(c1 * c1) + EPSILON)
    n1 = c1 * inv1
    x1 = n1 * gain_one + shift_one
    x1_low = x1.astype(bf16)
    up = dot(x1_low, w_up_ref[...]) + b_up
    cdf = 0.5 + 0.5 * lax.erf(up * (0.5**0.5))
    slope = cdf + up * (jnp.exp(-0.5 * up * up) * (1.0 / math.sqrt(2.0 * math.pi)))
    act = (up * cdf).astype(bf16)
    h2 = x1 + dot(act, w_down_ref[...]) + b_down
    c2 = h2 - mean(h2)
    inv2 = lax.rsqrt(mean(c2 * c2) + EPSILON)
    n2 = c2 * inv2
    out = (n2 * gain_two + shift_two).astype(bf16)
    cot = cot_ref[...].astype(f32)
    g_gain_two = rows(cot * n2)
    g_shift_two = rows(cot)
    gn2 = cot * gain_two
    gh2 = inv2 * (gn2 - mean(gn2) - n2 * mean(gn2 * n2))
    g_down = gh2.astype(bf16)
    w_acc[2 * model :, :] += dot(act, g_down, TN)
    g_b_down = rows(g_down.astype(f32))
    g_up = (slope * dot(g_down, w_down_ref[...], NT)).astype(bf16)
    w_acc[model : 2 * model, :] += dot(x1_low, g_up, TN)
    g_b_up = rows(g_up.astype(f32))
    gx1 = gh2 + dot(g_up, w_up_ref[...], NT)
    g_gain_one = rows(gx1 * n1)
    g_shift_one = rows(gx1)
    gn1 = gx1 * gain_one
    gh1 = inv1 * (gn1 - mean(gn1) - n1 * mean(gn1 * n1))
    g_attn = gh1.astype(bf16)
    w_acc[0:model, :] += dot(attn_in, g_attn)
    g_b_out = rows(g_attn.astype(f32))
    g_mix = dot(w_out_ref[...], g_attn, NT).astype(bf16)
    size = model // HEADS
    delta = (g_mix.astype(f32) * attn_in.astype(f32)).reshape(HEADS, size, -1).sum(1, keepdims=True)
    results = (out, gh1, g_mix.reshape(HEADS, size, -1), delta)
    sums = (g_b_out, g_gain_one, g_shift_one, g_b_up, g_b_down, g_gain_two, g_shift_two)
    for at, term in enumerate(sums):
        v_acc[at : at + 1, :] += term

    @pl.when(step < last)
    def _():
        for ref, value in zip(outs_a, results):
            ref[...] = value

    @pl.when(step == last)
    def _():
        for ref, value in zip(outs_b, results):
            ref[...] = value
        w_low[...] = w_acc[...].astype(bf16)
        split_halves(here_ref, mine_ref, other_ref, w_low, v_acc[...])


def middle(here, mix, x, cot, weights, vectors):
    _, part, model = cot[0].shape
    block = 2 * part
    size = model // HEADS
    steps = 2
    whole = lambda shape: pl.BlockSpec(shape, lambda i: (0,) * len(shape))
    places = (lambda i: jnp.minimum(i, steps - 1), lambda i: 0)
    by_row = [pl.BlockSpec((block, model), lambda i, at=at: (at(i), 0)) for at in places]
    by_column = [pl.BlockSpec((model, block), lambda i, at=at: (0, at(i))) for at in places]
    by_head = [pl.BlockSpec((HEADS, size, block), lambda i, at=at: (0, 0, at(i))) for at in places]
    stats = [pl.BlockSpec((HEADS, 1, block), lambda i, at=at: (0, 0, at(i))) for at in places]
    square = whole((model, model))
    half_shape = (3 * model // 2 + 16, model)
    inputs, in_specs, out_shape, out_specs = [], [], [], []
    for k in range(2):
        rows = mix[k].shape[1]
        inputs += [mix[k], x[k]]
        in_specs += [by_column[k], by_row[k]]
        out_shape += [
            jax.ShapeDtypeStruct((rows, model), bf16),
            jax.ShapeDtypeStruct((rows, model), f32),
            jax.ShapeDtypeStruct((HEADS, size, rows), bf16),
            jax.ShapeDtypeStruct((HEADS, 1, rows), f32),
        ]
        out_specs += [by_row[k], by_row[k], by_head[k], stats[k]]
    return pl.pallas_call(
        middle_kernel,
        grid=(steps + 1,),
        out_shape=(
            *out_shape,
            jax.ShapeDtypeStruct(half_shape, bf16),
            jax.ShapeDtypeStruct(half_shape, bf16),
        ),
        in_specs=[
            pl.BlockSpec(memory_space=pltpu.SMEM),
            *in_specs,
            *[whole(piece.shape) for piece in cot],
            square,
            square,
            square,
            whole(vectors.shape),
        ],
        out_specs=(*out_specs, whole(half_shape), whole(half_shape)),
        scratch_shapes=[
            pltpu.VMEM((model, block), bf16),
            pltpu.VMEM((block, model), bf16),
            pltpu.VMEM((block, model), bf16),
            pltpu.VMEM((3 * model, model), f32),
            pltpu.VMEM((16, model), f32),
            pltpu.VMEM((3 * model, model), bf16),
        ],
        compiler_params=pltpu.CompilerParams(
            vmem_limit_bytes=MIDDLE_BYTES, dimension_semantics=("arbitrary",)
        ),
        cost_estimate=pl.CostEstimate(
            flops=36 * (steps + 1) * block * model * model,
            bytes_accessed=8 << 20,
            transcendentals=0,
        ),
        name="middle",
    )(here, *inputs, *cot, *weights, vectors)


def backward_kernel(
    sizes,
    has_before,
    after,
    cell,
    here_ref,
    place_ref,
    own_ref,
    wkT_ref,
    wv_ref,
    vec_ref,
    q_hbm,
    ko_hbm,
    vo_hbm,
    packed_hbm,
    keys_hbm,
    lse_ref,
    self_ref,
    gmix_ref,
    delta_ref,
    *rest,
):
    if has_before:
        before_w_ref, before_v_ref, *rest = rest
    rest = rest[after:]
    gk_hbm, gv_hbm, gq_hbm, gko_hbm, gvo_hbm, first_ref, second_ref, *rest = rest
    q_ref, ko_ref, vo_ref, packed_ref, keys_ref, gk_ref, gv_ref, gq_s, gko_s, gvo_s, *rest = rest
    kT_s, v_s, gk_s, gv_s, w_acc, v_acc, q_s, gm_s, w_low, sems = rest
    heads, size, rows = q_ref.shape
    model = heads * size
    length = packed_ref.shape[0]
    held = ((q_hbm, q_ref), (ko_hbm, ko_ref), (vo_hbm, vo_ref))
    loads = [pltpu.make_async_copy(*pair, sems.at[n]) for n, pair in enumerate(held)]
    for load in loads:
        load.start()
    plain = size ** (-0.5)
    scale = plain * LOG2E
    place = place_ref[cell : cell + 1, :]
    count = count_of(place)
    pad_heads(gm_s, gmix_ref[...].reshape(model, rows))

    def run(n):
        first = pl.ds(0, n)
        held = ((packed_hbm, packed_ref), (keys_hbm, keys_ref))
        late = [
            pltpu.make_async_copy(far.at[first], near.at[first], sems.at[3 + at])
            for at, (far, near) in enumerate(held)
        ]
        for load in late:
            load.start()
        for load in loads:
            load.wait()
        pad_heads(q_s, q_ref[...].reshape(model, rows))
        for load in late:
            load.wait()
        packed = packed_ref[0:n, :]
        kT_s[:, :, 0:n] = dot(wkT_ref[...], packed, NT).astype(bf16).reshape(heads, size, n)
        values = (dot(packed, wv_ref[...]) + vec_ref[7:8, :]).astype(bf16)
        v_s[0:n, :] = values

        def head(h, at, wide):
            here = pl.ds(at, wide)
            pair = pl.ds(pl.multiple_of(h // 2 * 2 * size, 2 * size), 2 * size)
            k_pair = keys_ref[0:n, pair]
            v_pair = v_s[0:n, pair]
            q_full = q_s[h, :, here]
            gm_full = gm_s[h, :, here]
            lse = lse_ref[h, :, here]
            delta = delta_ref[h, :, here]
            raw = dot(k_pair, q_full)
            seen = lax.broadcasted_iota(jnp.int32, raw.shape, 0) < count
            weights = jnp.where(seen, jnp.exp2(raw * scale - lse), 0.0)
            g_weights = dot(v_pair, gm_full)
            g_raw = ((plain * weights) * (g_weights - delta)).astype(bf16)
            gv_s[0:n, pair] += dot(weights.astype(bf16), gm_full, NT)
            gk_s[0:n, pair] += dot(g_raw, q_full, NT)
            gq = dot(kT_s[h, :, 0:n], g_raw)
            own_weight = jnp.exp2(self_ref[h, :, here] - lse)
            ko = ko_ref[h, :, here].astype(f32)
            vo = vo_ref[h, :, here].astype(f32)
            gm = gmix_ref[h, :, here].astype(f32)
            g_own = jnp.sum(gm * vo, axis=0, keepdims=True)
            g_own_raw = (plain * own_weight * (g_own - delta)).astype(bf16).astype(f32)
            gq_s[h, :, here] = (gq + g_own_raw * ko).astype(bf16)
            gko_s[h, :, here] = (g_own_raw * q_ref[h, :, here].astype(f32)).astype(bf16)
            gvo_s[h, :, here] = (own_weight * gm).astype(bf16)

        gk_s[0:n, :] = jnp.zeros((n, model), f32)
        gv_s[0:n, :] = jnp.zeros((n, model), f32)
        over_heads(head, heads, rows, n < length)
        gk = gk_s[0:n, :].astype(bf16)
        gv = gv_s[0:n, :].astype(bf16)
        gk_ref[0:n, :] = gk
        gv_ref[0:n, :] = gv
        held = ((gk_ref, gk_hbm), (gv_ref, gv_hbm))
        saves = [
            pltpu.make_async_copy(near.at[first], far.at[first], sems.at[3 + at])
            for at, (near, far) in enumerate(held)
        ]
        for save in saves:
            save.start()
        w_acc[model : 2 * model, :] = dot(gk, packed, TN)
        w_acc[2 * model :, :] = dot(gv, packed, TN)
        v_acc[1:2, :] = jnp.sum(gv.astype(f32), axis=0, keepdims=True)
        for save in saves:
            save.wait()

    by_size(count, sizes, run)
    held = ((gq_s, gq_hbm), (gko_s, gko_hbm), (gvo_s, gvo_hbm))
    saves = [pltpu.make_async_copy(*pair, sems.at[n]) for n, pair in enumerate(held)]
    for save in saves:
        save.start()
    gq = gq_s[...].reshape(model, rows)
    gko = gko_s[...].reshape(model, rows)
    gvo = gvo_s[...].reshape(model, rows)
    x_own = own_ref[0:rows, :]
    ones = jnp.ones((8, rows), bf16)
    w_q = dot(gq, x_own)
    w_k = w_acc[model : 2 * model, :] + dot(gko, x_own)
    w_v = w_acc[2 * model :, :] + dot(gvo, x_own)
    v_q = dot(ones, gq, NT)[0:1, :]
    v_v = v_acc[1:2, :] + dot(ones, gvo, NT)[0:1, :]
    if has_before:
        w_q = w_q + before_w_ref[0:model, :]
        w_k = w_k + before_w_ref[model : 2 * model, :]
        w_v = w_v + before_w_ref[2 * model :, :]
        v_q = v_q + before_v_ref[0:1, :]
        v_v = v_v + before_v_ref[1:2, :]
    if has_before:
        for at, total in enumerate((w_q, w_k, w_v)):
            w_low[at * model : (at + 1) * model, :] = total.T.astype(bf16)
        blank = jnp.zeros((8, model), f32)
        small = jnp.concatenate([blank, v_q, v_v, blank[2:]], 0)
        split_halves(here_ref, first_ref, second_ref, w_low, small)
    else:
        for at, total in enumerate((w_q, w_k, w_v)):
            first_ref[at * model : (at + 1) * model, :] = total
        second_ref[0:1, :] = v_q
        second_ref[1:2, :] = v_v
    for save in saves:
        save.wait()


def attention_backward(cell, here, place, own, weights, saved, stats, before, after, rows):
    half, model = own.shape
    length = 2 * half
    size = model // HEADS
    vmem = pl.BlockSpec(memory_space=pltpu.VMEM)
    before = before or ()
    inputs = (here, place, own, *weights, *saved, *stats, *before, *after)
    hbm = pl.BlockSpec(memory_space=pltpu.HBM)
    anywhere = pl.BlockSpec(memory_space=pl.ANY)
    per_key = pltpu.VMEM((length, model), bf16)
    key_sum = pltpu.VMEM((length, model), f32)
    per_head = pltpu.VMEM((HEADS, size, rows), bf16)
    padded = pltpu.VMEM((HEADS, 2 * size, rows), bf16)
    by_key = pltpu.HBM((length, model), bf16)
    by_head = pltpu.HBM((HEADS, size, rows), bf16)
    if not before:
        sums = [
            jax.ShapeDtypeStruct((3 * model, model), f32),
            jax.ShapeDtypeStruct((8, model), f32),
        ]
    else:
        sums = [jax.ShapeDtypeStruct((3 * model // 2 + 16, model), bf16)] * 2
    return pl.pallas_call(
        functools.partial(backward_kernel, sizes_of(length), bool(before), len(after), cell),
        out_shape=(by_key, by_key, by_head, by_head, by_head, *sums),
        in_specs=[
            pl.BlockSpec(memory_space=pltpu.SMEM),
            *[vmem] * (2 + len(weights)),
            *[hbm] * len(saved),
            *[vmem] * (len(stats) + len(before)),
            *[anywhere] * len(after),
        ],
        out_specs=(hbm,) * 5 + (vmem,) * 2,
        scratch_shapes=[
            per_head,
            per_head,
            per_head,
            per_key,
            per_key,
            per_key,
            per_key,
            per_head,
            per_head,
            per_head,
            pltpu.VMEM((HEADS, size, length), bf16),
            per_key,
            key_sum,
            key_sum,
            pltpu.VMEM((3 * model, model), f32),
            pltpu.VMEM((8, model), f32),
            padded,
            padded,
            pltpu.VMEM((3 * model, model), bf16),
            pltpu.SemaphoreType.DMA((5,)),
        ],
        compiler_params=pltpu.CompilerParams(vmem_limit_bytes=BACKWARD_BYTES),
        cost_estimate=pl.CostEstimate(
            flops=30 * rows * length * model, bytes_accessed=16 << 20, transcendentals=0
        ),
        name="attention_backward",
    )(*inputs)


def inputs_kernel(
    sizes,
    cell,
    after,
    place_ref,
    gk_hbm,
    gv_hbm,
    gq_hbm,
    gko_hbm,
    gvo_hbm,
    wqT_ref,
    wkT_ref,
    wvT_ref,
    gh1_ref,
    *rest,
):
    kept_ref, sent_ref, gk_ref, gv_ref, gq_ref, gko_ref, gvo_ref, full_s, sems = rest[after:]
    held = ((gq_hbm, gq_ref), (gko_hbm, gko_ref), (gvo_hbm, gvo_ref))
    loads = [pltpu.make_async_copy(*pair, sems.at[n]) for n, pair in enumerate(held)]
    heads, size, rows = gq_ref.shape
    length, model = gk_ref.shape
    half = length // 2
    place = place_ref[cell : cell + 1, :]

    def run(n):
        first = pl.ds(0, n)
        late = [
            pltpu.make_async_copy(far.at[first], near.at[first], sems.at[3 + at])
            for at, (far, near) in enumerate(((gk_hbm, gk_ref), (gv_hbm, gv_ref)))
        ]
        for load in late + loads:
            load.start()
        for load in late:
            load.wait()
        g_packed = dot(gk_ref[0:n, :], wkT_ref[...]) + dot(gv_ref[0:n, :], wvT_ref[...])
        spot = lax.broadcasted_iota(jnp.int32, (length, n), 1).astype(f32)
        spread = (spot == column(place, 8)).astype(f32).astype(bf16)
        full_s[...] = dot(spread, g_packed.astype(bf16))

    by_size(count_of(place), sizes, run)
    for load in loads:
        load.wait()
    whole = lambda ref: ref[...].reshape(model, rows)
    mine = dot(whole(gq_ref), wqT_ref[...], TN) + dot(whole(gko_ref), wkT_ref[...], TN)
    mine = mine + dot(whole(gvo_ref), wvT_ref[...], TN)
    kept_ref[0:rows, :] = full_s[0:rows, :] + mine + gh1_ref[...]
    if rows < half:
        kept_ref[rows:, :] = full_s[rows:half, :]
    sent_ref[...] = full_s[half:, :].astype(bf16)


def input_gradients(cell, place, grads, weights, gh1, after):
    length, model = grads[0].shape
    rows = gh1.shape[0]
    vmem = pl.BlockSpec(memory_space=pltpu.VMEM)
    hbm = pl.BlockSpec(memory_space=pltpu.HBM)
    per_key = pltpu.VMEM((length, model), bf16)
    per_head = pltpu.VMEM(grads[2].shape, bf16)
    grads = [pltpu.with_memory_space_constraint(array, pltpu.HBM) for array in grads]
    return pl.pallas_call(
        functools.partial(inputs_kernel, sizes_of(length), cell, len(after)),
        out_shape=(
            jax.ShapeDtypeStruct((length // 2, model), f32),
            jax.ShapeDtypeStruct((length // 2, model), bf16),
        ),
        in_specs=[vmem]
        + [hbm] * 5
        + [vmem] * 4
        + [pl.BlockSpec(memory_space=pl.ANY)] * len(after),
        out_specs=(vmem,) * 2,
        scratch_shapes=[
            per_key,
            per_key,
            per_head,
            per_head,
            per_head,
            pltpu.VMEM((length, model), f32),
            pltpu.SemaphoreType.DMA((5,)),
        ],
        compiler_params=pltpu.CompilerParams(vmem_limit_bytes=INPUTS_BYTES),
        cost_estimate=pl.CostEstimate(
            flops=4 * length * length * model, bytes_accessed=8 << 20, transcendentals=0
        ),
        name="input_gradients",
    )(place, *grads, *weights, gh1, *after)


def exchange(piece, axis, partner):
    count = lax.axis_size(axis)
    return lax.ppermute(piece, axis, [(i, i ^ partner) for i in range(count)])


def radices_of(count):
    radices = []
    while count > 1:
        radix = 4 if count % 4 == 0 else 2
        radices.append(radix)
        count //= radix
    return radices


def reduce_plan():
    plan = [("cells", 2, 1)]
    for axis, stride in (("blk", 1), ("cells", 2)):
        for radix in radices_of(lax.axis_size(axis) // stride):
            plan.append((axis, radix, stride))
            stride *= radix
    return plan


def send_step(step, big, small):
    axis, radix, stride = step
    digit = (lax.axis_index(axis) // stride) % radix
    parts, rows, model = big.shape
    count = rows // radix
    arrived = []
    for other in range(1, radix):
        piece = lax.dynamic_slice_in_dim(big, (digit ^ other) * count, count, 1)
        sent = jnp.concatenate([piece.reshape(parts * count, model), small], 0)
        arrived.append(exchange(sent, axis, other * stride))
    return arrived


def sum_step(step, big, small, arrived):
    axis, radix, stride = step
    digit = (lax.axis_index(axis) // stride) % radix
    parts, rows, model = big.shape
    count = rows // radix
    big = lax.dynamic_slice_in_dim(big, digit * count, count, 1).astype(f32)
    small = small.astype(f32)
    for got in arrived:
        big = big + got[: parts * count].reshape(parts, count, model).astype(f32)
        small = small + got[parts * count :].astype(f32)
    return big.astype(bf16), small.astype(bf16)


def reduce_step(step, big, small):
    return sum_step(step, big, small, send_step(step, big, small))


def core_step(mine, other):
    total = mine.astype(f32) + exchange(other, "cells", 1).astype(f32)
    total = total.astype(bf16)
    count = total.shape[0] - 16
    return total[None, :count], total[count:]


def share_step(step, big):
    axis, radix, stride = step
    return [big] + [exchange(big, axis, other * stride) for other in range(1, radix)]


def gather_step(step, parts):
    axis, radix, stride = step
    digit = (lax.axis_index(axis) // stride) % radix
    ordered = []
    for place in range(radix):
        chosen = parts[place]
        for d in range(1, radix):
            chosen = jnp.where(digit == d, parts[place ^ d], chosen)
        ordered.append(chosen)
    return jnp.concatenate(ordered, 1)


def finish_kernel(here_ref, near_ref, far_ref, *rest):
    outs, (whole_s, sems) = rest[:-2], rest[-2:]
    core = here_ref[2]
    parts, count, model = near_ref.shape
    size = outs[0].shape[0]
    saves = []
    for part in range(parts):
        for ref, side in ((near_ref, core), (far_ref, 1 - core)):
            rows = pl.ds(pl.multiple_of(side * count, count), count)
            whole_s[part, rows, :] = ref[part].astype(f32)
        for at in range(2 * count // size):
            out = part * (2 * count // size) + at
            save = pltpu.make_async_copy(
                whole_s.at[part, pl.ds(at * size, size)], outs[out], sems.at[out]
            )
            save.start()
            saves.append(save)
    for save in saves:
        save.wait()


def finish(here, near, far):
    parts, count, model = near.shape
    number = parts * 2 * count // model
    vmem = pl.BlockSpec(memory_space=pltpu.VMEM)
    return pl.pallas_call(
        finish_kernel,
        out_shape=[pltpu.HBM((model, model), f32)] * number,
        in_specs=[pl.BlockSpec(memory_space=pltpu.SMEM), vmem, vmem],
        out_specs=[pl.BlockSpec(memory_space=pltpu.HBM)] * number,
        scratch_shapes=[
            pltpu.VMEM((parts, 2 * count, model), f32),
            pltpu.SemaphoreType.DMA((number,)),
        ],
        compiler_params=pltpu.CompilerParams(vmem_limit_bytes=INPUTS_BYTES),
        name="finish",
    )(here, near, far)


def swap(parts, flag):
    first, second = parts
    return jnp.where(flag == 1, second, first), jnp.where(flag == 1, first, second)


def body(
    tokens,
    known_flags,
    w_query,
    b_query,
    w_key,
    w_value,
    b_value,
    w_out,
    b_out,
    gain_one,
    shift_one,
    w_up,
    b_up,
    w_down,
    b_down,
    gain_two,
    shift_two,
    cotangent,
):
    cells, rows, model = tokens.shape
    blocks = lax.axis_size("blk")
    others = lax.axis_size("cells")
    part = rows // 2
    half = 2 * rows
    length = 2 * half
    block = lax.axis_index("blk")
    core = lax.axis_index("cells") % 2
    x, y = block % 2, block // 2
    axes = ("blk", "cells")

    def route(i, j):
        pairs = []
        for b in range(blocks):
            for c in range(others):
                there = 2 * (c % 2) + ((b % 2) ^ i)
                pairs.append((b * others + c, there * others + c - c % 2 + ((b // 2) ^ j)))
        return pairs

    def route_back(i, j):
        return [(there, here) for here, there in route(i, j)]

    both = ((0, 0), (0, 1), (1, 0), (1, 1))

    def near_rows(source, j):
        return lax.dynamic_slice_in_dim(source, (y ^ j) * part, part, 1)

    def cell_of(rows_sent, i):
        return lax.dynamic_slice_in_dim(rows_sent, x ^ i, 1, 0)

    turned = (w_query.T, w_key.T, w_value.T)
    vectors = [b_out, gain_one, shift_one, b_up, b_down, gain_two, shift_two, b_value, b_query]
    vectors = jnp.concatenate([jnp.stack(vectors).astype(f32), jnp.zeros((7, model), f32)], 0)
    first = {}
    for i, j in both:
        first[i, j] = lax.ppermute(cell_of(near_rows(tokens, j), i)[0], axes, route(i, j))
    here = jnp.stack([x, y, core]).astype(jnp.int32)
    place, *payloads = prepare(
        here, known_flags, exchange(known_flags, "cells", 1), tokens, cotangent
    )
    rest = {
        ij: lax.ppermute(sent, axes, route(*ij)) for ij, sent in zip(both, payloads[:4])
    }
    cot = [lax.ppermute(sent, axes, route(*ij)) for ij, sent in zip(both, payloads[4:])]
    wqT, wkT, wvT = turned
    pieces = [first[ij] for ij in both]
    own = list(join(pieces, [[(n, None) for n in range(4)]], (place, *turned, vectors)))
    other = [exchange(own[0], "cells", 1)]
    work = (half, rows)

    def attend(k):
        return attention_forward(
            k, place, own[k], other[k], (wqT, wkT, w_key, wvT, vectors), work[k]
        )

    forward = [attend(0)]
    mix = forward[0][0]
    own += join([rest[ij] for ij in both], [[(n, None) for n in range(4)]], (mix,))
    other.append(exchange(own[1], "cells", 1))
    forward.append(attend(1))
    mids = middle(
        here,
        [mix.reshape(model, half), forward[1][0].reshape(model, rows)],
        own,
        cot,
        (w_out, w_up, w_down),
        vectors,
    )
    mids, halves = (mids[:4], mids[4:8]), mids[8:]
    plan = reduce_plan()
    early, early_small = core_step(*halves)

    out_back = {}
    for i, j in both:
        pieces = [mids[0][0][(2 * i + j) * part : (2 * i + j + 1) * part]]
        if i == 0:
            pieces.append(mids[1][0][j * part : (j + 1) * part])
        out_back[i, j] = lax.ppermute(jnp.stack(pieces), axes, route_back(i, j))

    def rejoin(from_i):
        return jnp.concatenate(swap(from_i, y), 0)

    near, far = (rejoin((out_back[i, 0][0], out_back[i, 1][0])) for i in range(2))
    layer_out = jnp.stack([*swap((near, far), x), rejoin((out_back[0, 0][1], out_back[0, 1][1]))])

    def attend_back(k, before, after):
        mix, lse, own_score, *saved = forward[k]
        out, gh1, g_mix, delta = mids[k]
        return attention_backward(
            k,
            here,
            place,
            own[k],
            (wkT, w_value, vectors),
            saved,
            (lse, own_score, g_mix, delta),
            before,
            after,
            work[k],
        )

    def keep(k, grads, after):
        return input_gradients(k, place, grads, (wqT, wkT, wvT), mids[k][1], after)

    def whole_rows(mine, sent):
        return (mine + exchange(sent, "cells", 1).astype(f32)).astype(bf16)

    def give_back(kept):
        back = []
        for n, (i, j) in enumerate(both):
            sent = jnp.stack([rows[n * part : (n + 1) * part] for rows in kept])
            back.append(lax.ppermute(sent, axes, route_back(i, j)))
        return back

    *grads_a, first_sum, second_sum = attend_back(0, None, ())
    *grads_b, mine, other_half = attend_back(1, (first_sum, second_sum), (early, layer_out))
    early, early_small = reduce_step(plan[1], early, early_small)
    mine, other_half, early, early_small = lax.optimization_barrier(
        (mine, other_half, early, early_small)
    )
    late, late_small = core_step(mine, other_half)
    kept = keep(0, grads_a, (late,))
    late, late_small = reduce_step(plan[1], late, late_small)
    late, late_small, kept = lax.optimization_barrier((late, late_small, kept))
    kept_a = whole_rows(*kept)
    kept = keep(1, grads_b, (late,))
    big = jnp.concatenate([early, late], 0)
    small = (early_small.astype(f32) + late_small.astype(f32)).astype(bf16)
    for at, step in enumerate(plan[2:]):
        arrived = send_step(step, big, small)
        if at == 0:
            arrived, kept = lax.optimization_barrier((arrived, kept))
        big, small = sum_step(step, big, small, arrived)
    back = give_back([kept_a, whole_rows(*kept)])
    for step in reversed(plan[2:]):
        parts = share_step(step, big)
        if step is plan[2]:
            parts, back = lax.optimization_barrier((parts, back))
        big = gather_step(step, parts)
    big = gather_step(plan[1], share_step(plan[1], big))

    near, far, near_last, far_last = (
        rejoin((back[2 * i][k], back[2 * i + 1][k])).astype(f32) for k in range(2) for i in range(2)
    )
    grad_tokens = jnp.stack([*swap((near, far), x), near_last + far_last])
    big, small, grad_tokens = lax.optimization_barrier((big, small, grad_tokens))
    g_out, g_up, g_down, g_query, g_key, g_value = finish(here, big, exchange(big, "cells", 1))
    small = small.astype(f32)
    g_b_out, g_gain_one, g_shift_one, g_b_up, g_b_down, g_gain_two, g_shift_two = (
        small[n] for n in range(7)
    )
    return (
        layer_out,
        grad_tokens,
        g_query,
        small[8],
        g_key,
        g_value,
        small[9],
        g_out,
        g_b_out,
        g_gain_one,
        g_shift_one,
        g_up,
        g_b_up,
        g_down,
        g_b_down,
        g_gain_two,
        g_shift_two,
    )


def solution(mesh):
    rows = P("cells", "blk", None)
    return jax.shard_map(
        body,
        mesh=mesh,
        in_specs=(rows, P("cells", None)) + (P(),) * 15 + (rows,),
        out_specs=(rows, rows) + (P(),) * 15,
        check_vma=False,
    )
```

```python
import functools
import math

import jax
import jax.numpy as jnp
from jax import lax
from jax.experimental import pallas as pl
from jax.experimental.pallas import tpu as pltpu
from jax.sharding import PartitionSpec as P

HEADS = 8
EPSILON = 1e-05
LOG2E = math.log2(math.e)
NONE = -1e30
NN = (((1,), (0,)), ((), ()))
NT = (((1,), (1,)), ((), ()))
TN = (((0,), (0,)), ((), ()))
f32 = jnp.float32
bf16 = jnp.bfloat16
SMALL_BYTES = 6 * 1024 * 1024
INPUTS_BYTES = 20 * 1024 * 1024
FORWARD_BYTES = 20 * 1024 * 1024
MIDDLE_BYTES = 20 * 1024 * 1024
BACKWARD_BYTES = 40 * 1024 * 1024
UNROLL = 4


def dot(a, b, dims=NN):
    return lax.dot_general(a, b, dims, preferred_element_type=f32)


def sizes_of(length):
    return [length * 13 // 24 // 64 * 64, length]


def by_size(count, sizes, run):
    low = 0
    for at, size in enumerate(sizes):
        fits = count <= size
        if at:
            fits = fits & (count > low)
        pl.when(fits)(functools.partial(run, size))
        low = size


def pad_heads(padded, whole):
    heads, double, _ = padded.shape
    size = double // 2
    blank = jnp.zeros((size, whole.shape[1]), whole.dtype)
    for h in range(heads):
        part = whole[h * size : (h + 1) * size, :]
        padded[h] = jnp.concatenate([part, blank] if h % 2 == 0 else [blank, part], 0)


def over_heads(run, heads, rows, common):
    if common:

        def step(i, carry):
            for t in range(UNROLL):
                run(UNROLL * i + t, 0, rows)
            return carry

        lax.fori_loop(0, heads // UNROLL, step, 0)
    else:
        wide = 128
        chunks = rows // wide

        def step(i, carry):
            run(i // chunks, pl.multiple_of(i % chunks * wide, wide), wide)
            return carry

        lax.fori_loop(0, heads * chunks, step, 0)


def prepare_kernel(here_ref, near_ref, far_ref, tokens_ref, cot_ref, place_ref, *sent):
    x, y, core = here_ref[0], here_ref[1], here_ref[2]
    count = tokens_ref.shape[1] // 2
    sent, cots = sent[:4], sent[4:]
    for at, ref in enumerate(sent):
        rows = pl.ds(pl.multiple_of((y ^ (at % 2)) * count, count), count)
        ref[...] = tokens_ref[2, rows, :]
        cots[at][0] = cot_ref[x ^ (at // 2), rows, :]
        if at < 2:
            cots[at][1] = cot_ref[2, rows, :]
    length = near_ref.shape[1]
    part = length // 8
    flags = jnp.where(core == y, near_ref[...], far_ref[...]).astype(f32)
    flags = jnp.concatenate([jnp.where(x == 1, flags[1:2], flags[0:1]), flags[2:3]], 0)
    pieces = {}
    for at in range(8):
        pieces[at // 4, at // 2 % 2, at % 2] = flags[:, at * part : (at + 1) * part]
    for bit, axis in ((core, 2), (x, 1)):
        turn = lambda k, axis=axis: tuple(1 - v if n == axis else v for n, v in enumerate(k))
        pieces = {k: jnp.where(bit == 1, pieces[turn(k)], v) for k, v in pieces.items()}
    ordered = []
    for side in range(2):
        for i in range(2):
            for j in range(2):
                swapped = core != side
                ordered.append(jnp.where(swapped, pieces[1 - j, i, side], pieces[j, i, side]))
    flags = jnp.concatenate(ordered, 1)
    width = 128
    rows = lax.broadcasted_iota(jnp.int32, (width, width), 0)
    lower = (rows <= lax.broadcasted_iota(jnp.int32, (width, width), 1)).astype(f32).astype(bf16)
    tiles = jnp.concatenate([flags[:, at : at + width] for at in range(0, length, width)], 0)
    inside = dot(tiles.astype(bf16), lower)
    ahead = jnp.full((2, 1), -1.0, f32)
    placed = []
    for at in range(length // width):
        tile = inside[2 * at : 2 * at + 2, :]
        placed.append(tile + ahead)
        ahead = ahead + tile[:, width - 1 :]
    place_ref[...] = jnp.where(flags > 0, jnp.concatenate(placed, 1), -1.0)


def prepare(here, near, far, tokens, cotangent):
    _, rows, model = tokens.shape
    vmem = pl.BlockSpec(memory_space=pltpu.VMEM)
    sent = [jax.ShapeDtypeStruct((rows // 2, model), bf16)] * 4
    sent += [jax.ShapeDtypeStruct((n, rows // 2, model), bf16) for n in (2, 2, 1, 1)]
    return pl.pallas_call(
        prepare_kernel,
        out_shape=[jax.ShapeDtypeStruct((2, near.shape[1]), f32), *sent],
        in_specs=[pl.BlockSpec(memory_space=pltpu.SMEM)] + [vmem] * 4,
        out_specs=[vmem] * 9,
        compiler_params=pltpu.CompilerParams(vmem_limit_bytes=SMALL_BYTES),
        name="prepare",
    )(here, near, far, tokens, cotangent)


def count_of(place):
    return (jnp.max(place) + 1.0).astype(jnp.int32)


def column(row, lanes):
    return jnp.broadcast_to(row, (lanes, row.shape[1])).T[:, 0:1]


def join_kernel(layout, after, *refs):
    outs = refs[len(refs) - len(layout) :]
    for out_ref, pieces in zip(outs, layout):
        count = out_ref.shape[0] // len(pieces)
        for at, (source, place) in enumerate(pieces):
            piece = refs[source][...] if place is None else refs[source][place]
            out_ref[at * count : (at + 1) * count, :] = piece


def join(pieces, layout, after=()):
    count, model = pieces[0].shape[-2:]
    vmem = pl.BlockSpec(memory_space=pltpu.VMEM)
    anywhere = pl.BlockSpec(memory_space=pl.ANY)
    return pl.pallas_call(
        functools.partial(join_kernel, layout, len(after)),
        out_shape=[jax.ShapeDtypeStruct((count * len(p), model), bf16) for p in layout],
        in_specs=[vmem] * len(pieces) + [anywhere] * len(after),
        out_specs=[vmem] * len(layout),
        compiler_params=pltpu.CompilerParams(vmem_limit_bytes=SMALL_BYTES),
        name="join",
    )(*pieces, *after)


def forward_kernel(
    sizes,
    cell,
    place_ref,
    own_ref,
    other_ref,
    wqT_ref,
    wkT_ref,
    wk_ref,
    wvT_ref,
    vec_ref,
    mix_ref,
    lse_ref,
    self_ref,
    q_hbm,
    ko_hbm,
    vo_hbm,
    packed_hbm,
    keys_hbm,
    q_ref,
    ko_ref,
    vo_ref,
    packed_ref,
    keys_ref,
    v_s,
    q_s,
    sems,
):
    heads, size, rows = q_ref.shape
    scale = size ** (-0.5) * LOG2E
    place = place_ref[cell : cell + 1, :]
    count = count_of(place)
    half = own_ref.shape[0]
    length = 2 * half
    b_value = column(vec_ref[7:8, :], 8)
    x_own = own_ref[0:rows, :]
    q = (dot(wqT_ref[...], x_own, NT) + column(vec_ref[8:9, :], 8)).astype(bf16)
    ko = dot(wkT_ref[...], x_own, NT).astype(bf16)
    vo = (dot(wvT_ref[...], x_own, NT) + b_value).astype(bf16)
    q_ref[...] = q.reshape(heads, size, rows)
    ko_ref[...] = ko.reshape(heads, size, rows)
    vo_ref[...] = vo.reshape(heads, size, rows)
    held = ((q_ref, q_hbm), (ko_ref, ko_hbm), (vo_ref, vo_hbm))
    saves = [pltpu.make_async_copy(*pair, sems.at[n]) for n, pair in enumerate(held)]
    for save in saves:
        save.start()
    own_score = (q.astype(f32) * ko.astype(f32)).reshape(heads, size, rows).sum(1, keepdims=True)
    self_ref[...] = jnp.where(place[None, :, 0:rows] < 0, own_score * scale, NONE)
    pad_heads(q_s, q)

    def run(n):
        spot = lax.broadcasted_iota(jnp.int32, (n, half), 0).astype(f32)
        pick_own = (spot == place[:, 0:half]).astype(f32).astype(bf16)
        pick_other = (spot == place[:, half:]).astype(f32).astype(bf16)
        packed = (dot(pick_own, own_ref[...]) + dot(pick_other, other_ref[...])).astype(bf16)
        packed_ref[0:n, :] = packed
        keys = dot(packed, wk_ref[...]).astype(bf16)
        keys_ref[0:n, :] = keys
        first = pl.ds(0, n)
        held = ((packed_ref, packed_hbm), (keys_ref, keys_hbm))
        late = [
            pltpu.make_async_copy(near.at[first], far.at[first], sems.at[3 + at])
            for at, (near, far) in enumerate(held)
        ]
        for save in late:
            save.start()
        v_s[:, :, 0:n] = (
            (dot(wvT_ref[...], packed, NT) + b_value).astype(bf16).reshape(heads, size, n)
        )

        def head(h, at, wide):
            pair = pl.ds(pl.multiple_of(h // 2 * 2 * size, 2 * size), 2 * size)
            raw = dot(keys_ref[0:n, pair], q_s[h, :, pl.ds(at, wide)])
            seen = lax.broadcasted_iota(jnp.int32, raw.shape, 0) < count
            scores = jnp.where(seen, raw * scale, NONE)
            own = self_ref[h, :, pl.ds(at, wide)]
            top = jnp.maximum(jnp.max(scores, axis=0, keepdims=True), own)
            weights = jnp.exp2(scores - top)
            own_weight = jnp.exp2(own - top)
            total = jnp.sum(weights, axis=0, keepdims=True) + own_weight
            mixed = dot(v_s[h, :, 0:n], weights.astype(bf16))
            mixed = mixed + own_weight * vo_ref[h, :, pl.ds(at, wide)].astype(f32)
            mix_ref[h, :, pl.ds(at, wide)] = (mixed / total).astype(bf16)
            lse_ref[h, :, pl.ds(at, wide)] = top + jnp.log(total) * LOG2E

        over_heads(head, heads, rows, n < length)
        for save in late:
            save.wait()

    by_size(count, sizes, run)
    for save in saves:
        save.wait()


def attention_forward(cell, place, own, other, weights, rows):
    held = [pltpu.with_memory_space_constraint(w, pltpu.HBM) for w in weights]
    weights = held if cell else (*weights[:-1], held[-1])
    half, model = own.shape
    length = 2 * half
    size = model // HEADS
    vmem = pl.BlockSpec(memory_space=pltpu.VMEM)
    by_head = pltpu.VMEM((HEADS, size, rows), bf16)
    by_key = pltpu.VMEM((length, model), bf16)
    head_rows = jax.ShapeDtypeStruct((HEADS, size, rows), bf16)
    row_stat = jax.ShapeDtypeStruct((HEADS, 1, rows), f32)
    return pl.pallas_call(
        functools.partial(forward_kernel, sizes_of(length), cell),
        out_shape=(
            head_rows,
            row_stat,
            row_stat,
            *[pltpu.HBM(head_rows.shape, bf16)] * 3,
            *[pltpu.HBM((length, model), bf16)] * 2,
        ),
        in_specs=[vmem] * (3 + len(weights)),
        out_specs=(vmem,) * 3 + (pl.BlockSpec(memory_space=pltpu.HBM),) * 5,
        scratch_shapes=[
            by_head,
            by_head,
            by_head,
            by_key,
            by_key,
            pltpu.VMEM((HEADS, size, length), bf16),
            pltpu.VMEM((HEADS, 2 * size, rows), bf16),
            pltpu.SemaphoreType.DMA((5,)),
        ],
        compiler_params=pltpu.CompilerParams(vmem_limit_bytes=FORWARD_BYTES),
        cost_estimate=pl.CostEstimate(
            flops=16 * rows * length * model, bytes_accessed=8 << 20, transcendentals=0
        ),
        name="attention_forward",
    )(place, own, other, *weights)


def split_halves(here_ref, mine_ref, other_ref, whole_ref, small):
    count = whole_ref.shape[0] // 2
    core = here_ref[2]
    for ref, side in ((mine_ref, core), (other_ref, 1 - core)):
        ref[0:count, :] = whole_ref[pl.ds(pl.multiple_of(side * count, count), count), :]
        ref[count:, :] = small.astype(bf16)


def middle_kernel(
    here_ref,
    mix_a_ref,
    x_a_ref,
    mix_b_ref,
    x_b_ref,
    cot_0_ref,
    cot_1_ref,
    cot_2_ref,
    cot_3_ref,
    w_out_ref,
    w_up_ref,
    w_down_ref,
    vec_ref,
    *rest,
):
    outs_a, outs_b, (mine_ref, other_ref, mix_ref, x_ref, cot_ref, w_acc, v_acc, w_low) = (
        rest[:4],
        rest[4:8],
        rest[8:],
    )
    step = pl.program_id(0)
    last = pl.num_programs(0) - 1
    model = x_ref.shape[1]

    @pl.when(step == 0)
    def _():
        w_acc[...] = jnp.zeros_like(w_acc)
        v_acc[...] = jnp.zeros_like(v_acc)

    part = cot_ref.shape[0] // 2
    for at, pair in enumerate(((cot_0_ref, cot_1_ref), (cot_2_ref, cot_3_ref))):

        @pl.when(step == at)
        def _():
            mix_ref[...] = mix_a_ref[...]
            x_ref[...] = x_a_ref[...]
            cot_ref[0:part, :] = pair[0][0]
            cot_ref[part:, :] = pair[1][0]

    @pl.when(step == last)
    def _():
        mix_ref[...] = mix_b_ref[...]
        x_ref[...] = x_b_ref[...]
        cot_ref[0:part, :] = cot_0_ref[1]
        cot_ref[part:, :] = cot_1_ref[1]

    b_out, gain_one, shift_one, b_up, b_down, gain_two, shift_two = (
        vec_ref[i : i + 1, :] for i in range(7)
    )

    def mean(v):
        return jnp.mean(v, axis=-1, keepdims=True)

    def rows(v):
        return jnp.sum(v, axis=0, keepdims=True)

    attn_in = mix_ref[...]
    h1 = x_ref[...].astype(f32) + dot(attn_in, w_out_ref[...], TN) + b_out
    c1 = h1 - mean(h1)
    inv1 = lax.rsqrt(mean(c1 * c1) + EPSILON)
    n1 = c1 * inv1
    x1 = n1 * gain_one + shift_one
    x1_low = x1.astype(bf16)
    up = dot(x1_low, w_up_ref[...]) + b_up
    cdf = 0.5 + 0.5 * lax.erf(up * (0.5**0.5))
    slope = cdf + up * (jnp.exp(-0.5 * up * up) * (1.0 / math.sqrt(2.0 * math.pi)))
    act = (up * cdf).astype(bf16)
    h2 = x1 + dot(act, w_down_ref[...]) + b_down
    c2 = h2 - mean(h2)
    inv2 = lax.rsqrt(mean(c2 * c2) + EPSILON)
    n2 = c2 * inv2
    out = (n2 * gain_two + shift_two).astype(bf16)
    cot = cot_ref[...].astype(f32)
    g_gain_two = rows(cot * n2)
    g_shift_two = rows(cot)
    gn2 = cot * gain_two
    gh2 = inv2 * (gn2 - mean(gn2) - n2 * mean(gn2 * n2))
    g_down = gh2.astype(bf16)
    w_acc[2 * model :, :] += dot(act, g_down, TN)
    g_b_down = rows(g_down.astype(f32))
    g_up = (slope * dot(g_down, w_down_ref[...], NT)).astype(bf16)
    w_acc[model : 2 * model, :] += dot(x1_low, g_up, TN)
    g_b_up = rows(g_up.astype(f32))
    gx1 = gh2 + dot(g_up, w_up_ref[...], NT)
    g_gain_one = rows(gx1 * n1)
    g_shift_one = rows(gx1)
    gn1 = gx1 * gain_one
    gh1 = inv1 * (gn1 - mean(gn1) - n1 * mean(gn1 * n1))
    g_attn = gh1.astype(bf16)
    w_acc[0:model, :] += dot(attn_in, g_attn)
    g_b_out = rows(g_attn.astype(f32))
    g_mix = dot(w_out_ref[...], g_attn, NT).astype(bf16)
    size = model // HEADS
    delta = (g_mix.astype(f32) * attn_in.astype(f32)).reshape(HEADS, size, -1).sum(1, keepdims=True)
    results = (out, gh1, g_mix.reshape(HEADS, size, -1), delta)
    sums = (g_b_out, g_gain_one, g_shift_one, g_b_up, g_b_down, g_gain_two, g_shift_two)
    for at, term in enumerate(sums):
        v_acc[at : at + 1, :] += term

    @pl.when(step < last)
    def _():
        for ref, value in zip(outs_a, results):
            ref[...] = value

    @pl.when(step == last)
    def _():
        for ref, value in zip(outs_b, results):
            ref[...] = value
        w_low[...] = w_acc[...].astype(bf16)
        split_halves(here_ref, mine_ref, other_ref, w_low, v_acc[...])


def middle(here, mix, x, cot, weights, vectors):
    _, part, model = cot[0].shape
    block = 2 * part
    size = model // HEADS
    steps = 2
    whole = lambda shape: pl.BlockSpec(shape, lambda i: (0,) * len(shape))
    places = (lambda i: jnp.minimum(i, steps - 1), lambda i: 0)
    by_row = [pl.BlockSpec((block, model), lambda i, at=at: (at(i), 0)) for at in places]
    by_column = [pl.BlockSpec((model, block), lambda i, at=at: (0, at(i))) for at in places]
    by_head = [pl.BlockSpec((HEADS, size, block), lambda i, at=at: (0, 0, at(i))) for at in places]
    stats = [pl.BlockSpec((HEADS, 1, block), lambda i, at=at: (0, 0, at(i))) for at in places]
    square = whole((model, model))
    half_shape = (3 * model // 2 + 16, model)
    inputs, in_specs, out_shape, out_specs = [], [], [], []
    for k in range(2):
        rows = mix[k].shape[1]
        inputs += [mix[k], x[k]]
        in_specs += [by_column[k], by_row[k]]
        out_shape += [
            jax.ShapeDtypeStruct((rows, model), bf16),
            jax.ShapeDtypeStruct((rows, model), f32),
            jax.ShapeDtypeStruct((HEADS, size, rows), bf16),
            jax.ShapeDtypeStruct((HEADS, 1, rows), f32),
        ]
        out_specs += [by_row[k], by_row[k], by_head[k], stats[k]]
    return pl.pallas_call(
        middle_kernel,
        grid=(steps + 1,),
        out_shape=(
            *out_shape,
            jax.ShapeDtypeStruct(half_shape, bf16),
            jax.ShapeDtypeStruct(half_shape, bf16),
        ),
        in_specs=[
            pl.BlockSpec(memory_space=pltpu.SMEM),
            *in_specs,
            *[whole(piece.shape) for piece in cot],
            square,
            square,
            square,
            whole(vectors.shape),
        ],
        out_specs=(*out_specs, whole(half_shape), whole(half_shape)),
        scratch_shapes=[
            pltpu.VMEM((model, block), bf16),
            pltpu.VMEM((block, model), bf16),
            pltpu.VMEM((block, model), bf16),
            pltpu.VMEM((3 * model, model), f32),
            pltpu.VMEM((16, model), f32),
            pltpu.VMEM((3 * model, model), bf16),
        ],
        compiler_params=pltpu.CompilerParams(
            vmem_limit_bytes=MIDDLE_BYTES, dimension_semantics=("arbitrary",)
        ),
        cost_estimate=pl.CostEstimate(
            flops=36 * (steps + 1) * block * model * model,
            bytes_accessed=8 << 20,
            transcendentals=0,
        ),
        name="middle",
    )(here, *inputs, *cot, *weights, vectors)


def backward_kernel(
    sizes,
    has_before,
    after,
    cell,
    here_ref,
    place_ref,
    own_ref,
    wkT_ref,
    wv_ref,
    vec_ref,
    q_hbm,
    ko_hbm,
    vo_hbm,
    packed_hbm,
    keys_hbm,
    lse_ref,
    self_ref,
    gmix_ref,
    delta_ref,
    *rest,
):
    if has_before:
        before_w_ref, before_v_ref, *rest = rest
    rest = rest[after:]
    gk_hbm, gv_hbm, gq_hbm, gko_hbm, gvo_hbm, first_ref, second_ref, *rest = rest
    q_ref, ko_ref, vo_ref, packed_ref, keys_ref, gk_ref, gv_ref, gq_s, gko_s, gvo_s, *rest = rest
    kT_s, v_s, gk_s, gv_s, w_acc, v_acc, q_s, gm_s, w_low, sems = rest
    heads, size, rows = q_ref.shape
    model = heads * size
    length = packed_ref.shape[0]
    held = ((q_hbm, q_ref), (ko_hbm, ko_ref), (vo_hbm, vo_ref))
    loads = [pltpu.make_async_copy(*pair, sems.at[n]) for n, pair in enumerate(held)]
    for load in loads:
        load.start()
    plain = size ** (-0.5)
    scale = plain * LOG2E
    place = place_ref[cell : cell + 1, :]
    count = count_of(place)
    pad_heads(gm_s, gmix_ref[...].reshape(model, rows))

    def run(n):
        first = pl.ds(0, n)
        held = ((packed_hbm, packed_ref), (keys_hbm, keys_ref))
        late = [
            pltpu.make_async_copy(far.at[first], near.at[first], sems.at[3 + at])
            for at, (far, near) in enumerate(held)
        ]
        for load in late:
            load.start()
        for load in loads:
            load.wait()
        pad_heads(q_s, q_ref[...].reshape(model, rows))
        for load in late:
            load.wait()
        packed = packed_ref[0:n, :]
        kT_s[:, :, 0:n] = dot(wkT_ref[...], packed, NT).astype(bf16).reshape(heads, size, n)
        values = (dot(packed, wv_ref[...]) + vec_ref[7:8, :]).astype(bf16)
        v_s[0:n, :] = values

        def head(h, at, wide):
            here = pl.ds(at, wide)
            pair = pl.ds(pl.multiple_of(h // 2 * 2 * size, 2 * size), 2 * size)
            k_pair = keys_ref[0:n, pair]
            v_pair = v_s[0:n, pair]
            q_full = q_s[h, :, here]
            gm_full = gm_s[h, :, here]
            lse = lse_ref[h, :, here]
            delta = delta_ref[h, :, here]
            raw = dot(k_pair, q_full)
            seen = lax.broadcasted_iota(jnp.int32, raw.shape, 0) < count
            weights = jnp.where(seen, jnp.exp2(raw * scale - lse), 0.0)
            g_weights = dot(v_pair, gm_full)
            g_raw = ((plain * weights) * (g_weights - delta)).astype(bf16)
            gv_s[0:n, pair] += dot(weights.astype(bf16), gm_full, NT)
            gk_s[0:n, pair] += dot(g_raw, q_full, NT)
            gq = dot(kT_s[h, :, 0:n], g_raw)
            own_weight = jnp.exp2(self_ref[h, :, here] - lse)
            ko = ko_ref[h, :, here].astype(f32)
            vo = vo_ref[h, :, here].astype(f32)
            gm = gmix_ref[h, :, here].astype(f32)
            g_own = jnp.sum(gm * vo, axis=0, keepdims=True)
            g_own_raw = (plain * own_weight * (g_own - delta)).astype(bf16).astype(f32)
            gq_s[h, :, here] = (gq + g_own_raw * ko).astype(bf16)
            gko_s[h, :, here] = (g_own_raw * q_ref[h, :, here].astype(f32)).astype(bf16)
            gvo_s[h, :, here] = (own_weight * gm).astype(bf16)

        gk_s[0:n, :] = jnp.zeros((n, model), f32)
        gv_s[0:n, :] = jnp.zeros((n, model), f32)
        over_heads(head, heads, rows, n < length)
        gk = gk_s[0:n, :].astype(bf16)
        gv = gv_s[0:n, :].astype(bf16)
        gk_ref[0:n, :] = gk
        gv_ref[0:n, :] = gv
        held = ((gk_ref, gk_hbm), (gv_ref, gv_hbm))
        saves = [
            pltpu.make_async_copy(near.at[first], far.at[first], sems.at[3 + at])
            for at, (near, far) in enumerate(held)
        ]
        for save in saves:
            save.start()
        w_acc[model : 2 * model, :] = dot(gk, packed, TN)
        w_acc[2 * model :, :] = dot(gv, packed, TN)
        v_acc[1:2, :] = jnp.sum(gv.astype(f32), axis=0, keepdims=True)
        for save in saves:
            save.wait()

    by_size(count, sizes, run)
    held = ((gq_s, gq_hbm), (gko_s, gko_hbm), (gvo_s, gvo_hbm))
    saves = [pltpu.make_async_copy(*pair, sems.at[n]) for n, pair in enumerate(held)]
    for save in saves:
        save.start()
    gq = gq_s[...].reshape(model, rows)
    gko = gko_s[...].reshape(model, rows)
    gvo = gvo_s[...].reshape(model, rows)
    x_own = own_ref[0:rows, :]
    ones = jnp.ones((8, rows), bf16)
    w_q = dot(gq, x_own)
    w_k = w_acc[model : 2 * model, :] + dot(gko, x_own)
    w_v = w_acc[2 * model :, :] + dot(gvo, x_own)
    v_q = dot(ones, gq, NT)[0:1, :]
    v_v = v_acc[1:2, :] + dot(ones, gvo, NT)[0:1, :]
    if has_before:
        w_q = w_q + before_w_ref[0:model, :]
        w_k = w_k + before_w_ref[model : 2 * model, :]
        w_v = w_v + before_w_ref[2 * model :, :]
        v_q = v_q + before_v_ref[0:1, :]
        v_v = v_v + before_v_ref[1:2, :]
    if has_before:
        for at, total in enumerate((w_q, w_k, w_v)):
            w_low[at * model : (at + 1) * model, :] = total.T.astype(bf16)
        blank = jnp.zeros((8, model), f32)
        small = jnp.concatenate([blank, v_q, v_v, blank[2:]], 0)
        split_halves(here_ref, first_ref, second_ref, w_low, small)
    else:
        for at, total in enumerate((w_q, w_k, w_v)):
            first_ref[at * model : (at + 1) * model, :] = total
        second_ref[0:1, :] = v_q
        second_ref[1:2, :] = v_v
    for save in saves:
        save.wait()


def attention_backward(cell, here, place, own, weights, saved, stats, before, after, rows):
    half, model = own.shape
    length = 2 * half
    size = model // HEADS
    vmem = pl.BlockSpec(memory_space=pltpu.VMEM)
    before = before or ()
    inputs = (here, place, own, *weights, *saved, *stats, *before, *after)
    hbm = pl.BlockSpec(memory_space=pltpu.HBM)
    anywhere = pl.BlockSpec(memory_space=pl.ANY)
    per_key = pltpu.VMEM((length, model), bf16)
    key_sum = pltpu.VMEM((length, model), f32)
    per_head = pltpu.VMEM((HEADS, size, rows), bf16)
    padded = pltpu.VMEM((HEADS, 2 * size, rows), bf16)
    by_key = pltpu.HBM((length, model), bf16)
    by_head = pltpu.HBM((HEADS, size, rows), bf16)
    if not before:
        sums = [
            jax.ShapeDtypeStruct((3 * model, model), f32),
            jax.ShapeDtypeStruct((8, model), f32),
        ]
    else:
        sums = [jax.ShapeDtypeStruct((3 * model // 2 + 16, model), bf16)] * 2
    return pl.pallas_call(
        functools.partial(backward_kernel, sizes_of(length), bool(before), len(after), cell),
        out_shape=(by_key, by_key, by_head, by_head, by_head, *sums),
        in_specs=[
            pl.BlockSpec(memory_space=pltpu.SMEM),
            *[vmem] * (2 + len(weights)),
            *[hbm] * len(saved),
            *[vmem] * (len(stats) + len(before)),
            *[anywhere] * len(after),
        ],
        out_specs=(hbm,) * 5 + (vmem,) * 2,
        scratch_shapes=[
            per_head,
            per_head,
            per_head,
            per_key,
            per_key,
            per_key,
            per_key,
            per_head,
            per_head,
            per_head,
            pltpu.VMEM((HEADS, size, length), bf16),
            per_key,
            key_sum,
            key_sum,
            pltpu.VMEM((3 * model, model), f32),
            pltpu.VMEM((8, model), f32),
            padded,
            padded,
            pltpu.VMEM((3 * model, model), bf16),
            pltpu.SemaphoreType.DMA((5,)),
        ],
        compiler_params=pltpu.CompilerParams(vmem_limit_bytes=BACKWARD_BYTES),
        cost_estimate=pl.CostEstimate(
            flops=30 * rows * length * model, bytes_accessed=16 << 20, transcendentals=0
        ),
        name="attention_backward",
    )(*inputs)


def inputs_kernel(
    sizes,
    cell,
    after,
    place_ref,
    gk_hbm,
    gv_hbm,
    gq_hbm,
    gko_hbm,
    gvo_hbm,
    wqT_ref,
    wkT_ref,
    wvT_ref,
    gh1_ref,
    *rest,
):
    kept_ref, sent_ref, gk_ref, gv_ref, gq_ref, gko_ref, gvo_ref, full_s, sems = rest[after:]
    held = ((gq_hbm, gq_ref), (gko_hbm, gko_ref), (gvo_hbm, gvo_ref))
    loads = [pltpu.make_async_copy(*pair, sems.at[n]) for n, pair in enumerate(held)]
    heads, size, rows = gq_ref.shape
    length, model = gk_ref.shape
    half = length // 2
    place = place_ref[cell : cell + 1, :]

    def run(n):
        first = pl.ds(0, n)
        late = [
            pltpu.make_async_copy(far.at[first], near.at[first], sems.at[3 + at])
            for at, (far, near) in enumerate(((gk_hbm, gk_ref), (gv_hbm, gv_ref)))
        ]
        for load in late + loads:
            load.start()
        for load in late:
            load.wait()
        g_packed = dot(gk_ref[0:n, :], wkT_ref[...]) + dot(gv_ref[0:n, :], wvT_ref[...])
        spot = lax.broadcasted_iota(jnp.int32, (length, n), 1).astype(f32)
        spread = (spot == column(place, 8)).astype(f32).astype(bf16)
        full_s[...] = dot(spread, g_packed.astype(bf16))

    by_size(count_of(place), sizes, run)
    for load in loads:
        load.wait()
    whole = lambda ref: ref[...].reshape(model, rows)
    mine = dot(whole(gq_ref), wqT_ref[...], TN) + dot(whole(gko_ref), wkT_ref[...], TN)
    mine = mine + dot(whole(gvo_ref), wvT_ref[...], TN)
    kept_ref[0:rows, :] = full_s[0:rows, :] + mine + gh1_ref[...]
    if rows < half:
        kept_ref[rows:, :] = full_s[rows:half, :]
    sent_ref[...] = full_s[half:, :].astype(bf16)


def input_gradients(cell, place, grads, weights, gh1, after):
    length, model = grads[0].shape
    rows = gh1.shape[0]
    vmem = pl.BlockSpec(memory_space=pltpu.VMEM)
    hbm = pl.BlockSpec(memory_space=pltpu.HBM)
    per_key = pltpu.VMEM((length, model), bf16)
    per_head = pltpu.VMEM(grads[2].shape, bf16)
    grads = [pltpu.with_memory_space_constraint(array, pltpu.HBM) for array in grads]
    return pl.pallas_call(
        functools.partial(inputs_kernel, sizes_of(length), cell, len(after)),
        out_shape=(
            jax.ShapeDtypeStruct((length // 2, model), f32),
            jax.ShapeDtypeStruct((length // 2, model), bf16),
        ),
        in_specs=[vmem]
        + [hbm] * 5
        + [vmem] * 4
        + [pl.BlockSpec(memory_space=pl.ANY)] * len(after),
        out_specs=(vmem,) * 2,
        scratch_shapes=[
            per_key,
            per_key,
            per_head,
            per_head,
            per_head,
            pltpu.VMEM((length, model), f32),
            pltpu.SemaphoreType.DMA((5,)),
        ],
        compiler_params=pltpu.CompilerParams(vmem_limit_bytes=INPUTS_BYTES),
        cost_estimate=pl.CostEstimate(
            flops=4 * length * length * model, bytes_accessed=8 << 20, transcendentals=0
        ),
        name="input_gradients",
    )(place, *grads, *weights, gh1, *after)


def exchange(piece, axis, partner):
    count = lax.axis_size(axis)
    return lax.ppermute(piece, axis, [(i, i ^ partner) for i in range(count)])


def radices_of(count):
    radices = []
    while count > 1:
        radix = 4 if count % 4 == 0 else 2
        radices.append(radix)
        count //= radix
    return radices


def reduce_plan():
    plan = [("cells", 2, 1)]
    for axis, stride in (("blk", 1), ("cells", 2)):
        for radix in radices_of(lax.axis_size(axis) // stride):
            plan.append((axis, radix, stride))
            stride *= radix
    return plan


def send_step(step, big, small):
    axis, radix, stride = step
    digit = (lax.axis_index(axis) // stride) % radix
    parts, rows, model = big.shape
    count = rows // radix
    arrived = []
    for other in range(1, radix):
        piece = lax.dynamic_slice_in_dim(big, (digit ^ other) * count, count, 1)
        sent = jnp.concatenate([piece.reshape(parts * count, model), small], 0)
        arrived.append(exchange(sent, axis, other * stride))
    return arrived


def sum_step(step, big, small, arrived):
    axis, radix, stride = step
    digit = (lax.axis_index(axis) // stride) % radix
    parts, rows, model = big.shape
    count = rows // radix
    big = lax.dynamic_slice_in_dim(big, digit * count, count, 1).astype(f32)
    small = small.astype(f32)
    for got in arrived:
        big = big + got[: parts * count].reshape(parts, count, model).astype(f32)
        small = small + got[parts * count :].astype(f32)
    return big.astype(bf16), small.astype(bf16)


def reduce_step(step, big, small):
    return sum_step(step, big, small, send_step(step, big, small))


def core_step(mine, other):
    total = mine.astype(f32) + exchange(other, "cells", 1).astype(f32)
    total = total.astype(bf16)
    count = total.shape[0] - 16
    return total[None, :count], total[count:]


def share_step(step, big):
    axis, radix, stride = step
    return [big] + [exchange(big, axis, other * stride) for other in range(1, radix)]


def gather_step(step, parts):
    axis, radix, stride = step
    digit = (lax.axis_index(axis) // stride) % radix
    ordered = []
    for place in range(radix):
        chosen = parts[place]
        for d in range(1, radix):
            chosen = jnp.where(digit == d, parts[place ^ d], chosen)
        ordered.append(chosen)
    return jnp.concatenate(ordered, 1)


def finish_kernel(here_ref, near_ref, far_ref, *rest):
    outs, (whole_s, sems) = rest[:-2], rest[-2:]
    core = here_ref[2]
    parts, count, model = near_ref.shape
    size = outs[0].shape[0]
    saves = []
    for part in range(parts):
        for ref, side in ((near_ref, core), (far_ref, 1 - core)):
            rows = pl.ds(pl.multiple_of(side * count, count), count)
            whole_s[part, rows, :] = ref[part].astype(f32)
        for at in range(2 * count // size):
            out = part * (2 * count // size) + at
            save = pltpu.make_async_copy(
                whole_s.at[part, pl.ds(at * size, size)], outs[out], sems.at[out]
            )
            save.start()
            saves.append(save)
    for save in saves:
        save.wait()


def finish(here, near, far):
    parts, count, model = near.shape
    number = parts * 2 * count // model
    vmem = pl.BlockSpec(memory_space=pltpu.VMEM)
    return pl.pallas_call(
        finish_kernel,
        out_shape=[pltpu.HBM((model, model), f32)] * number,
        in_specs=[pl.BlockSpec(memory_space=pltpu.SMEM), vmem, vmem],
        out_specs=[pl.BlockSpec(memory_space=pltpu.HBM)] * number,
        scratch_shapes=[
            pltpu.VMEM((parts, 2 * count, model), f32),
            pltpu.SemaphoreType.DMA((number,)),
        ],
        compiler_params=pltpu.CompilerParams(vmem_limit_bytes=INPUTS_BYTES),
        name="finish",
    )(here, near, far)


def swap(parts, flag):
    first, second = parts
    return jnp.where(flag == 1, second, first), jnp.where(flag == 1, first, second)


def body(
    tokens,
    known_flags,
    w_query,
    b_query,
    w_key,
    w_value,
    b_value,
    w_out,
    b_out,
    gain_one,
    shift_one,
    w_up,
    b_up,
    w_down,
    b_down,
    gain_two,
    shift_two,
    cotangent,
):
    cells, rows, model = tokens.shape
    blocks = lax.axis_size("blk")
    others = lax.axis_size("cells")
    part = rows // 2
    half = 2 * rows
    length = 2 * half
    block = lax.axis_index("blk")
    core = lax.axis_index("cells") % 2
    x, y = block % 2, block // 2
    axes = ("blk", "cells")

    def route(i, j):
        pairs = []
        for b in range(blocks):
            for c in range(others):
                there = 2 * (c % 2) + ((b % 2) ^ i)
                pairs.append((b * others + c, there * others + c - c % 2 + ((b // 2) ^ j)))
        return pairs

    def route_back(i, j):
        return [(there, here) for here, there in route(i, j)]

    both = ((0, 0), (0, 1), (1, 0), (1, 1))

    def near_rows(source, j):
        return lax.dynamic_slice_in_dim(source, (y ^ j) * part, part, 1)

    def cell_of(rows_sent, i):
        return lax.dynamic_slice_in_dim(rows_sent, x ^ i, 1, 0)

    turned = (w_query.T, w_key.T, w_value.T)
    vectors = [b_out, gain_one, shift_one, b_up, b_down, gain_two, shift_two, b_value, b_query]
    vectors = jnp.concatenate([jnp.stack(vectors).astype(f32), jnp.zeros((7, model), f32)], 0)
    first = {}
    for i, j in both:
        first[i, j] = lax.ppermute(cell_of(near_rows(tokens, j), i)[0], axes, route(i, j))
    here = jnp.stack([x, y, core]).astype(jnp.int32)
    place, *payloads = prepare(
        here, known_flags, exchange(known_flags, "cells", 1), tokens, cotangent
    )
    rest = {
        ij: lax.ppermute(sent, axes, route(*ij)) for ij, sent in zip(both, payloads[:4])
    }
    cot = [lax.ppermute(sent, axes, route(*ij)) for ij, sent in zip(both, payloads[4:])]
    wqT, wkT, wvT = turned
    pieces = [first[ij] for ij in both]
    own = list(join(pieces, [[(n, None) for n in range(4)]], (place, *turned, vectors)))
    other = [exchange(own[0], "cells", 1)]
    work = (half, rows)

    def attend(k):
        return attention_forward(
            k, place, own[k], other[k], (wqT, wkT, w_key, wvT, vectors), work[k]
        )

    forward = [attend(0)]
    mix = forward[0][0]
    own += join([rest[ij] for ij in both], [[(n, None) for n in range(4)]], (mix,))
    other.append(exchange(own[1], "cells", 1))
    forward.append(attend(1))
    mids = middle(
        here,
        [mix.reshape(model, half), forward[1][0].reshape(model, rows)],
        own,
        cot,
        (w_out, w_up, w_down),
        vectors,
    )
    mids, halves = (mids[:4], mids[4:8]), mids[8:]
    plan = reduce_plan()
    early, early_small = core_step(*halves)

    out_back = {}
    for i, j in both:
        pieces = [mids[0][0][(2 * i + j) * part : (2 * i + j + 1) * part]]
        if i == 0:
            pieces.append(mids[1][0][j * part : (j + 1) * part])
        out_back[i, j] = lax.ppermute(jnp.stack(pieces), axes, route_back(i, j))

    def rejoin(from_i):
        return jnp.concatenate(swap(from_i, y), 0)

    near, far = (rejoin((out_back[i, 0][0], out_back[i, 1][0])) for i in range(2))
    layer_out = jnp.stack([*swap((near, far), x), rejoin((out_back[0, 0][1], out_back[0, 1][1]))])

    def attend_back(k, before, after):
        mix, lse, own_score, *saved = forward[k]
        out, gh1, g_mix, delta = mids[k]
        return attention_backward(
            k,
            here,
            place,
            own[k],
            (wkT, w_value, vectors),
            saved,
            (lse, own_score, g_mix, delta),
            before,
            after,
            work[k],
        )

    def keep(k, grads, after):
        return input_gradients(k, place, grads, (wqT, wkT, wvT), mids[k][1], after)

    def whole_rows(mine, sent):
        return (mine + exchange(sent, "cells", 1).astype(f32)).astype(bf16)

    def give_back(kept):
        back = []
        for n, (i, j) in enumerate(both):
            sent = jnp.stack([rows[n * part : (n + 1) * part] for rows in kept])
            back.append(lax.ppermute(sent, axes, route_back(i, j)))
        return back

    *grads_a, first_sum, second_sum = attend_back(0, None, ())
    *grads_b, mine, other_half = attend_back(1, (first_sum, second_sum), (early, layer_out))
    early, early_small = reduce_step(plan[1], early, early_small)
    mine, other_half, early, early_small = lax.optimization_barrier(
        (mine, other_half, early, early_small)
    )
    late, late_small = core_step(mine, other_half)
    kept = keep(0, grads_a, (late,))
    late, late_small = reduce_step(plan[1], late, late_small)
    late, late_small, kept = lax.optimization_barrier((late, late_small, kept))
    kept_a = whole_rows(*kept)
    kept = keep(1, grads_b, (late,))
    big = jnp.concatenate([early, late], 0)
    small = (early_small.astype(f32) + late_small.astype(f32)).astype(bf16)
    for at, step in enumerate(plan[2:]):
        arrived = send_step(step, big, small)
        if at == 0:
            arrived, kept = lax.optimization_barrier((arrived, kept))
        big, small = sum_step(step, big, small, arrived)
    back = give_back([kept_a, whole_rows(*kept)])
    for step in reversed(plan[2:]):
        parts = share_step(step, big)
        if step is plan[2]:
            parts, back = lax.optimization_barrier((parts, back))
        big = gather_step(step, parts)
    big = gather_step(plan[1], share_step(plan[1], big))

    near, far, near_last, far_last = (
        rejoin((back[2 * i][k], back[2 * i + 1][k])).astype(f32) for k in range(2) for i in range(2)
    )
    grad_tokens = jnp.stack([*swap((near, far), x), near_last + far_last])
    big, small, grad_tokens = lax.optimization_barrier((big, small, grad_tokens))
    g_out, g_up, g_down, g_query, g_key, g_value = finish(here, big, exchange(big, "cells", 1))
    small = small.astype(f32)
    g_b_out, g_gain_one, g_shift_one, g_b_up, g_b_down, g_gain_two, g_shift_two = (
        small[n] for n in range(7)
    )
    return (
        layer_out,
        grad_tokens,
        g_query,
        small[8],
        g_key,
        g_value,
        small[9],
        g_out,
        g_b_out,
        g_gain_one,
        g_shift_one,
        g_up,
        g_b_up,
        g_down,
        g_b_down,
        g_gain_two,
        g_shift_two,
    )


def solution(mesh):
    rows = P("cells", "blk", None)
    return jax.shard_map(
        body,
        mesh=mesh,
        in_specs=(rows, P("cells", None)) + (P(),) * 15 + (rows,),
        out_specs=(rows, rows) + (P(),) * 15,
        check_vma=False,
    )
```

```python
import functools
import math

import jax
import jax.numpy as jnp
from jax import lax
from jax.experimental import pallas as pl
from jax.experimental.pallas import tpu as pltpu
from jax.sharding import PartitionSpec as P

HEADS = 8
EPSILON = 1e-05
LOG2E = math.log2(math.e)
NONE = -1e30
NN = (((1,), (0,)), ((), ()))
NT = (((1,), (1,)), ((), ()))
TN = (((0,), (0,)), ((), ()))
f32 = jnp.float32
bf16 = jnp.bfloat16
SMALL_BYTES = 6 * 1024 * 1024
INPUTS_BYTES = 20 * 1024 * 1024
FORWARD_BYTES = 20 * 1024 * 1024
MIDDLE_BYTES = 20 * 1024 * 1024
BACKWARD_BYTES = 40 * 1024 * 1024
UNROLL = 8


def dot(a, b, dims=NN):
    return lax.dot_general(a, b, dims, preferred_element_type=f32)


def sizes_of(length):
    return [length * 13 // 24 // 64 * 64, length]


def by_size(count, sizes, run):
    low = 0
    for at, size in enumerate(sizes):
        fits = count <= size
        if at:
            fits = fits & (count > low)
        pl.when(fits)(functools.partial(run, size))
        low = size


def pad_heads(padded, whole):
    heads, double, _ = padded.shape
    size = double // 2
    blank = jnp.zeros((size, whole.shape[1]), whole.dtype)
    for h in range(heads):
        part = whole[h * size : (h + 1) * size, :]
        padded[h] = jnp.concatenate([part, blank] if h % 2 == 0 else [blank, part], 0)


def over_heads(run, heads, rows, common):
    if common:

        def step(i, carry):
            for t in range(UNROLL):
                run(UNROLL * i + t, 0, rows)
            return carry

        lax.fori_loop(0, heads // UNROLL, step, 0)
    else:
        wide = 128
        chunks = rows // wide

        def step(i, carry):
            run(i // chunks, pl.multiple_of(i % chunks * wide, wide), wide)
            return carry

        lax.fori_loop(0, heads * chunks, step, 0)


def prepare_kernel(here_ref, near_ref, far_ref, tokens_ref, cot_ref, place_ref, *sent):
    x, y, core = here_ref[0], here_ref[1], here_ref[2]
    count = tokens_ref.shape[1] // 2
    sent, cots = sent[:4], sent[4:]
    for at, ref in enumerate(sent):
        rows = pl.ds(pl.multiple_of((y ^ (at % 2)) * count, count), count)
        ref[...] = tokens_ref[2, rows, :]
        cots[at][0] = cot_ref[x ^ (at // 2), rows, :]
        if at < 2:
            cots[at][1] = cot_ref[2, rows, :]
    length = near_ref.shape[1]
    part = length // 8
    flags = jnp.where(core == y, near_ref[...], far_ref[...]).astype(f32)
    flags = jnp.concatenate([jnp.where(x == 1, flags[1:2], flags[0:1]), flags[2:3]], 0)
    pieces = {}
    for at in range(8):
        pieces[at // 4, at // 2 % 2, at % 2] = flags[:, at * part : (at + 1) * part]
    for bit, axis in ((core, 2), (x, 1)):
        turn = lambda k, axis=axis: tuple(1 - v if n == axis else v for n, v in enumerate(k))
        pieces = {k: jnp.where(bit == 1, pieces[turn(k)], v) for k, v in pieces.items()}
    ordered = []
    for side in range(2):
        for i in range(2):
            for j in range(2):
                swapped = core != side
                ordered.append(jnp.where(swapped, pieces[1 - j, i, side], pieces[j, i, side]))
    flags = jnp.concatenate(ordered, 1)
    width = 128
    rows = lax.broadcasted_iota(jnp.int32, (width, width), 0)
    lower = (rows <= lax.broadcasted_iota(jnp.int32, (width, width), 1)).astype(f32).astype(bf16)
    tiles = jnp.concatenate([flags[:, at : at + width] for at in range(0, length, width)], 0)
    inside = dot(tiles.astype(bf16), lower)
    ahead = jnp.full((2, 1), -1.0, f32)
    placed = []
    for at in range(length // width):
        tile = inside[2 * at : 2 * at + 2, :]
        placed.append(tile + ahead)
        ahead = ahead + tile[:, width - 1 :]
    place_ref[...] = jnp.where(flags > 0, jnp.concatenate(placed, 1), -1.0)


def prepare(here, near, far, tokens, cotangent):
    _, rows, model = tokens.shape
    vmem = pl.BlockSpec(memory_space=pltpu.VMEM)
    sent = [jax.ShapeDtypeStruct((rows // 2, model), bf16)] * 4
    sent += [jax.ShapeDtypeStruct((n, rows // 2, model), bf16) for n in (2, 2, 1, 1)]
    return pl.pallas_call(
        prepare_kernel,
        out_shape=[jax.ShapeDtypeStruct((2, near.shape[1]), f32), *sent],
        in_specs=[pl.BlockSpec(memory_space=pltpu.SMEM)] + [vmem] * 4,
        out_specs=[vmem] * 9,
        compiler_params=pltpu.CompilerParams(vmem_limit_bytes=SMALL_BYTES),
        name="prepare",
    )(here, near, far, tokens, cotangent)


def count_of(place):
    return (jnp.max(place) + 1.0).astype(jnp.int32)


def column(row, lanes):
    return jnp.broadcast_to(row, (lanes, row.shape[1])).T[:, 0:1]


def join_kernel(layout, after, *refs):
    outs = refs[len(refs) - len(layout) :]
    for out_ref, pieces in zip(outs, layout):
        count = out_ref.shape[0] // len(pieces)
        for at, (source, place) in enumerate(pieces):
            piece = refs[source][...] if place is None else refs[source][place]
            out_ref[at * count : (at + 1) * count, :] = piece


def join(pieces, layout, after=()):
    count, model = pieces[0].shape[-2:]
    vmem = pl.BlockSpec(memory_space=pltpu.VMEM)
    anywhere = pl.BlockSpec(memory_space=pl.ANY)
    return pl.pallas_call(
        functools.partial(join_kernel, layout, len(after)),
        out_shape=[jax.ShapeDtypeStruct((count * len(p), model), bf16) for p in layout],
        in_specs=[vmem] * len(pieces) + [anywhere] * len(after),
        out_specs=[vmem] * len(layout),
        compiler_params=pltpu.CompilerParams(vmem_limit_bytes=SMALL_BYTES),
        name="join",
    )(*pieces, *after)


def forward_kernel(
    sizes,
    cell,
    place_ref,
    own_ref,
    other_ref,
    wqT_ref,
    wkT_ref,
    wk_ref,
    wvT_ref,
    vec_ref,
    mix_ref,
    lse_ref,
    self_ref,
    q_hbm,
    ko_hbm,
    vo_hbm,
    packed_hbm,
    keys_hbm,
    q_ref,
    ko_ref,
    vo_ref,
    packed_ref,
    keys_ref,
    v_s,
    q_s,
    sems,
):
    heads, size, rows = q_ref.shape
    scale = size ** (-0.5) * LOG2E
    place = place_ref[cell : cell + 1, :]
    count = count_of(place)
    half = own_ref.shape[0]
    length = 2 * half
    b_value = column(vec_ref[7:8, :], 8)
    x_own = own_ref[0:rows, :]
    q = (dot(wqT_ref[...], x_own, NT) + column(vec_ref[8:9, :], 8)).astype(bf16)
    ko = dot(wkT_ref[...], x_own, NT).astype(bf16)
    vo = (dot(wvT_ref[...], x_own, NT) + b_value).astype(bf16)
    q_ref[...] = q.reshape(heads, size, rows)
    ko_ref[...] = ko.reshape(heads, size, rows)
    vo_ref[...] = vo.reshape(heads, size, rows)
    held = ((q_ref, q_hbm), (ko_ref, ko_hbm), (vo_ref, vo_hbm))
    saves = [pltpu.make_async_copy(*pair, sems.at[n]) for n, pair in enumerate(held)]
    for save in saves:
        save.start()
    own_score = (q.astype(f32) * ko.astype(f32)).reshape(heads, size, rows).sum(1, keepdims=True)
    self_ref[...] = jnp.where(place[None, :, 0:rows] < 0, own_score * scale, NONE)
    pad_heads(q_s, q)

    def run(n):
        spot = lax.broadcasted_iota(jnp.int32, (n, half), 0).astype(f32)
        pick_own = (spot == place[:, 0:half]).astype(f32).astype(bf16)
        pick_other = (spot == place[:, half:]).astype(f32).astype(bf16)
        packed = (dot(pick_own, own_ref[...]) + dot(pick_other, other_ref[...])).astype(bf16)
        packed_ref[0:n, :] = packed
        keys = dot(packed, wk_ref[...]).astype(bf16)
        keys_ref[0:n, :] = keys
        first = pl.ds(0, n)
        held = ((packed_ref, packed_hbm), (keys_ref, keys_hbm))
        late = [
            pltpu.make_async_copy(near.at[first], far.at[first], sems.at[3 + at])
            for at, (near, far) in enumerate(held)
        ]
        for save in late:
            save.start()
        v_s[:, :, 0:n] = (
            (dot(wvT_ref[...], packed, NT) + b_value).astype(bf16).reshape(heads, size, n)
        )

        def head(h, at, wide):
            pair = pl.ds(pl.multiple_of(h // 2 * 2 * size, 2 * size), 2 * size)
            raw = dot(keys_ref[0:n, pair], q_s[h, :, pl.ds(at, wide)])
            seen = lax.broadcasted_iota(jnp.int32, raw.shape, 0) < count
            scores = jnp.where(seen, raw * scale, NONE)
            own = self_ref[h, :, pl.ds(at, wide)]
            top = jnp.maximum(jnp.max(scores, axis=0, keepdims=True), own)
            weights = jnp.exp2(scores - top)
            own_weight = jnp.exp2(own - top)
            total = jnp.sum(weights, axis=0, keepdims=True) + own_weight
            mixed = dot(v_s[h, :, 0:n], weights.astype(bf16))
            mixed = mixed + own_weight * vo_ref[h, :, pl.ds(at, wide)].astype(f32)
            mix_ref[h, :, pl.ds(at, wide)] = (mixed / total).astype(bf16)
            lse_ref[h, :, pl.ds(at, wide)] = top + jnp.log(total) * LOG2E

        over_heads(head, heads, rows, n < length)
        for save in late:
            save.wait()

    by_size(count, sizes, run)
    for save in saves:
        save.wait()


def attention_forward(cell, place, own, other, weights, rows):
    held = [pltpu.with_memory_space_constraint(w, pltpu.HBM) for w in weights]
    weights = held if cell else (*weights[:-1], held[-1])
    half, model = own.shape
    length = 2 * half
    size = model // HEADS
    vmem = pl.BlockSpec(memory_space=pltpu.VMEM)
    by_head = pltpu.VMEM((HEADS, size, rows), bf16)
    by_key = pltpu.VMEM((length, model), bf16)
    head_rows = jax.ShapeDtypeStruct((HEADS, size, rows), bf16)
    row_stat = jax.ShapeDtypeStruct((HEADS, 1, rows), f32)
    return pl.pallas_call(
        functools.partial(forward_kernel, sizes_of(length), cell),
        out_shape=(
            head_rows,
            row_stat,
            row_stat,
            *[pltpu.HBM(head_rows.shape, bf16)] * 3,
            *[pltpu.HBM((length, model), bf16)] * 2,
        ),
        in_specs=[vmem] * (3 + len(weights)),
        out_specs=(vmem,) * 3 + (pl.BlockSpec(memory_space=pltpu.HBM),) * 5,
        scratch_shapes=[
            by_head,
            by_head,
            by_head,
            by_key,
            by_key,
            pltpu.VMEM((HEADS, size, length), bf16),
            pltpu.VMEM((HEADS, 2 * size, rows), bf16),
            pltpu.SemaphoreType.DMA((5,)),
        ],
        compiler_params=pltpu.CompilerParams(vmem_limit_bytes=FORWARD_BYTES),
        cost_estimate=pl.CostEstimate(
            flops=16 * rows * length * model, bytes_accessed=8 << 20, transcendentals=0
        ),
        name="attention_forward",
    )(place, own, other, *weights)


def split_halves(here_ref, mine_ref, other_ref, whole_ref, small):
    count = whole_ref.shape[0] // 2
    core = here_ref[2]
    for ref, side in ((mine_ref, core), (other_ref, 1 - core)):
        ref[0:count, :] = whole_ref[pl.ds(pl.multiple_of(side * count, count), count), :]
        ref[count:, :] = small.astype(bf16)


def middle_kernel(
    here_ref,
    mix_a_ref,
    x_a_ref,
    mix_b_ref,
    x_b_ref,
    cot_0_ref,
    cot_1_ref,
    cot_2_ref,
    cot_3_ref,
    w_out_ref,
    w_up_ref,
    w_down_ref,
    vec_ref,
    *rest,
):
    outs_a, outs_b, (mine_ref, other_ref, mix_ref, x_ref, cot_ref, w_acc, v_acc, w_low) = (
        rest[:4],
        rest[4:8],
        rest[8:],
    )
    step = pl.program_id(0)
    last = pl.num_programs(0) - 1
    model = x_ref.shape[1]

    @pl.when(step == 0)
    def _():
        w_acc[...] = jnp.zeros_like(w_acc)
        v_acc[...] = jnp.zeros_like(v_acc)

    part = cot_ref.shape[0] // 2
    for at, pair in enumerate(((cot_0_ref, cot_1_ref), (cot_2_ref, cot_3_ref))):

        @pl.when(step == at)
        def _():
            mix_ref[...] = mix_a_ref[...]
            x_ref[...] = x_a_ref[...]
            cot_ref[0:part, :] = pair[0][0]
            cot_ref[part:, :] = pair[1][0]

    @pl.when(step == last)
    def _():
        mix_ref[...] = mix_b_ref[...]
        x_ref[...] = x_b_ref[...]
        cot_ref[0:part, :] = cot_0_ref[1]
        cot_ref[part:, :] = cot_1_ref[1]

    b_out, gain_one, shift_one, b_up, b_down, gain_two, shift_two = (
        vec_ref[i : i + 1, :] for i in range(7)
    )

    def mean(v):
        return jnp.mean(v, axis=-1, keepdims=True)

    def rows(v):
        return jnp.sum(v, axis=0, keepdims=True)

    attn_in = mix_ref[...]
    h1 = x_ref[...].astype(f32) + dot(attn_in, w_out_ref[...], TN) + b_out
    c1 = h1 - mean(h1)
    inv1 = lax.rsqrt(mean(c1 * c1) + EPSILON)
    n1 = c1 * inv1
    x1 = n1 * gain_one + shift_one
    x1_low = x1.astype(bf16)
    up = dot(x1_low, w_up_ref[...]) + b_up
    cdf = 0.5 + 0.5 * lax.erf(up * (0.5**0.5))
    slope = cdf + up * (jnp.exp(-0.5 * up * up) * (1.0 / math.sqrt(2.0 * math.pi)))
    act = (up * cdf).astype(bf16)
    h2 = x1 + dot(act, w_down_ref[...]) + b_down
    c2 = h2 - mean(h2)
    inv2 = lax.rsqrt(mean(c2 * c2) + EPSILON)
    n2 = c2 * inv2
    out = (n2 * gain_two + shift_two).astype(bf16)
    cot = cot_ref[...].astype(f32)
    g_gain_two = rows(cot * n2)
    g_shift_two = rows(cot)
    gn2 = cot * gain_two
    gh2 = inv2 * (gn2 - mean(gn2) - n2 * mean(gn2 * n2))
    g_down = gh2.astype(bf16)
    w_acc[2 * model :, :] += dot(act, g_down, TN)
    g_b_down = rows(g_down.astype(f32))
    g_up = (slope * dot(g_down, w_down_ref[...], NT)).astype(bf16)
    w_acc[model : 2 * model, :] += dot(x1_low, g_up, TN)
    g_b_up = rows(g_up.astype(f32))
    gx1 = gh2 + dot(g_up, w_up_ref[...], NT)
    g_gain_one = rows(gx1 * n1)
    g_shift_one = rows(gx1)
    gn1 = gx1 * gain_one
    gh1 = inv1 * (gn1 - mean(gn1) - n1 * mean(gn1 * n1))
    g_attn = gh1.astype(bf16)
    w_acc[0:model, :] += dot(attn_in, g_attn)
    g_b_out = rows(g_attn.astype(f32))
    g_mix = dot(w_out_ref[...], g_attn, NT).astype(bf16)
    size = model // HEADS
    delta = (g_mix.astype(f32) * attn_in.astype(f32)).reshape(HEADS, size, -1).sum(1, keepdims=True)
    results = (out, gh1, g_mix.reshape(HEADS, size, -1), delta)
    sums = (g_b_out, g_gain_one, g_shift_one, g_b_up, g_b_down, g_gain_two, g_shift_two)
    for at, term in enumerate(sums):
        v_acc[at : at + 1, :] += term

    @pl.when(step < last)
    def _():
        for ref, value in zip(outs_a, results):
            ref[...] = value

    @pl.when(step == last)
    def _():
        for ref, value in zip(outs_b, results):
            ref[...] = value
        w_low[...] = w_acc[...].astype(bf16)
        split_halves(here_ref, mine_ref, other_ref, w_low, v_acc[...])


def middle(here, mix, x, cot, weights, vectors):
    _, part, model = cot[0].shape
    block = 2 * part
    size = model // HEADS
    steps = 2
    whole = lambda shape: pl.BlockSpec(shape, lambda i: (0,) * len(shape))
    places = (lambda i: jnp.minimum(i, steps - 1), lambda i: 0)
    by_row = [pl.BlockSpec((block, model), lambda i, at=at: (at(i), 0)) for at in places]
    by_column = [pl.BlockSpec((model, block), lambda i, at=at: (0, at(i))) for at in places]
    by_head = [pl.BlockSpec((HEADS, size, block), lambda i, at=at: (0, 0, at(i))) for at in places]
    stats = [pl.BlockSpec((HEADS, 1, block), lambda i, at=at: (0, 0, at(i))) for at in places]
    square = whole((model, model))
    half_shape = (3 * model // 2 + 16, model)
    inputs, in_specs, out_shape, out_specs = [], [], [], []
    for k in range(2):
        rows = mix[k].shape[1]
        inputs += [mix[k], x[k]]
        in_specs += [by_column[k], by_row[k]]
        out_shape += [
            jax.ShapeDtypeStruct((rows, model), bf16),
            jax.ShapeDtypeStruct((rows, model), f32),
            jax.ShapeDtypeStruct((HEADS, size, rows), bf16),
            jax.ShapeDtypeStruct((HEADS, 1, rows), f32),
        ]
        out_specs += [by_row[k], by_row[k], by_head[k], stats[k]]
    return pl.pallas_call(
        middle_kernel,
        grid=(steps + 1,),
        out_shape=(
            *out_shape,
            jax.ShapeDtypeStruct(half_shape, bf16),
            jax.ShapeDtypeStruct(half_shape, bf16),
        ),
        in_specs=[
            pl.BlockSpec(memory_space=pltpu.SMEM),
            *in_specs,
            *[whole(piece.shape) for piece in cot],
            square,
            square,
            square,
            whole(vectors.shape),
        ],
        out_specs=(*out_specs, whole(half_shape), whole(half_shape)),
        scratch_shapes=[
            pltpu.VMEM((model, block), bf16),
            pltpu.VMEM((block, model), bf16),
            pltpu.VMEM((block, model), bf16),
            pltpu.VMEM((3 * model, model), f32),
            pltpu.VMEM((16, model), f32),
            pltpu.VMEM((3 * model, model), bf16),
        ],
        compiler_params=pltpu.CompilerParams(
            vmem_limit_bytes=MIDDLE_BYTES, dimension_semantics=("arbitrary",)
        ),
        cost_estimate=pl.CostEstimate(
            flops=36 * (steps + 1) * block * model * model,
            bytes_accessed=8 << 20,
            transcendentals=0,
        ),
        name="middle",
    )(here, *inputs, *cot, *weights, vectors)


def backward_kernel(
    sizes,
    has_before,
    after,
    cell,
    here_ref,
    place_ref,
    own_ref,
    wkT_ref,
    wv_ref,
    vec_ref,
    q_hbm,
    ko_hbm,
    vo_hbm,
    packed_hbm,
    keys_hbm,
    lse_ref,
    self_ref,
    gmix_ref,
    delta_ref,
    *rest,
):
    if has_before:
        before_w_ref, before_v_ref, *rest = rest
    rest = rest[after:]
    gk_hbm, gv_hbm, gq_hbm, gko_hbm, gvo_hbm, first_ref, second_ref, *rest = rest
    q_ref, ko_ref, vo_ref, packed_ref, keys_ref, gk_ref, gv_ref, gq_s, gko_s, gvo_s, *rest = rest
    kT_s, v_s, gk_s, gv_s, w_acc, v_acc, q_s, gm_s, w_low, sems = rest
    heads, size, rows = q_ref.shape
    model = heads * size
    length = packed_ref.shape[0]
    held = ((q_hbm, q_ref), (ko_hbm, ko_ref), (vo_hbm, vo_ref))
    loads = [pltpu.make_async_copy(*pair, sems.at[n]) for n, pair in enumerate(held)]
    for load in loads:
        load.start()
    plain = size ** (-0.5)
    scale = plain * LOG2E
    place = place_ref[cell : cell + 1, :]
    count = count_of(place)
    pad_heads(gm_s, gmix_ref[...].reshape(model, rows))

    def run(n):
        first = pl.ds(0, n)
        held = ((packed_hbm, packed_ref), (keys_hbm, keys_ref))
        late = [
            pltpu.make_async_copy(far.at[first], near.at[first], sems.at[3 + at])
            for at, (far, near) in enumerate(held)
        ]
        for load in late:
            load.start()
        for load in loads:
            load.wait()
        pad_heads(q_s, q_ref[...].reshape(model, rows))
        for load in late:
            load.wait()
        packed = packed_ref[0:n, :]
        kT_s[:, :, 0:n] = dot(wkT_ref[...], packed, NT).astype(bf16).reshape(heads, size, n)
        values = (dot(packed, wv_ref[...]) + vec_ref[7:8, :]).astype(bf16)
        v_s[0:n, :] = values

        def head(h, at, wide):
            here = pl.ds(at, wide)
            pair = pl.ds(pl.multiple_of(h // 2 * 2 * size, 2 * size), 2 * size)
            k_pair = keys_ref[0:n, pair]
            v_pair = v_s[0:n, pair]
            q_full = q_s[h, :, here]
            gm_full = gm_s[h, :, here]
            lse = lse_ref[h, :, here]
            delta = delta_ref[h, :, here]
            raw = dot(k_pair, q_full)
            seen = lax.broadcasted_iota(jnp.int32, raw.shape, 0) < count
            weights = jnp.where(seen, jnp.exp2(raw * scale - lse), 0.0)
            g_weights = dot(v_pair, gm_full)
            g_raw = ((plain * weights) * (g_weights - delta)).astype(bf16)
            gv_s[0:n, pair] += dot(weights.astype(bf16), gm_full, NT)
            gk_s[0:n, pair] += dot(g_raw, q_full, NT)
            gq = dot(kT_s[h, :, 0:n], g_raw)
            own_weight = jnp.exp2(self_ref[h, :, here] - lse)
            ko = ko_ref[h, :, here].astype(f32)
            vo = vo_ref[h, :, here].astype(f32)
            gm = gmix_ref[h, :, here].astype(f32)
            g_own = jnp.sum(gm * vo, axis=0, keepdims=True)
            g_own_raw = (plain * own_weight * (g_own - delta)).astype(bf16).astype(f32)
            gq_s[h, :, here] = (gq + g_own_raw * ko).astype(bf16)
            gko_s[h, :, here] = (g_own_raw * q_ref[h, :, here].astype(f32)).astype(bf16)
            gvo_s[h, :, here] = (own_weight * gm).astype(bf16)

        gk_s[0:n, :] = jnp.zeros((n, model), f32)
        gv_s[0:n, :] = jnp.zeros((n, model), f32)
        over_heads(head, heads, rows, n < length)
        gk = gk_s[0:n, :].astype(bf16)
        gv = gv_s[0:n, :].astype(bf16)
        gk_ref[0:n, :] = gk
        gv_ref[0:n, :] = gv
        held = ((gk_ref, gk_hbm), (gv_ref, gv_hbm))
        saves = [
            pltpu.make_async_copy(near.at[first], far.at[first], sems.at[3 + at])
            for at, (near, far) in enumerate(held)
        ]
        for save in saves:
            save.start()
        w_acc[model : 2 * model, :] = dot(gk, packed, TN)
        w_acc[2 * model :, :] = dot(gv, packed, TN)
        v_acc[1:2, :] = jnp.sum(gv.astype(f32), axis=0, keepdims=True)
        for save in saves:
            save.wait()

    by_size(count, sizes, run)
    held = ((gq_s, gq_hbm), (gko_s, gko_hbm), (gvo_s, gvo_hbm))
    saves = [pltpu.make_async_copy(*pair, sems.at[n]) for n, pair in enumerate(held)]
    for save in saves:
        save.start()
    gq = gq_s[...].reshape(model, rows)
    gko = gko_s[...].reshape(model, rows)
    gvo = gvo_s[...].reshape(model, rows)
    x_own = own_ref[0:rows, :]
    ones = jnp.ones((8, rows), bf16)
    w_q = dot(gq, x_own)
    w_k = w_acc[model : 2 * model, :] + dot(gko, x_own)
    w_v = w_acc[2 * model :, :] + dot(gvo, x_own)
    v_q = dot(ones, gq, NT)[0:1, :]
    v_v = v_acc[1:2, :] + dot(ones, gvo, NT)[0:1, :]
    if has_before:
        w_q = w_q + before_w_ref[0:model, :]
        w_k = w_k + before_w_ref[model : 2 * model, :]
        w_v = w_v + before_w_ref[2 * model :, :]
        v_q = v_q + before_v_ref[0:1, :]
        v_v = v_v + before_v_ref[1:2, :]
    if has_before:
        for at, total in enumerate((w_q, w_k, w_v)):
            w_low[at * model : (at + 1) * model, :] = total.T.astype(bf16)
        blank = jnp.zeros((8, model), f32)
        small = jnp.concatenate([blank, v_q, v_v, blank[2:]], 0)
        split_halves(here_ref, first_ref, second_ref, w_low, small)
    else:
        for at, total in enumerate((w_q, w_k, w_v)):
            first_ref[at * model : (at + 1) * model, :] = total
        second_ref[0:1, :] = v_q
        second_ref[1:2, :] = v_v
    for save in saves:
        save.wait()


def attention_backward(cell, here, place, own, weights, saved, stats, before, after, rows):
    half, model = own.shape
    length = 2 * half
    size = model // HEADS
    vmem = pl.BlockSpec(memory_space=pltpu.VMEM)
    before = before or ()
    inputs = (here, place, own, *weights, *saved, *stats, *before, *after)
    hbm = pl.BlockSpec(memory_space=pltpu.HBM)
    anywhere = pl.BlockSpec(memory_space=pl.ANY)
    per_key = pltpu.VMEM((length, model), bf16)
    key_sum = pltpu.VMEM((length, model), f32)
    per_head = pltpu.VMEM((HEADS, size, rows), bf16)
    padded = pltpu.VMEM((HEADS, 2 * size, rows), bf16)
    by_key = pltpu.HBM((length, model), bf16)
    by_head = pltpu.HBM((HEADS, size, rows), bf16)
    if not before:
        sums = [
            jax.ShapeDtypeStruct((3 * model, model), f32),
            jax.ShapeDtypeStruct((8, model), f32),
        ]
    else:
        sums = [jax.ShapeDtypeStruct((3 * model // 2 + 16, model), bf16)] * 2
    return pl.pallas_call(
        functools.partial(backward_kernel, sizes_of(length), bool(before), len(after), cell),
        out_shape=(by_key, by_key, by_head, by_head, by_head, *sums),
        in_specs=[
            pl.BlockSpec(memory_space=pltpu.SMEM),
            *[vmem] * (2 + len(weights)),
            *[hbm] * len(saved),
            *[vmem] * (len(stats) + len(before)),
            *[anywhere] * len(after),
        ],
        out_specs=(hbm,) * 5 + (vmem,) * 2,
        scratch_shapes=[
            per_head,
            per_head,
            per_head,
            per_key,
            per_key,
            per_key,
            per_key,
            per_head,
            per_head,
            per_head,
            pltpu.VMEM((HEADS, size, length), bf16),
            per_key,
            key_sum,
            key_sum,
            pltpu.VMEM((3 * model, model), f32),
            pltpu.VMEM((8, model), f32),
            padded,
            padded,
            pltpu.VMEM((3 * model, model), bf16),
            pltpu.SemaphoreType.DMA((5,)),
        ],
        compiler_params=pltpu.CompilerParams(vmem_limit_bytes=BACKWARD_BYTES),
        cost_estimate=pl.CostEstimate(
            flops=30 * rows * length * model, bytes_accessed=16 << 20, transcendentals=0
        ),
        name="attention_backward",
    )(*inputs)


def inputs_kernel(
    sizes,
    cell,
    after,
    place_ref,
    gk_hbm,
    gv_hbm,
    gq_hbm,
    gko_hbm,
    gvo_hbm,
    wqT_ref,
    wkT_ref,
    wvT_ref,
    gh1_ref,
    *rest,
):
    kept_ref, sent_ref, gk_ref, gv_ref, gq_ref, gko_ref, gvo_ref, full_s, sems = rest[after:]
    held = ((gq_hbm, gq_ref), (gko_hbm, gko_ref), (gvo_hbm, gvo_ref))
    loads = [pltpu.make_async_copy(*pair, sems.at[n]) for n, pair in enumerate(held)]
    heads, size, rows = gq_ref.shape
    length, model = gk_ref.shape
    half = length // 2
    place = place_ref[cell : cell + 1, :]

    def run(n):
        first = pl.ds(0, n)
        late = [
            pltpu.make_async_copy(far.at[first], near.at[first], sems.at[3 + at])
            for at, (far, near) in enumerate(((gk_hbm, gk_ref), (gv_hbm, gv_ref)))
        ]
        for load in late + loads:
            load.start()
        for load in late:
            load.wait()
        g_packed = dot(gk_ref[0:n, :], wkT_ref[...]) + dot(gv_ref[0:n, :], wvT_ref[...])
        spot = lax.broadcasted_iota(jnp.int32, (length, n), 1).astype(f32)
        spread = (spot == column(place, 8)).astype(f32).astype(bf16)
        full_s[...] = dot(spread, g_packed.astype(bf16))

    by_size(count_of(place), sizes, run)
    for load in loads:
        load.wait()
    whole = lambda ref: ref[...].reshape(model, rows)
    mine = dot(whole(gq_ref), wqT_ref[...], TN) + dot(whole(gko_ref), wkT_ref[...], TN)
    mine = mine + dot(whole(gvo_ref), wvT_ref[...], TN)
    kept_ref[0:rows, :] = full_s[0:rows, :] + mine + gh1_ref[...]
    if rows < half:
        kept_ref[rows:, :] = full_s[rows:half, :]
    sent_ref[...] = full_s[half:, :].astype(bf16)


def input_gradients(cell, place, grads, weights, gh1, after):
    length, model = grads[0].shape
    rows = gh1.shape[0]
    vmem = pl.BlockSpec(memory_space=pltpu.VMEM)
    hbm = pl.BlockSpec(memory_space=pltpu.HBM)
    per_key = pltpu.VMEM((length, model), bf16)
    per_head = pltpu.VMEM(grads[2].shape, bf16)
    grads = [pltpu.with_memory_space_constraint(array, pltpu.HBM) for array in grads]
    return pl.pallas_call(
        functools.partial(inputs_kernel, sizes_of(length), cell, len(after)),
        out_shape=(
            jax.ShapeDtypeStruct((length // 2, model), f32),
            jax.ShapeDtypeStruct((length // 2, model), bf16),
        ),
        in_specs=[vmem]
        + [hbm] * 5
        + [vmem] * 4
        + [pl.BlockSpec(memory_space=pl.ANY)] * len(after),
        out_specs=(vmem,) * 2,
        scratch_shapes=[
            per_key,
            per_key,
            per_head,
            per_head,
            per_head,
            pltpu.VMEM((length, model), f32),
            pltpu.SemaphoreType.DMA((5,)),
        ],
        compiler_params=pltpu.CompilerParams(vmem_limit_bytes=INPUTS_BYTES),
        cost_estimate=pl.CostEstimate(
            flops=4 * length * length * model, bytes_accessed=8 << 20, transcendentals=0
        ),
        name="input_gradients",
    )(place, *grads, *weights, gh1, *after)


def exchange(piece, axis, partner):
    count = lax.axis_size(axis)
    return lax.ppermute(piece, axis, [(i, i ^ partner) for i in range(count)])


def radices_of(count):
    radices = []
    while count > 1:
        radix = 4 if count % 4 == 0 else 2
        radices.append(radix)
        count //= radix
    return radices


def reduce_plan():
    plan = [("cells", 2, 1)]
    for axis, stride in (("blk", 1), ("cells", 2)):
        for radix in radices_of(lax.axis_size(axis) // stride):
            plan.append((axis, radix, stride))
            stride *= radix
    return plan


def send_step(step, big, small):
    axis, radix, stride = step
    digit = (lax.axis_index(axis) // stride) % radix
    parts, rows, model = big.shape
    count = rows // radix
    arrived = []
    for other in range(1, radix):
        piece = lax.dynamic_slice_in_dim(big, (digit ^ other) * count, count, 1)
        sent = jnp.concatenate([piece.reshape(parts * count, model), small], 0)
        arrived.append(exchange(sent, axis, other * stride))
    return arrived


def sum_step(step, big, small, arrived):
    axis, radix, stride = step
    digit = (lax.axis_index(axis) // stride) % radix
    parts, rows, model = big.shape
    count = rows // radix
    big = lax.dynamic_slice_in_dim(big, digit * count, count, 1).astype(f32)
    small = small.astype(f32)
    for got in arrived:
        big = big + got[: parts * count].reshape(parts, count, model).astype(f32)
        small = small + got[parts * count :].astype(f32)
    return big.astype(bf16), small.astype(bf16)


def reduce_step(step, big, small):
    return sum_step(step, big, small, send_step(step, big, small))


def core_step(mine, other):
    total = mine.astype(f32) + exchange(other, "cells", 1).astype(f32)
    total = total.astype(bf16)
    count = total.shape[0] - 16
    return total[None, :count], total[count:]


def share_step(step, big):
    axis, radix, stride = step
    return [big] + [exchange(big, axis, other * stride) for other in range(1, radix)]


def gather_step(step, parts):
    axis, radix, stride = step
    digit = (lax.axis_index(axis) // stride) % radix
    ordered = []
    for place in range(radix):
        chosen = parts[place]
        for d in range(1, radix):
            chosen = jnp.where(digit == d, parts[place ^ d], chosen)
        ordered.append(chosen)
    return jnp.concatenate(ordered, 1)


def finish_kernel(here_ref, near_ref, far_ref, *rest):
    outs, (whole_s, sems) = rest[:-2], rest[-2:]
    core = here_ref[2]
    parts, count, model = near_ref.shape
    size = outs[0].shape[0]
    saves = []
    for part in range(parts):
        for ref, side in ((near_ref, core), (far_ref, 1 - core)):
            rows = pl.ds(pl.multiple_of(side * count, count), count)
            whole_s[part, rows, :] = ref[part].astype(f32)
        for at in range(2 * count // size):
            out = part * (2 * count // size) + at
            save = pltpu.make_async_copy(
                whole_s.at[part, pl.ds(at * size, size)], outs[out], sems.at[out]
            )
            save.start()
            saves.append(save)
    for save in saves:
        save.wait()


def finish(here, near, far):
    parts, count, model = near.shape
    number = parts * 2 * count // model
    vmem = pl.BlockSpec(memory_space=pltpu.VMEM)
    return pl.pallas_call(
        finish_kernel,
        out_shape=[pltpu.HBM((model, model), f32)] * number,
        in_specs=[pl.BlockSpec(memory_space=pltpu.SMEM), vmem, vmem],
        out_specs=[pl.BlockSpec(memory_space=pltpu.HBM)] * number,
        scratch_shapes=[
            pltpu.VMEM((parts, 2 * count, model), f32),
            pltpu.SemaphoreType.DMA((number,)),
        ],
        compiler_params=pltpu.CompilerParams(vmem_limit_bytes=INPUTS_BYTES),
        name="finish",
    )(here, near, far)


def swap(parts, flag):
    first, second = parts
    return jnp.where(flag == 1, second, first), jnp.where(flag == 1, first, second)


def body(
    tokens,
    known_flags,
    w_query,
    b_query,
    w_key,
    w_value,
    b_value,
    w_out,
    b_out,
    gain_one,
    shift_one,
    w_up,
    b_up,
    w_down,
    b_down,
    gain_two,
    shift_two,
    cotangent,
):
    cells, rows, model = tokens.shape
    blocks = lax.axis_size("blk")
    others = lax.axis_size("cells")
    part = rows // 2
    half = 2 * rows
    length = 2 * half
    block = lax.axis_index("blk")
    core = lax.axis_index("cells") % 2
    x, y = block % 2, block // 2
    axes = ("blk", "cells")

    def route(i, j):
        pairs = []
        for b in range(blocks):
            for c in range(others):
                there = 2 * (c % 2) + ((b % 2) ^ i)
                pairs.append((b * others + c, there * others + c - c % 2 + ((b // 2) ^ j)))
        return pairs

    def route_back(i, j):
        return [(there, here) for here, there in route(i, j)]

    both = ((0, 0), (0, 1), (1, 0), (1, 1))

    def near_rows(source, j):
        return lax.dynamic_slice_in_dim(source, (y ^ j) * part, part, 1)

    def cell_of(rows_sent, i):
        return lax.dynamic_slice_in_dim(rows_sent, x ^ i, 1, 0)

    turned = (w_query.T, w_key.T, w_value.T)
    vectors = [b_out, gain_one, shift_one, b_up, b_down, gain_two, shift_two, b_value, b_query]
    vectors = jnp.concatenate([jnp.stack(vectors).astype(f32), jnp.zeros((7, model), f32)], 0)
    first = {}
    for i, j in both:
        first[i, j] = lax.ppermute(cell_of(near_rows(tokens, j), i)[0], axes, route(i, j))
    here = jnp.stack([x, y, core]).astype(jnp.int32)
    place, *payloads = prepare(
        here, known_flags, exchange(known_flags, "cells", 1), tokens, cotangent
    )
    rest = {
        ij: lax.ppermute(sent, axes, route(*ij)) for ij, sent in zip(both, payloads[:4])
    }
    cot = [lax.ppermute(sent, axes, route(*ij)) for ij, sent in zip(both, payloads[4:])]
    wqT, wkT, wvT = turned
    pieces = [first[ij] for ij in both]
    own = list(join(pieces, [[(n, None) for n in range(4)]], (place, *turned, vectors)))
    other = [exchange(own[0], "cells", 1)]
    work = (half, rows)

    def attend(k):
        return attention_forward(
            k, place, own[k], other[k], (wqT, wkT, w_key, wvT, vectors), work[k]
        )

    forward = [attend(0)]
    mix = forward[0][0]
    own += join([rest[ij] for ij in both], [[(n, None) for n in range(4)]], (mix,))
    other.append(exchange(own[1], "cells", 1))
    forward.append(attend(1))
    mids = middle(
        here,
        [mix.reshape(model, half), forward[1][0].reshape(model, rows)],
        own,
        cot,
        (w_out, w_up, w_down),
        vectors,
    )
    mids, halves = (mids[:4], mids[4:8]), mids[8:]
    plan = reduce_plan()
    early, early_small = core_step(*halves)

    out_back = {}
    for i, j in both:
        pieces = [mids[0][0][(2 * i + j) * part : (2 * i + j + 1) * part]]
        if i == 0:
            pieces.append(mids[1][0][j * part : (j + 1) * part])
        out_back[i, j] = lax.ppermute(jnp.stack(pieces), axes, route_back(i, j))

    def rejoin(from_i):
        return jnp.concatenate(swap(from_i, y), 0)

    near, far = (rejoin((out_back[i, 0][0], out_back[i, 1][0])) for i in range(2))
    layer_out = jnp.stack([*swap((near, far), x), rejoin((out_back[0, 0][1], out_back[0, 1][1]))])

    def attend_back(k, before, after):
        mix, lse, own_score, *saved = forward[k]
        out, gh1, g_mix, delta = mids[k]
        return attention_backward(
            k,
            here,
            place,
            own[k],
            (wkT, w_value, vectors),
            saved,
            (lse, own_score, g_mix, delta),
            before,
            after,
            work[k],
        )

    def keep(k, grads, after):
        return input_gradients(k, place, grads, (wqT, wkT, wvT), mids[k][1], after)

    def whole_rows(mine, sent):
        return (mine + exchange(sent, "cells", 1).astype(f32)).astype(bf16)

    def give_back(kept):
        back = []
        for n, (i, j) in enumerate(both):
            sent = jnp.stack([rows[n * part : (n + 1) * part] for rows in kept])
            back.append(lax.ppermute(sent, axes, route_back(i, j)))
        return back

    *grads_a, first_sum, second_sum = attend_back(0, None, ())
    *grads_b, mine, other_half = attend_back(1, (first_sum, second_sum), (early, layer_out))
    early, early_small = reduce_step(plan[1], early, early_small)
    mine, other_half, early, early_small = lax.optimization_barrier(
        (mine, other_half, early, early_small)
    )
    late, late_small = core_step(mine, other_half)
    kept = keep(0, grads_a, (late,))
    late, late_small = reduce_step(plan[1], late, late_small)
    late, late_small, kept = lax.optimization_barrier((late, late_small, kept))
    kept_a = whole_rows(*kept)
    kept = keep(1, grads_b, (late,))
    big = jnp.concatenate([early, late], 0)
    small = (early_small.astype(f32) + late_small.astype(f32)).astype(bf16)
    for at, step in enumerate(plan[2:]):
        arrived = send_step(step, big, small)
        if at == 0:
            arrived, kept = lax.optimization_barrier((arrived, kept))
        big, small = sum_step(step, big, small, arrived)
    back = give_back([kept_a, whole_rows(*kept)])
    for step in reversed(plan[2:]):
        parts = share_step(step, big)
        if step is plan[2]:
            parts, back = lax.optimization_barrier((parts, back))
        big = gather_step(step, parts)
    big = gather_step(plan[1], share_step(plan[1], big))

    near, far, near_last, far_last = (
        rejoin((back[2 * i][k], back[2 * i + 1][k])).astype(f32) for k in range(2) for i in range(2)
    )
    grad_tokens = jnp.stack([*swap((near, far), x), near_last + far_last])
    big, small, grad_tokens = lax.optimization_barrier((big, small, grad_tokens))
    g_out, g_up, g_down, g_query, g_key, g_value = finish(here, big, exchange(big, "cells", 1))
    small = small.astype(f32)
    g_b_out, g_gain_one, g_shift_one, g_b_up, g_b_down, g_gain_two, g_shift_two = (
        small[n] for n in range(7)
    )
    return (
        layer_out,
        grad_tokens,
        g_query,
        small[8],
        g_key,
        g_value,
        small[9],
        g_out,
        g_b_out,
        g_gain_one,
        g_shift_one,
        g_up,
        g_b_up,
        g_down,
        g_b_down,
        g_gain_two,
        g_shift_two,
    )


def solution(mesh):
    rows = P("cells", "blk", None)
    return jax.shard_map(
        body,
        mesh=mesh,
        in_specs=(rows, P("cells", None)) + (P(),) * 15 + (rows,),
        out_specs=(rows, rows) + (P(),) * 15,
        check_vma=False,
    )
```

```python
import functools
import math

import jax
import jax.numpy as jnp
from jax import lax
from jax.experimental import pallas as pl
from jax.experimental.pallas import tpu as pltpu
from jax.sharding import PartitionSpec as P

HEADS = 8
EPSILON = 1e-05
LOG2E = math.log2(math.e)
NONE = -1e30
NN = (((1,), (0,)), ((), ()))
NT = (((1,), (1,)), ((), ()))
TN = (((0,), (0,)), ((), ()))
f32 = jnp.float32
bf16 = jnp.bfloat16
SMALL_BYTES = 6 * 1024 * 1024
INPUTS_BYTES = 20 * 1024 * 1024
FORWARD_BYTES = 20 * 1024 * 1024
MIDDLE_BYTES = 20 * 1024 * 1024
BACKWARD_BYTES = 40 * 1024 * 1024


def dot(a, b, dims=NN):
    return lax.dot_general(a, b, dims, preferred_element_type=f32)


def sizes_of(length):
    return [length * 13 // 24 // 64 * 64, length]


def by_size(count, sizes, run):
    low = 0
    for at, size in enumerate(sizes):
        fits = count <= size
        if at:
            fits = fits & (count > low)
        pl.when(fits)(functools.partial(run, size))
        low = size


def pad_heads(padded, whole):
    heads, double, _ = padded.shape
    size = double // 2
    blank = jnp.zeros((size, whole.shape[1]), whole.dtype)
    for h in range(heads):
        part = whole[h * size : (h + 1) * size, :]
        padded[h] = jnp.concatenate([part, blank] if h % 2 == 0 else [blank, part], 0)


def pair_of(head, wide):
    start = head // 2 * wide
    return pl.ds(start if isinstance(head, int) else pl.multiple_of(start, wide), wide)


def over_heads(run, heads, rows, common):
    if common:

        for h in range(heads):
            run(h, 0, rows)
    else:
        wide = 128
        chunks = rows // wide

        def step(i, carry):
            run(i // chunks, pl.multiple_of(i % chunks * wide, wide), wide)
            return carry

        lax.fori_loop(0, heads * chunks, step, 0)


def prepare_kernel(here_ref, near_ref, far_ref, tokens_ref, cot_ref, place_ref, *sent):
    x, y, core = here_ref[0], here_ref[1], here_ref[2]
    count = tokens_ref.shape[1] // 2
    sent, cots = sent[:4], sent[4:]
    for at, ref in enumerate(sent):
        rows = pl.ds(pl.multiple_of((y ^ (at % 2)) * count, count), count)
        ref[...] = tokens_ref[2, rows, :]
        cots[at][0] = cot_ref[x ^ (at // 2), rows, :]
        if at < 2:
            cots[at][1] = cot_ref[2, rows, :]
    length = near_ref.shape[1]
    part = length // 8
    flags = jnp.where(core == y, near_ref[...], far_ref[...]).astype(f32)
    flags = jnp.concatenate([jnp.where(x == 1, flags[1:2], flags[0:1]), flags[2:3]], 0)
    pieces = {}
    for at in range(8):
        pieces[at // 4, at // 2 % 2, at % 2] = flags[:, at * part : (at + 1) * part]
    for bit, axis in ((core, 2), (x, 1)):
        turn = lambda k, axis=axis: tuple(1 - v if n == axis else v for n, v in enumerate(k))
        pieces = {k: jnp.where(bit == 1, pieces[turn(k)], v) for k, v in pieces.items()}
    ordered = []
    for side in range(2):
        for i in range(2):
            for j in range(2):
                swapped = core != side
                ordered.append(jnp.where(swapped, pieces[1 - j, i, side], pieces[j, i, side]))
    flags = jnp.concatenate(ordered, 1)
    width = 128
    rows = lax.broadcasted_iota(jnp.int32, (width, width), 0)
    lower = (rows <= lax.broadcasted_iota(jnp.int32, (width, width), 1)).astype(f32).astype(bf16)
    tiles = jnp.concatenate([flags[:, at : at + width] for at in range(0, length, width)], 0)
    inside = dot(tiles.astype(bf16), lower)
    ahead = jnp.full((2, 1), -1.0, f32)
    placed = []
    for at in range(length // width):
        tile = inside[2 * at : 2 * at + 2, :]
        placed.append(tile + ahead)
        ahead = ahead + tile[:, width - 1 :]
    place_ref[...] = jnp.where(flags > 0, jnp.concatenate(placed, 1), -1.0)


def prepare(here, near, far, tokens, cotangent):
    _, rows, model = tokens.shape
    vmem = pl.BlockSpec(memory_space=pltpu.VMEM)
    sent = [jax.ShapeDtypeStruct((rows // 2, model), bf16)] * 4
    sent += [jax.ShapeDtypeStruct((n, rows // 2, model), bf16) for n in (2, 2, 1, 1)]
    return pl.pallas_call(
        prepare_kernel,
        out_shape=[jax.ShapeDtypeStruct((2, near.shape[1]), f32), *sent],
        in_specs=[pl.BlockSpec(memory_space=pltpu.SMEM)] + [vmem] * 4,
        out_specs=[vmem] * 9,
        compiler_params=pltpu.CompilerParams(vmem_limit_bytes=SMALL_BYTES),
        name="prepare",
    )(here, near, far, tokens, cotangent)


def count_of(place):
    return (jnp.max(place) + 1.0).astype(jnp.int32)


def column(row, lanes):
    return jnp.broadcast_to(row, (lanes, row.shape[1])).T[:, 0:1]


def join_kernel(layout, after, *refs):
    outs = refs[len(refs) - len(layout) :]
    for out_ref, pieces in zip(outs, layout):
        count = out_ref.shape[0] // len(pieces)
        for at, (source, place) in enumerate(pieces):
            piece = refs[source][...] if place is None else refs[source][place]
            out_ref[at * count : (at + 1) * count, :] = piece


def join(pieces, layout, after=()):
    count, model = pieces[0].shape[-2:]
    vmem = pl.BlockSpec(memory_space=pltpu.VMEM)
    anywhere = pl.BlockSpec(memory_space=pl.ANY)
    return pl.pallas_call(
        functools.partial(join_kernel, layout, len(after)),
        out_shape=[jax.ShapeDtypeStruct((count * len(p), model), bf16) for p in layout],
        in_specs=[vmem] * len(pieces) + [anywhere] * len(after),
        out_specs=[vmem] * len(layout),
        compiler_params=pltpu.CompilerParams(vmem_limit_bytes=SMALL_BYTES),
        name="join",
    )(*pieces, *after)


def forward_kernel(
    sizes,
    cell,
    place_ref,
    own_ref,
    other_ref,
    wqT_ref,
    wkT_ref,
    wk_ref,
    wvT_ref,
    vec_ref,
    mix_ref,
    lse_ref,
    self_ref,
    q_hbm,
    ko_hbm,
    vo_hbm,
    packed_hbm,
    keys_hbm,
    q_ref,
    ko_ref,
    vo_ref,
    packed_ref,
    keys_ref,
    v_s,
    q_s,
    sems,
):
    heads, size, rows = q_ref.shape
    scale = size ** (-0.5) * LOG2E
    place = place_ref[cell : cell + 1, :]
    count = count_of(place)
    half = own_ref.shape[0]
    length = 2 * half
    b_value = column(vec_ref[7:8, :], 8)
    x_own = own_ref[0:rows, :]
    q = (dot(wqT_ref[...], x_own, NT) + column(vec_ref[8:9, :], 8)).astype(bf16)
    ko = dot(wkT_ref[...], x_own, NT).astype(bf16)
    vo = (dot(wvT_ref[...], x_own, NT) + b_value).astype(bf16)
    q_ref[...] = q.reshape(heads, size, rows)
    ko_ref[...] = ko.reshape(heads, size, rows)
    vo_ref[...] = vo.reshape(heads, size, rows)
    held = ((q_ref, q_hbm), (ko_ref, ko_hbm), (vo_ref, vo_hbm))
    saves = [pltpu.make_async_copy(*pair, sems.at[n]) for n, pair in enumerate(held)]
    for save in saves:
        save.start()
    own_score = (q.astype(f32) * ko.astype(f32)).reshape(heads, size, rows).sum(1, keepdims=True)
    self_ref[...] = jnp.where(place[None, :, 0:rows] < 0, own_score * scale, NONE)
    pad_heads(q_s, q)

    def run(n):
        spot = lax.broadcasted_iota(jnp.int32, (n, half), 0).astype(f32)
        pick_own = (spot == place[:, 0:half]).astype(f32).astype(bf16)
        pick_other = (spot == place[:, half:]).astype(f32).astype(bf16)
        packed = (dot(pick_own, own_ref[...]) + dot(pick_other, other_ref[...])).astype(bf16)
        packed_ref[0:n, :] = packed
        keys = dot(packed, wk_ref[...]).astype(bf16)
        keys_ref[0:n, :] = keys
        first = pl.ds(0, n)
        held = ((packed_ref, packed_hbm), (keys_ref, keys_hbm))
        late = [
            pltpu.make_async_copy(near.at[first], far.at[first], sems.at[3 + at])
            for at, (near, far) in enumerate(held)
        ]
        for save in late:
            save.start()
        v_s[:, :, 0:n] = (
            (dot(wvT_ref[...], packed, NT) + b_value).astype(bf16).reshape(heads, size, n)
        )

        def head(h, at, wide):
            pair = pair_of(h, 2 * size)
            raw = dot(keys_ref[0:n, pair], q_s[h, :, pl.ds(at, wide)])
            seen = lax.broadcasted_iota(jnp.int32, raw.shape, 0) < count
            scores = jnp.where(seen, raw * scale, NONE)
            own = self_ref[h, :, pl.ds(at, wide)]
            top = jnp.maximum(jnp.max(scores, axis=0, keepdims=True), own)
            weights = jnp.exp2(scores - top)
            own_weight = jnp.exp2(own - top)
            total = jnp.sum(weights, axis=0, keepdims=True) + own_weight
            mixed = dot(v_s[h, :, 0:n], weights.astype(bf16))
            mixed = mixed + own_weight * vo_ref[h, :, pl.ds(at, wide)].astype(f32)
            mix_ref[h, :, pl.ds(at, wide)] = (mixed / total).astype(bf16)
            lse_ref[h, :, pl.ds(at, wide)] = top + jnp.log(total) * LOG2E

        over_heads(head, heads, rows, n < length)
        for save in late:
            save.wait()

    by_size(count, sizes, run)
    for save in saves:
        save.wait()


def attention_forward(cell, place, own, other, weights, rows):
    held = [pltpu.with_memory_space_constraint(w, pltpu.HBM) for w in weights]
    weights = held if cell else (*weights[:-1], held[-1])
    half, model = own.shape
    length = 2 * half
    size = model // HEADS
    vmem = pl.BlockSpec(memory_space=pltpu.VMEM)
    by_head = pltpu.VMEM((HEADS, size, rows), bf16)
    by_key = pltpu.VMEM((length, model), bf16)
    head_rows = jax.ShapeDtypeStruct((HEADS, size, rows), bf16)
    row_stat = jax.ShapeDtypeStruct((HEADS, 1, rows), f32)
    return pl.pallas_call(
        functools.partial(forward_kernel, sizes_of(length), cell),
        out_shape=(
            head_rows,
            row_stat,
            row_stat,
            *[pltpu.HBM(head_rows.shape, bf16)] * 3,
            *[pltpu.HBM((length, model), bf16)] * 2,
        ),
        in_specs=[vmem] * (3 + len(weights)),
        out_specs=(vmem,) * 3 + (pl.BlockSpec(memory_space=pltpu.HBM),) * 5,
        scratch_shapes=[
            by_head,
            by_head,
            by_head,
            by_key,
            by_key,
            pltpu.VMEM((HEADS, size, length), bf16),
            pltpu.VMEM((HEADS, 2 * size, rows), bf16),
            pltpu.SemaphoreType.DMA((5,)),
        ],
        compiler_params=pltpu.CompilerParams(vmem_limit_bytes=FORWARD_BYTES),
        cost_estimate=pl.CostEstimate(
            flops=16 * rows * length * model, bytes_accessed=8 << 20, transcendentals=0
        ),
        name="attention_forward",
    )(place, own, other, *weights)


def split_halves(here_ref, mine_ref, other_ref, whole_ref, small):
    count = whole_ref.shape[0] // 2
    core = here_ref[2]
    for ref, side in ((mine_ref, core), (other_ref, 1 - core)):
        ref[0:count, :] = whole_ref[pl.ds(pl.multiple_of(side * count, count), count), :]
        ref[count:, :] = small.astype(bf16)


def middle_kernel(
    here_ref,
    mix_a_ref,
    x_a_ref,
    mix_b_ref,
    x_b_ref,
    cot_0_ref,
    cot_1_ref,
    cot_2_ref,
    cot_3_ref,
    w_out_ref,
    w_up_ref,
    w_down_ref,
    vec_ref,
    *rest,
):
    outs_a, outs_b, (mine_ref, other_ref, mix_ref, x_ref, cot_ref, w_acc, v_acc, w_low) = (
        rest[:4],
        rest[4:8],
        rest[8:],
    )
    step = pl.program_id(0)
    last = pl.num_programs(0) - 1
    model = x_ref.shape[1]

    @pl.when(step == 0)
    def _():
        w_acc[...] = jnp.zeros_like(w_acc)
        v_acc[...] = jnp.zeros_like(v_acc)

    part = cot_ref.shape[0] // 2
    for at, pair in enumerate(((cot_0_ref, cot_1_ref), (cot_2_ref, cot_3_ref))):

        @pl.when(step == at)
        def _():
            mix_ref[...] = mix_a_ref[...]
            x_ref[...] = x_a_ref[...]
            cot_ref[0:part, :] = pair[0][0]
            cot_ref[part:, :] = pair[1][0]

    @pl.when(step == last)
    def _():
        mix_ref[...] = mix_b_ref[...]
        x_ref[...] = x_b_ref[...]
        cot_ref[0:part, :] = cot_0_ref[1]
        cot_ref[part:, :] = cot_1_ref[1]

    b_out, gain_one, shift_one, b_up, b_down, gain_two, shift_two = (
        vec_ref[i : i + 1, :] for i in range(7)
    )

    def mean(v):
        return jnp.mean(v, axis=-1, keepdims=True)

    def rows(v):
        return jnp.sum(v, axis=0, keepdims=True)

    attn_in = mix_ref[...]
    h1 = x_ref[...].astype(f32) + dot(attn_in, w_out_ref[...], TN) + b_out
    c1 = h1 - mean(h1)
    inv1 = lax.rsqrt(mean(c1 * c1) + EPSILON)
    n1 = c1 * inv1
    x1 = n1 * gain_one + shift_one
    x1_low = x1.astype(bf16)
    up = dot(x1_low, w_up_ref[...]) + b_up
    cdf = 0.5 + 0.5 * lax.erf(up * (0.5**0.5))
    slope = cdf + up * (jnp.exp(-0.5 * up * up) * (1.0 / math.sqrt(2.0 * math.pi)))
    act = (up * cdf).astype(bf16)
    h2 = x1 + dot(act, w_down_ref[...]) + b_down
    c2 = h2 - mean(h2)
    inv2 = lax.rsqrt(mean(c2 * c2) + EPSILON)
    n2 = c2 * inv2
    out = (n2 * gain_two + shift_two).astype(bf16)
    cot = cot_ref[...].astype(f32)
    g_gain_two = rows(cot * n2)
    g_shift_two = rows(cot)
    gn2 = cot * gain_two
    gh2 = inv2 * (gn2 - mean(gn2) - n2 * mean(gn2 * n2))
    g_down = gh2.astype(bf16)
    w_acc[2 * model :, :] += dot(act, g_down, TN)
    g_b_down = rows(g_down.astype(f32))
    g_up = (slope * dot(g_down, w_down_ref[...], NT)).astype(bf16)
    w_acc[model : 2 * model, :] += dot(x1_low, g_up, TN)
    g_b_up = rows(g_up.astype(f32))
    gx1 = gh2 + dot(g_up, w_up_ref[...], NT)
    g_gain_one = rows(gx1 * n1)
    g_shift_one = rows(gx1)
    gn1 = gx1 * gain_one
    gh1 = inv1 * (gn1 - mean(gn1) - n1 * mean(gn1 * n1))
    g_attn = gh1.astype(bf16)
    w_acc[0:model, :] += dot(attn_in, g_attn)
    g_b_out = rows(g_attn.astype(f32))
    g_mix = dot(w_out_ref[...], g_attn, NT).astype(bf16)
    size = model // HEADS
    delta = (g_mix.astype(f32) * attn_in.astype(f32)).reshape(HEADS, size, -1).sum(1, keepdims=True)
    results = (out, gh1, g_mix.reshape(HEADS, size, -1), delta)
    sums = (g_b_out, g_gain_one, g_shift_one, g_b_up, g_b_down, g_gain_two, g_shift_two)
    for at, term in enumerate(sums):
        v_acc[at : at + 1, :] += term

    @pl.when(step < last)
    def _():
        for ref, value in zip(outs_a, results):
            ref[...] = value

    @pl.when(step == last)
    def _():
        for ref, value in zip(outs_b, results):
            ref[...] = value
        w_low[...] = w_acc[...].astype(bf16)
        split_halves(here_ref, mine_ref, other_ref, w_low, v_acc[...])


def middle(here, mix, x, cot, weights, vectors):
    _, part, model = cot[0].shape
    block = 2 * part
    size = model // HEADS
    steps = 2
    whole = lambda shape: pl.BlockSpec(shape, lambda i: (0,) * len(shape))
    places = (lambda i: jnp.minimum(i, steps - 1), lambda i: 0)
    by_row = [pl.BlockSpec((block, model), lambda i, at=at: (at(i), 0)) for at in places]
    by_column = [pl.BlockSpec((model, block), lambda i, at=at: (0, at(i))) for at in places]
    by_head = [pl.BlockSpec((HEADS, size, block), lambda i, at=at: (0, 0, at(i))) for at in places]
    stats = [pl.BlockSpec((HEADS, 1, block), lambda i, at=at: (0, 0, at(i))) for at in places]
    square = whole((model, model))
    half_shape = (3 * model // 2 + 16, model)
    inputs, in_specs, out_shape, out_specs = [], [], [], []
    for k in range(2):
        rows = mix[k].shape[1]
        inputs += [mix[k], x[k]]
        in_specs += [by_column[k], by_row[k]]
        out_shape += [
            jax.ShapeDtypeStruct((rows, model), bf16),
            jax.ShapeDtypeStruct((rows, model), f32),
            jax.ShapeDtypeStruct((HEADS, size, rows), bf16),
            jax.ShapeDtypeStruct((HEADS, 1, rows), f32),
        ]
        out_specs += [by_row[k], by_row[k], by_head[k], stats[k]]
    return pl.pallas_call(
        middle_kernel,
        grid=(steps + 1,),
        out_shape=(
            *out_shape,
            jax.ShapeDtypeStruct(half_shape, bf16),
            jax.ShapeDtypeStruct(half_shape, bf16),
        ),
        in_specs=[
            pl.BlockSpec(memory_space=pltpu.SMEM),
            *in_specs,
            *[whole(piece.shape) for piece in cot],
            square,
            square,
            square,
            whole(vectors.shape),
        ],
        out_specs=(*out_specs, whole(half_shape), whole(half_shape)),
        scratch_shapes=[
            pltpu.VMEM((model, block), bf16),
            pltpu.VMEM((block, model), bf16),
            pltpu.VMEM((block, model), bf16),
            pltpu.VMEM((3 * model, model), f32),
            pltpu.VMEM((16, model), f32),
            pltpu.VMEM((3 * model, model), bf16),
        ],
        compiler_params=pltpu.CompilerParams(
            vmem_limit_bytes=MIDDLE_BYTES, dimension_semantics=("arbitrary",)
        ),
        cost_estimate=pl.CostEstimate(
            flops=36 * (steps + 1) * block * model * model,
            bytes_accessed=8 << 20,
            transcendentals=0,
        ),
        name="middle",
    )(here, *inputs, *cot, *weights, vectors)


def backward_kernel(
    sizes,
    has_before,
    after,
    cell,
    here_ref,
    place_ref,
    own_ref,
    wkT_ref,
    wv_ref,
    vec_ref,
    q_hbm,
    ko_hbm,
    vo_hbm,
    packed_hbm,
    keys_hbm,
    lse_ref,
    self_ref,
    gmix_ref,
    delta_ref,
    *rest,
):
    if has_before:
        before_w_ref, before_v_ref, *rest = rest
    rest = rest[after:]
    gk_hbm, gv_hbm, gq_hbm, gko_hbm, gvo_hbm, first_ref, second_ref, *rest = rest
    q_ref, ko_ref, vo_ref, packed_ref, keys_ref, gk_ref, gv_ref, gq_s, gko_s, gvo_s, *rest = rest
    kT_s, v_s, gk_s, gv_s, w_acc, v_acc, q_s, gm_s, w_low, sems = rest
    heads, size, rows = q_ref.shape
    model = heads * size
    length = packed_ref.shape[0]
    held = ((q_hbm, q_ref), (ko_hbm, ko_ref), (vo_hbm, vo_ref))
    loads = [pltpu.make_async_copy(*pair, sems.at[n]) for n, pair in enumerate(held)]
    for load in loads:
        load.start()
    plain = size ** (-0.5)
    scale = plain * LOG2E
    place = place_ref[cell : cell + 1, :]
    count = count_of(place)
    pad_heads(gm_s, gmix_ref[...].reshape(model, rows))

    def run(n):
        first = pl.ds(0, n)
        held = ((packed_hbm, packed_ref), (keys_hbm, keys_ref))
        late = [
            pltpu.make_async_copy(far.at[first], near.at[first], sems.at[3 + at])
            for at, (far, near) in enumerate(held)
        ]
        for load in late:
            load.start()
        for load in loads:
            load.wait()
        pad_heads(q_s, q_ref[...].reshape(model, rows))
        for load in late:
            load.wait()
        packed = packed_ref[0:n, :]
        kT_s[:, :, 0:n] = dot(wkT_ref[...], packed, NT).astype(bf16).reshape(heads, size, n)
        values = (dot(packed, wv_ref[...]) + vec_ref[7:8, :]).astype(bf16)
        v_s[0:n, :] = values

        def head(h, at, wide):
            here = pl.ds(at, wide)
            pair = pair_of(h, 2 * size)
            k_pair = keys_ref[0:n, pair]
            v_pair = v_s[0:n, pair]
            q_full = q_s[h, :, here]
            gm_full = gm_s[h, :, here]
            lse = lse_ref[h, :, here]
            delta = delta_ref[h, :, here]
            raw = dot(k_pair, q_full)
            seen = lax.broadcasted_iota(jnp.int32, raw.shape, 0) < count
            weights = jnp.where(seen, jnp.exp2(raw * scale - lse), 0.0)
            g_weights = dot(v_pair, gm_full)
            g_raw = ((plain * weights) * (g_weights - delta)).astype(bf16)
            gv_s[0:n, pair] += dot(weights.astype(bf16), gm_full, NT)
            gk_s[0:n, pair] += dot(g_raw, q_full, NT)
            gq = dot(kT_s[h, :, 0:n], g_raw)
            own_weight = jnp.exp2(self_ref[h, :, here] - lse)
            ko = ko_ref[h, :, here].astype(f32)
            vo = vo_ref[h, :, here].astype(f32)
            gm = gmix_ref[h, :, here].astype(f32)
            g_own = jnp.sum(gm * vo, axis=0, keepdims=True)
            g_own_raw = (plain * own_weight * (g_own - delta)).astype(bf16).astype(f32)
            gq_s[h, :, here] = (gq + g_own_raw * ko).astype(bf16)
            gko_s[h, :, here] = (g_own_raw * q_ref[h, :, here].astype(f32)).astype(bf16)
            gvo_s[h, :, here] = (own_weight * gm).astype(bf16)

        gk_s[0:n, :] = jnp.zeros((n, model), f32)
        gv_s[0:n, :] = jnp.zeros((n, model), f32)
        over_heads(head, heads, rows, n < length)
        gk = gk_s[0:n, :].astype(bf16)
        gv = gv_s[0:n, :].astype(bf16)
        gk_ref[0:n, :] = gk
        gv_ref[0:n, :] = gv
        held = ((gk_ref, gk_hbm), (gv_ref, gv_hbm))
        saves = [
            pltpu.make_async_copy(near.at[first], far.at[first], sems.at[3 + at])
            for at, (near, far) in enumerate(held)
        ]
        for save in saves:
            save.start()
        w_acc[model : 2 * model, :] = dot(gk, packed, TN)
        w_acc[2 * model :, :] = dot(gv, packed, TN)
        v_acc[1:2, :] = jnp.sum(gv.astype(f32), axis=0, keepdims=True)
        for save in saves:
            save.wait()

    by_size(count, sizes, run)
    held = ((gq_s, gq_hbm), (gko_s, gko_hbm), (gvo_s, gvo_hbm))
    saves = [pltpu.make_async_copy(*pair, sems.at[n]) for n, pair in enumerate(held)]
    for save in saves:
        save.start()
    gq = gq_s[...].reshape(model, rows)
    gko = gko_s[...].reshape(model, rows)
    gvo = gvo_s[...].reshape(model, rows)
    x_own = own_ref[0:rows, :]
    ones = jnp.ones((8, rows), bf16)
    w_q = dot(gq, x_own)
    w_k = w_acc[model : 2 * model, :] + dot(gko, x_own)
    w_v = w_acc[2 * model :, :] + dot(gvo, x_own)
    v_q = dot(ones, gq, NT)[0:1, :]
    v_v = v_acc[1:2, :] + dot(ones, gvo, NT)[0:1, :]
    if has_before:
        w_q = w_q + before_w_ref[0:model, :]
        w_k = w_k + before_w_ref[model : 2 * model, :]
        w_v = w_v + before_w_ref[2 * model :, :]
        v_q = v_q + before_v_ref[0:1, :]
        v_v = v_v + before_v_ref[1:2, :]
    if has_before:
        for at, total in enumerate((w_q, w_k, w_v)):
            w_low[at * model : (at + 1) * model, :] = total.T.astype(bf16)
        blank = jnp.zeros((8, model), f32)
        small = jnp.concatenate([blank, v_q, v_v, blank[2:]], 0)
        split_halves(here_ref, first_ref, second_ref, w_low, small)
    else:
        for at, total in enumerate((w_q, w_k, w_v)):
            first_ref[at * model : (at + 1) * model, :] = total
        second_ref[0:1, :] = v_q
        second_ref[1:2, :] = v_v
    for save in saves:
        save.wait()


def attention_backward(cell, here, place, own, weights, saved, stats, before, after, rows):
    half, model = own.shape
    length = 2 * half
    size = model // HEADS
    vmem = pl.BlockSpec(memory_space=pltpu.VMEM)
    before = before or ()
    inputs = (here, place, own, *weights, *saved, *stats, *before, *after)
    hbm = pl.BlockSpec(memory_space=pltpu.HBM)
    anywhere = pl.BlockSpec(memory_space=pl.ANY)
    per_key = pltpu.VMEM((length, model), bf16)
    key_sum = pltpu.VMEM((length, model), f32)
    per_head = pltpu.VMEM((HEADS, size, rows), bf16)
    padded = pltpu.VMEM((HEADS, 2 * size, rows), bf16)
    by_key = pltpu.HBM((length, model), bf16)
    by_head = pltpu.HBM((HEADS, size, rows), bf16)
    if not before:
        sums = [
            jax.ShapeDtypeStruct((3 * model, model), f32),
            jax.ShapeDtypeStruct((8, model), f32),
        ]
    else:
        sums = [jax.ShapeDtypeStruct((3 * model // 2 + 16, model), bf16)] * 2
    return pl.pallas_call(
        functools.partial(backward_kernel, sizes_of(length), bool(before), len(after), cell),
        out_shape=(by_key, by_key, by_head, by_head, by_head, *sums),
        in_specs=[
            pl.BlockSpec(memory_space=pltpu.SMEM),
            *[vmem] * (2 + len(weights)),
            *[hbm] * len(saved),
            *[vmem] * (len(stats) + len(before)),
            *[anywhere] * len(after),
        ],
        out_specs=(hbm,) * 5 + (vmem,) * 2,
        scratch_shapes=[
            per_head,
            per_head,
            per_head,
            per_key,
            per_key,
            per_key,
            per_key,
            per_head,
            per_head,
            per_head,
            pltpu.VMEM((HEADS, size, length), bf16),
            per_key,
            key_sum,
            key_sum,
            pltpu.VMEM((3 * model, model), f32),
            pltpu.VMEM((8, model), f32),
            padded,
            padded,
            pltpu.VMEM((3 * model, model), bf16),
            pltpu.SemaphoreType.DMA((5,)),
        ],
        compiler_params=pltpu.CompilerParams(vmem_limit_bytes=BACKWARD_BYTES),
        cost_estimate=pl.CostEstimate(
            flops=30 * rows * length * model, bytes_accessed=16 << 20, transcendentals=0
        ),
        name="attention_backward",
    )(*inputs)


def inputs_kernel(
    sizes,
    cell,
    after,
    place_ref,
    gk_hbm,
    gv_hbm,
    gq_hbm,
    gko_hbm,
    gvo_hbm,
    wqT_ref,
    wkT_ref,
    wvT_ref,
    gh1_ref,
    *rest,
):
    kept_ref, sent_ref, gk_ref, gv_ref, gq_ref, gko_ref, gvo_ref, full_s, sems = rest[after:]
    held = ((gq_hbm, gq_ref), (gko_hbm, gko_ref), (gvo_hbm, gvo_ref))
    loads = [pltpu.make_async_copy(*pair, sems.at[n]) for n, pair in enumerate(held)]
    heads, size, rows = gq_ref.shape
    length, model = gk_ref.shape
    half = length // 2
    place = place_ref[cell : cell + 1, :]

    def run(n):
        first = pl.ds(0, n)
        late = [
            pltpu.make_async_copy(far.at[first], near.at[first], sems.at[3 + at])
            for at, (far, near) in enumerate(((gk_hbm, gk_ref), (gv_hbm, gv_ref)))
        ]
        for load in late + loads:
            load.start()
        for load in late:
            load.wait()
        g_packed = dot(gk_ref[0:n, :], wkT_ref[...]) + dot(gv_ref[0:n, :], wvT_ref[...])
        spot = lax.broadcasted_iota(jnp.int32, (length, n), 1).astype(f32)
        spread = (spot == column(place, 8)).astype(f32).astype(bf16)
        full_s[...] = dot(spread, g_packed.astype(bf16))

    by_size(count_of(place), sizes, run)
    for load in loads:
        load.wait()
    whole = lambda ref: ref[...].reshape(model, rows)
    mine = dot(whole(gq_ref), wqT_ref[...], TN) + dot(whole(gko_ref), wkT_ref[...], TN)
    mine = mine + dot(whole(gvo_ref), wvT_ref[...], TN)
    kept_ref[0:rows, :] = full_s[0:rows, :] + mine + gh1_ref[...]
    if rows < half:
        kept_ref[rows:, :] = full_s[rows:half, :]
    sent_ref[...] = full_s[half:, :].astype(bf16)


def input_gradients(cell, place, grads, weights, gh1, after):
    length, model = grads[0].shape
    rows = gh1.shape[0]
    vmem = pl.BlockSpec(memory_space=pltpu.VMEM)
    hbm = pl.BlockSpec(memory_space=pltpu.HBM)
    per_key = pltpu.VMEM((length, model), bf16)
    per_head = pltpu.VMEM(grads[2].shape, bf16)
    grads = [pltpu.with_memory_space_constraint(array, pltpu.HBM) for array in grads]
    return pl.pallas_call(
        functools.partial(inputs_kernel, sizes_of(length), cell, len(after)),
        out_shape=(
            jax.ShapeDtypeStruct((length // 2, model), f32),
            jax.ShapeDtypeStruct((length // 2, model), bf16),
        ),
        in_specs=[vmem]
        + [hbm] * 5
        + [vmem] * 4
        + [pl.BlockSpec(memory_space=pl.ANY)] * len(after),
        out_specs=(vmem,) * 2,
        scratch_shapes=[
            per_key,
            per_key,
            per_head,
            per_head,
            per_head,
            pltpu.VMEM((length, model), f32),
            pltpu.SemaphoreType.DMA((5,)),
        ],
        compiler_params=pltpu.CompilerParams(vmem_limit_bytes=INPUTS_BYTES),
        cost_estimate=pl.CostEstimate(
            flops=4 * length * length * model, bytes_accessed=8 << 20, transcendentals=0
        ),
        name="input_gradients",
    )(place, *grads, *weights, gh1, *after)


def exchange(piece, axis, partner):
    count = lax.axis_size(axis)
    return lax.ppermute(piece, axis, [(i, i ^ partner) for i in range(count)])


def radices_of(count):
    radices = []
    while count > 1:
        radix = 4 if count % 4 == 0 else 2
        radices.append(radix)
        count //= radix
    return radices


def reduce_plan():
    plan = [("cells", 2, 1)]
    for axis, stride in (("blk", 1), ("cells", 2)):
        for radix in radices_of(lax.axis_size(axis) // stride):
            plan.append((axis, radix, stride))
            stride *= radix
    return plan


def send_step(step, big, small):
    axis, radix, stride = step
    digit = (lax.axis_index(axis) // stride) % radix
    parts, rows, model = big.shape
    count = rows // radix
    arrived = []
    for other in range(1, radix):
        piece = lax.dynamic_slice_in_dim(big, (digit ^ other) * count, count, 1)
        sent = jnp.concatenate([piece.reshape(parts * count, model), small], 0)
        arrived.append(exchange(sent, axis, other * stride))
    return arrived


def sum_step(step, big, small, arrived):
    axis, radix, stride = step
    digit = (lax.axis_index(axis) // stride) % radix
    parts, rows, model = big.shape
    count = rows // radix
    big = lax.dynamic_slice_in_dim(big, digit * count, count, 1).astype(f32)
    small = small.astype(f32)
    for got in arrived:
        big = big + got[: parts * count].reshape(parts, count, model).astype(f32)
        small = small + got[parts * count :].astype(f32)
    return big.astype(bf16), small.astype(bf16)


def reduce_step(step, big, small):
    return sum_step(step, big, small, send_step(step, big, small))


def core_step(mine, other):
    total = mine.astype(f32) + exchange(other, "cells", 1).astype(f32)
    total = total.astype(bf16)
    count = total.shape[0] - 16
    return total[None, :count], total[count:]


def share_step(step, big):
    axis, radix, stride = step
    return [big] + [exchange(big, axis, other * stride) for other in range(1, radix)]


def gather_step(step, parts):
    axis, radix, stride = step
    digit = (lax.axis_index(axis) // stride) % radix
    ordered = []
    for place in range(radix):
        chosen = parts[place]
        for d in range(1, radix):
            chosen = jnp.where(digit == d, parts[place ^ d], chosen)
        ordered.append(chosen)
    return jnp.concatenate(ordered, 1)


def finish_kernel(here_ref, near_ref, far_ref, *rest):
    outs, (whole_s, sems) = rest[:-2], rest[-2:]
    core = here_ref[2]
    parts, count, model = near_ref.shape
    size = outs[0].shape[0]
    saves = []
    for part in range(parts):
        for ref, side in ((near_ref, core), (far_ref, 1 - core)):
            rows = pl.ds(pl.multiple_of(side * count, count), count)
            whole_s[part, rows, :] = ref[part].astype(f32)
        for at in range(2 * count // size):
            out = part * (2 * count // size) + at
            save = pltpu.make_async_copy(
                whole_s.at[part, pl.ds(at * size, size)], outs[out], sems.at[out]
            )
            save.start()
            saves.append(save)
    for save in saves:
        save.wait()


def finish(here, near, far):
    parts, count, model = near.shape
    number = parts * 2 * count // model
    vmem = pl.BlockSpec(memory_space=pltpu.VMEM)
    return pl.pallas_call(
        finish_kernel,
        out_shape=[pltpu.HBM((model, model), f32)] * number,
        in_specs=[pl.BlockSpec(memory_space=pltpu.SMEM), vmem, vmem],
        out_specs=[pl.BlockSpec(memory_space=pltpu.HBM)] * number,
        scratch_shapes=[
            pltpu.VMEM((parts, 2 * count, model), f32),
            pltpu.SemaphoreType.DMA((number,)),
        ],
        compiler_params=pltpu.CompilerParams(vmem_limit_bytes=INPUTS_BYTES),
        name="finish",
    )(here, near, far)


def swap(parts, flag):
    first, second = parts
    return jnp.where(flag == 1, second, first), jnp.where(flag == 1, first, second)


def body(
    tokens,
    known_flags,
    w_query,
    b_query,
    w_key,
    w_value,
    b_value,
    w_out,
    b_out,
    gain_one,
    shift_one,
    w_up,
    b_up,
    w_down,
    b_down,
    gain_two,
    shift_two,
    cotangent,
):
    cells, rows, model = tokens.shape
    blocks = lax.axis_size("blk")
    others = lax.axis_size("cells")
    part = rows // 2
    half = 2 * rows
    length = 2 * half
    block = lax.axis_index("blk")
    core = lax.axis_index("cells") % 2
    x, y = block % 2, block // 2
    axes = ("blk", "cells")

    def route(i, j):
        pairs = []
        for b in range(blocks):
            for c in range(others):
                there = 2 * (c % 2) + ((b % 2) ^ i)
                pairs.append((b * others + c, there * others + c - c % 2 + ((b // 2) ^ j)))
        return pairs

    def route_back(i, j):
        return [(there, here) for here, there in route(i, j)]

    both = ((0, 0), (0, 1), (1, 0), (1, 1))

    def near_rows(source, j):
        return lax.dynamic_slice_in_dim(source, (y ^ j) * part, part, 1)

    def cell_of(rows_sent, i):
        return lax.dynamic_slice_in_dim(rows_sent, x ^ i, 1, 0)

    turned = (w_query.T, w_key.T, w_value.T)
    vectors = [b_out, gain_one, shift_one, b_up, b_down, gain_two, shift_two, b_value, b_query]
    vectors = jnp.concatenate([jnp.stack(vectors).astype(f32), jnp.zeros((7, model), f32)], 0)
    first = {}
    for i, j in both:
        first[i, j] = lax.ppermute(cell_of(near_rows(tokens, j), i)[0], axes, route(i, j))
    here = jnp.stack([x, y, core]).astype(jnp.int32)
    place, *payloads = prepare(
        here, known_flags, exchange(known_flags, "cells", 1), tokens, cotangent
    )
    rest = {
        ij: lax.ppermute(sent, axes, route(*ij)) for ij, sent in zip(both, payloads[:4])
    }
    cot = [lax.ppermute(sent, axes, route(*ij)) for ij, sent in zip(both, payloads[4:])]
    wqT, wkT, wvT = turned
    pieces = [first[ij] for ij in both]
    own = list(join(pieces, [[(n, None) for n in range(4)]], (place, *turned, vectors)))
    other = [exchange(own[0], "cells", 1)]
    work = (half, rows)

    def attend(k):
        return attention_forward(
            k, place, own[k], other[k], (wqT, wkT, w_key, wvT, vectors), work[k]
        )

    forward = [attend(0)]
    mix = forward[0][0]
    own += join([rest[ij] for ij in both], [[(n, None) for n in range(4)]], (mix,))
    other.append(exchange(own[1], "cells", 1))
    forward.append(attend(1))
    mids = middle(
        here,
        [mix.reshape(model, half), forward[1][0].reshape(model, rows)],
        own,
        cot,
        (w_out, w_up, w_down),
        vectors,
    )
    mids, halves = (mids[:4], mids[4:8]), mids[8:]
    plan = reduce_plan()
    early, early_small = core_step(*halves)

    out_back = {}
    for i, j in both:
        pieces = [mids[0][0][(2 * i + j) * part : (2 * i + j + 1) * part]]
        if i == 0:
            pieces.append(mids[1][0][j * part : (j + 1) * part])
        out_back[i, j] = lax.ppermute(jnp.stack(pieces), axes, route_back(i, j))

    def rejoin(from_i):
        return jnp.concatenate(swap(from_i, y), 0)

    near, far = (rejoin((out_back[i, 0][0], out_back[i, 1][0])) for i in range(2))
    layer_out = jnp.stack([*swap((near, far), x), rejoin((out_back[0, 0][1], out_back[0, 1][1]))])

    def attend_back(k, before, after):
        mix, lse, own_score, *saved = forward[k]
        out, gh1, g_mix, delta = mids[k]
        return attention_backward(
            k,
            here,
            place,
            own[k],
            (wkT, w_value, vectors),
            saved,
            (lse, own_score, g_mix, delta),
            before,
            after,
            work[k],
        )

    def keep(k, grads, after):
        return input_gradients(k, place, grads, (wqT, wkT, wvT), mids[k][1], after)

    def whole_rows(mine, sent):
        return (mine + exchange(sent, "cells", 1).astype(f32)).astype(bf16)

    def give_back(kept):
        back = []
        for n, (i, j) in enumerate(both):
            sent = jnp.stack([rows[n * part : (n + 1) * part] for rows in kept])
            back.append(lax.ppermute(sent, axes, route_back(i, j)))
        return back

    *grads_a, first_sum, second_sum = attend_back(0, None, ())
    *grads_b, mine, other_half = attend_back(1, (first_sum, second_sum), (early, layer_out))
    early, early_small = reduce_step(plan[1], early, early_small)
    mine, other_half, early, early_small = lax.optimization_barrier(
        (mine, other_half, early, early_small)
    )
    late, late_small = core_step(mine, other_half)
    kept = keep(0, grads_a, (late,))
    late, late_small = reduce_step(plan[1], late, late_small)
    late, late_small, kept = lax.optimization_barrier((late, late_small, kept))
    kept_a = whole_rows(*kept)
    kept = keep(1, grads_b, (late,))
    big = jnp.concatenate([early, late], 0)
    small = (early_small.astype(f32) + late_small.astype(f32)).astype(bf16)
    for at, step in enumerate(plan[2:]):
        arrived = send_step(step, big, small)
        if at == 0:
            arrived, kept = lax.optimization_barrier((arrived, kept))
        big, small = sum_step(step, big, small, arrived)
    back = give_back([kept_a, whole_rows(*kept)])
    for step in reversed(plan[2:]):
        parts = share_step(step, big)
        if step is plan[2]:
            parts, back = lax.optimization_barrier((parts, back))
        big = gather_step(step, parts)
    big = gather_step(plan[1], share_step(plan[1], big))

    near, far, near_last, far_last = (
        rejoin((back[2 * i][k], back[2 * i + 1][k])).astype(f32) for k in range(2) for i in range(2)
    )
    grad_tokens = jnp.stack([*swap((near, far), x), near_last + far_last])
    big, small, grad_tokens = lax.optimization_barrier((big, small, grad_tokens))
    g_out, g_up, g_down, g_query, g_key, g_value = finish(here, big, exchange(big, "cells", 1))
    small = small.astype(f32)
    g_b_out, g_gain_one, g_shift_one, g_b_up, g_b_down, g_gain_two, g_shift_two = (
        small[n] for n in range(7)
    )
    return (
        layer_out,
        grad_tokens,
        g_query,
        small[8],
        g_key,
        g_value,
        small[9],
        g_out,
        g_b_out,
        g_gain_one,
        g_shift_one,
        g_up,
        g_b_up,
        g_down,
        g_b_down,
        g_gain_two,
        g_shift_two,
    )


def solution(mesh):
    rows = P("cells", "blk", None)
    return jax.shard_map(
        body,
        mesh=mesh,
        in_specs=(rows, P("cells", None)) + (P(),) * 15 + (rows,),
        out_specs=(rows, rows) + (P(),) * 15,
        check_vma=False,
    )
```
